256 devices in a mesh: dp: 32 (over y, z_hi, core), expert: 8 (over x, z_lo).
Axes of the slice: x: 4, y: 4, z: 8 (z_hi: 4, z_lo: 2; z = z_hi * 2 + z_lo), core: 2. Of those that a mesh axis runs over, the one named last changes fastest.
Arguments:
- tokens: bfloat16 [65536, 2048], P(('dp', 'expert')), may hold values from -6 to 6
- grad_out: bfloat16 [65536, 2048], P(('dp', 'expert')), may hold values from -6 to 6
- router_weight: bfloat16 [2048, 8], replicated, may hold values from -0.125 to 0.125
- weight_in: bfloat16 [8, 2048, 1024], P('expert'), may hold values from -0.125 to 0.125
- weight_out: bfloat16 [8, 1024, 2048], P('expert'), may hold values from -0.1875 to 0.1875
- expert_ids: int32 [65536, 2], P(('dp', 'expert')), may hold values from 0 to 7, as said below
- slot_index: int32 [65536, 2], P(('dp', 'expert')), may hold values from 0 to 63, as said below
- keep_mask: int32 [65536, 2], P(('dp', 'expert')), may hold values from 0 to 1
Outputs:
- grad_tokens: bfloat16 [65536, 2048], P(('dp', 'expert'))
- grad_router: float32 [2048, 8], replicated
- grad_w_in: float32 [8, 2048, 1024], P('expert', 'dp')
- grad_w_out: float32 [8, 1024, 2048], P('expert', 'dp')
The draws below stay inside these ranges and needn't reach their ends.
Inputs may be any that keep to these rules, and one draw needn't show every extreme that they name: `expert_ids`: each row names 2 different experts. `slot_index`: within the 256 rows of one device, the kept assignments to one expert hold different slots; a dropped assignment has slot 0.
All inputs are finite; a program needn't handle non-finite values.
Results may differ from the reference program's by a relative error of at most 0.0062.
Values may be sent and summed in bfloat16 or wider, within the bound.
No kernel may reach another device: no remote copies, remote signals or barrier semaphores. Data moves between devices by JAX's collectives and lax.ppermute only.
A program may use at most 128 MiB of HBM per device.

```python
import jax
import jax.numpy as jnp
from jax import lax

D = 2048
HID = 1024
NE = 8
TOK_DEV = 256
TOPK = 2
CAP = 64
TOKENS = 65536
N_DP = 32
N_EXPERT = 8


def routing_table(key):
    scores = jax.random.randint(jax.random.fold_in(key, 101), (TOKENS, NE), 0, 1 << 20, dtype=jnp.int32)
    favour = jax.random.randint(jax.random.fold_in(key, 102), (NE,), 0, 1 << 20, dtype=jnp.int32)
    ranked = (scores + favour[None, :]) * NE + jnp.arange(NE, dtype=jnp.int32)[None, :]
    values_top, chosen = lax.top_k(ranked, TOPK)
    chosen = chosen.astype(jnp.int32)
    blocks = TOKENS // TOK_DEV
    grouped = chosen.reshape(blocks, TOK_DEV, TOPK)
    onehot = (grouped[:, :, :, None] == jnp.arange(NE, dtype=jnp.int32)[None, None, None, :]).astype(jnp.int32)
    ordered = jnp.transpose(onehot, (0, 2, 1, 3)).reshape(blocks, TOPK * TOK_DEV, NE)
    before = jnp.cumsum(ordered, axis=1) - ordered
    position = jnp.sum(before * ordered, axis=2).reshape(blocks, TOPK, TOK_DEV)
    position = jnp.transpose(position, (0, 2, 1)).reshape(TOKENS, TOPK)
    keep_flag = (position < CAP).astype(jnp.int32)
    slot_table = jnp.where(keep_flag == 1, position, 0).astype(jnp.int32)
    return (chosen, slot_table, keep_flag)


def draw_expert_ids(key, part):
    table = routing_table(key)
    return table[0]


def draw_slot_index(key, part):
    table = routing_table(key)
    return table[1]


def draw_keep_mask(key, part):
    table = routing_table(key)
    return table[2]


def block_scale(rng, extent, cuts, low, high):
    loudness = 1.0
    for dim, parts in cuts:
        heights = jax.random.uniform(jax.random.fold_in(jax.random.fold_in(rng, 6), dim), (parts,), jnp.float32, low / len(cuts), high / len(cuts))
        loudness = loudness * jnp.repeat(jnp.exp(heights), extent[dim] // parts).reshape((-1,) + (1,) * (len(extent) - 1 - dim))
    return loudness


def noise(stream_key, extent, width, bound, split=(), kind=jnp.bfloat16):
    drawn = jax.random.normal(stream_key, extent, jnp.float32) * width
    if len(split) > 0:
        drawn = block_scale(stream_key, extent, split, -0.22, 0.18) * drawn
    return jnp.clip(drawn, min=-bound, max=bound).astype(kind)


def setup_inputs(seed: int = 0) -> dict:
    key_list = jax.random.split(jax.random.key(seed), 9)
    return {
        "tokens": noise(key_list[0], (TOKENS, D), 1.0, 6.0, ((0, 256),)),
        "grad_out": noise(key_list[1], (TOKENS, D), 1.0, 6.0, ((0, 256),)),
        "router_weight": noise(key_list[2], (D, NE), D ** -0.5, 0.125),
        "weight_in": noise(key_list[3], (NE, D, HID), D ** -0.5, 0.125, ((0, 8),)),
        "weight_out": noise(key_list[4], (NE, HID, D), HID ** -0.5, 0.1875, ((0, 8),)),
        "expert_ids": draw_expert_ids(jax.random.fold_in(key_list[8], 71), 0),
        "slot_index": draw_slot_index(jax.random.fold_in(key_list[8], 71), 0),
        "keep_mask": draw_keep_mask(jax.random.fold_in(key_list[8], 71), 0),
    }


def gelu_parts(hidden_pre):
    normal_cdf = 0.5 * (1.0 + jax.scipy.special.erf(hidden_pre * 0.7071067811865476))
    normal_pdf = jnp.exp(-0.5 * hidden_pre * hidden_pre) * 0.3989422804014327
    return normal_cdf, normal_pdf


def contract_rows(left, right):
    return lax.dot_general(left, right, (((0,), (0,)), ((), ())), preferred_element_type=jnp.float32)


def contract_cols(left, right):
    return lax.dot_general(left, right, (((1,), (1,)), ((), ())), preferred_element_type=jnp.float32)


def expert_backward(operands):
    slot_tokens, slot_grads, slot_gates, weight_first, weight_second = operands
    hidden_pre = jnp.dot(slot_tokens, weight_first, preferred_element_type=jnp.float32)
    normal_cdf, normal_pdf = gelu_parts(hidden_pre)
    hidden_act = (hidden_pre * normal_cdf).astype(jnp.bfloat16)
    expert_out = jnp.dot(hidden_act, weight_second, preferred_element_type=jnp.float32)
    grads_wide = slot_grads.astype(jnp.float32)
    slot_combine_grad = jnp.sum(expert_out * grads_wide, axis=1).astype(jnp.bfloat16)
    scaled_grads = (slot_gates.astype(jnp.float32)[:, None] * grads_wide).astype(jnp.bfloat16)
    outer_grad = contract_rows(hidden_act, scaled_grads)
    grad_act = contract_cols(scaled_grads, weight_second)
    grad_pre = (grad_act * (normal_cdf + hidden_pre * normal_pdf)).astype(jnp.bfloat16)
    inner_grad = contract_rows(slot_tokens, grad_pre)
    grad_slots = contract_cols(grad_pre, weight_first).astype(jnp.bfloat16)
    return grad_slots, slot_combine_grad, inner_grad, outer_grad


def place_rows(source_rows, positions):
    empty = jnp.zeros((NE * CAP + 1,) + source_rows.shape[1:], source_rows.dtype)
    return empty.at[positions].set(source_rows)[: NE * CAP]


def take_rows(source_rows, positions):
    return source_rows[positions]


def reference(tokens, grad_out, router_weight, weight_in, weight_out, expert_ids, slot_index, keep_mask):
    devices_all = N_DP * N_EXPERT
    grad_scale = float(TOKENS) ** -0.5
    logits = jnp.dot(tokens, router_weight, preferred_element_type=jnp.float32)
    exp_logits = jnp.exp(logits)
    router_probs = exp_logits / jnp.sum(exp_logits, axis=1, keepdims=True)
    picked = expert_ids[:, :, None] == jnp.arange(NE, dtype=jnp.int32)[None, None, :]
    chosen = jnp.sum(jnp.where(picked, router_probs[:, None, :], jnp.float32(0.0)), axis=2)
    keep_float = keep_mask.astype(jnp.float32)
    denominator = jnp.sum(keep_float * chosen, axis=1) + (1.0 - jnp.max(keep_float, axis=1))
    combine = keep_float * chosen / denominator[:, None]
    combine_b = combine.astype(jnp.bfloat16)

    target = jnp.where(keep_mask == 1, expert_ids * CAP + slot_index, NE * CAP).astype(jnp.int32)
    dev_target = target.reshape(devices_all, TOK_DEV * TOPK)
    rep_tokens = jnp.repeat(tokens.reshape(devices_all, TOK_DEV, D), TOPK, axis=1)
    rep_grads = jnp.repeat(grad_out.reshape(devices_all, TOK_DEV, D), TOPK, axis=1)
    rep_gates = combine_b.reshape(devices_all, TOK_DEV * TOPK)
    buffer_tokens = jax.vmap(place_rows)(rep_tokens, dev_target)
    buffer_grads = jax.vmap(place_rows)(rep_grads, dev_target)
    buffer_gates = jax.vmap(place_rows)(rep_gates, dev_target)

    def by_expert(buffer_rows):
        shaped = buffer_rows.reshape((devices_all, NE, CAP) + buffer_rows.shape[2:])
        shaped = jnp.swapaxes(shaped, 0, 1)
        return shaped.reshape((NE, devices_all * CAP) + buffer_rows.shape[2:])

    grad_slots, slot_combine_grad, inner_grad, outer_grad = lax.map(
        expert_backward,
        (by_expert(buffer_tokens), by_expert(buffer_grads), by_expert(buffer_gates), weight_in, weight_out))
    grad_w_in = inner_grad * grad_scale
    grad_w_out = outer_grad * grad_scale

    def by_device(expert_rows):
        shaped = expert_rows.reshape((NE, devices_all, CAP) + expert_rows.shape[2:])
        shaped = jnp.swapaxes(shaped, 0, 1)
        return shaped.reshape((devices_all, NE * CAP) + expert_rows.shape[2:])

    back_rows = jnp.concatenate([by_device(grad_slots), jnp.zeros((devices_all, 1, D), jnp.bfloat16)], axis=1)
    back_combine = jnp.concatenate([by_device(slot_combine_grad), jnp.zeros((devices_all, 1), jnp.bfloat16)], axis=1)
    gathered = jax.vmap(take_rows)(back_rows, dev_target).reshape(TOKENS, TOPK, D)
    expert_grad = jnp.sum(gathered.astype(jnp.float32), axis=1)
    combine_grad = jax.vmap(take_rows)(back_combine, dev_target).reshape(TOKENS, TOPK).astype(jnp.float32)

    weighted_sum = jnp.sum(combine_grad * combine, axis=1)
    chosen_grad = keep_float * (combine_grad - weighted_sum[:, None]) / denominator[:, None]
    probs_grad = jnp.sum(jnp.where(picked, chosen_grad[:, :, None], jnp.float32(0.0)), axis=1)
    logit_grad = router_probs * (probs_grad - jnp.sum(probs_grad * router_probs, axis=1, keepdims=True))
    logit_b = logit_grad.astype(jnp.bfloat16)
    grad_tokens = (expert_grad + contract_cols(logit_b, router_weight)).astype(jnp.bfloat16)
    grad_router = contract_rows(tokens, logit_b) * grad_scale
    return grad_tokens, grad_router, grad_w_in, grad_w_out
```

```python
import jax
import jax.numpy as jnp
from jax import lax
from jax.sharding import Mesh, PartitionSpec as P

FINE = ("y", "zh", "core", "x", "zl")
FINE_SHAPE = (4, 4, 2, 4, 2)
GROUP = ("x", "zl")
F32 = jnp.float32
BF16 = jnp.bfloat16


def gelu_parts(hidden_pre):
    normal_cdf = 0.5 * (1.0 + jax.scipy.special.erf(hidden_pre * 0.7071067811865476))
    normal_pdf = jnp.exp(-0.5 * hidden_pre * hidden_pre) * 0.3989422804014327
    return (normal_cdf, normal_pdf)


def contract_rows(left, right):
    return lax.dot_general(left, right, (((0,), (0,)), ((), ())), preferred_element_type=F32)


def contract_cols(left, right):
    return lax.dot_general(left, right, (((1,), (1,)), ((), ())), preferred_element_type=F32)


def swap(values, axis, mask):
    size = lax.axis_size(axis)
    return lax.ppermute(values, axis, [(i, i ^ mask) for i in range(size)])


def exchange(values, axes):
    return lax.all_to_all(values, axes, split_axis=0, concat_axis=0, tiled=True)


def xor_blocks(values, me, blocks):
    width = values.shape[1] // blocks
    parts = [
        lax.dynamic_slice_in_dim(values, (me ^ r) * width, width, axis=1) for r in range(blocks)
    ]
    return jnp.concatenate(parts, axis=1)


def reduce_share(left, right, scale):
    rows = left.shape[1] // 4
    cols = right.shape[1]
    half = cols // 2
    right_a, right_b = right[:, :half], right[:, half:]
    send_a = contract_rows(left[:, rows : 3 * rows], right_a).astype(BF16)
    send_b = contract_rows(left[:, 2 * rows :], right_b).astype(BF16)
    got_a = swap(send_a, "y", 1).astype(F32)
    got_b = swap(send_b, "y", 3).astype(F32)
    far_a = contract_rows(left[:, 3 * rows :], right_a)
    far_b = contract_rows(left[:, rows : 2 * rows], right_b)
    near_a = contract_rows(left[:, :rows], right_a)
    near_b = contract_rows(left[:, :rows], right_b)
    far_a = (far_a + got_a[rows:]).astype(BF16)
    far_b = (far_b + got_b[:rows]).astype(BF16)
    got_far_a = swap(far_a, "y", 3).astype(F32)
    got_far_b = swap(far_b, "y", 1).astype(F32)
    near_a = near_a + got_a[:rows] + got_far_a
    near_b = near_b + got_b[rows:] + got_far_b
    near = jnp.concatenate([near_a, near_b], axis=1).astype(BF16)
    share = rows // 8
    pieces = exchange(near.reshape(8, share, cols), ("zh", "core")).astype(F32)
    total = jnp.sum(pieces.reshape(4, 2, share, cols), axis=0) * scale
    return jnp.concatenate([total[0], total[1]], axis=1)[None]


def per_device(
    tokens, grad_out, router_weight, weight_in, weight_out, expert_ids, slot_index, keep_mask
):
    tok_rows, model_width = tokens.shape
    experts = 8
    weight_in = weight_in[0]
    weight_out = weight_out[0]
    capacity = tok_rows * expert_ids.shape[1] // experts
    slot_count = experts * capacity
    grad_scale = float(tok_rows * 256) ** (-0.5)
    core = lax.axis_index("core")
    my_y = lax.axis_index("y")

    target = expert_ids * capacity + slot_index
    slot_iota = jnp.arange(slot_count, dtype=jnp.int32)[:, None]
    first_hit = (slot_iota == target[None, :, 0]) & (keep_mask[None, :, 0] == 1)
    second_hit = (slot_iota == target[None, :, 1]) & (keep_mask[None, :, 1] == 1)
    dispatch = (first_hit | second_hit).astype(BF16)

    send_tokens = jnp.dot(dispatch, tokens, preferred_element_type=F32).astype(BF16)
    slot_tokens = exchange(
        send_tokens.reshape(experts, capacity, model_width), GROUP
    ).reshape(slot_count, model_width)

    send_grads = jnp.dot(dispatch, grad_out, preferred_element_type=F32).astype(BF16)
    slot_grads = exchange(
        send_grads.reshape(experts, capacity, model_width), GROUP
    ).reshape(slot_count, model_width)

    logits = jnp.dot(tokens, router_weight, preferred_element_type=F32)
    exp_logits = jnp.exp(logits)
    router_probs = exp_logits / jnp.sum(exp_logits, axis=1, keepdims=True)
    picked = expert_ids[:, :, None] == jnp.arange(experts, dtype=jnp.int32)[None, None, :]
    chosen = jnp.sum(jnp.where(picked, router_probs[:, None, :], 0.0), axis=2)
    keep_float = keep_mask.astype(F32)
    denominator = jnp.sum(keep_float * chosen, axis=1) + (1.0 - jnp.max(keep_float, axis=1))
    combine = keep_float * chosen / denominator[:, None]
    gate_wide = combine.astype(BF16).astype(F32)
    send_gates = jnp.sum(
        jnp.where(first_hit, gate_wide[None, :, 0], 0.0)
        + jnp.where(second_hit, gate_wide[None, :, 1], 0.0),
        axis=1,
    ).astype(BF16)
    slot_gates = exchange(send_gates.reshape(experts, capacity), GROUP).reshape(slot_count, 1)
    gates = slot_gates.astype(F32)

    other_tokens = swap(slot_tokens, "core", 1)
    hidden_pre = jnp.dot(slot_tokens, weight_in, preferred_element_type=F32)
    normal_cdf, normal_pdf = gelu_parts(hidden_pre)
    hidden_act = (hidden_pre * normal_cdf).astype(BF16)
    act_slope = normal_cdf + hidden_pre * normal_pdf
    scaled_act = (gates * hidden_act.astype(F32)).astype(BF16)
    other_act = swap(scaled_act, "core", 1)
    left_in = xor_blocks(jnp.concatenate([slot_tokens, other_tokens], axis=0), my_y, 4)
    left_out = xor_blocks(jnp.concatenate([scaled_act, other_act], axis=0), my_y, 4)

    half_width = model_width // 2
    my_grads = lax.dynamic_slice_in_dim(slot_grads, core * half_width, half_width, axis=1)
    give_grads = lax.dynamic_slice_in_dim(slot_grads, (1 - core) * half_width, half_width, axis=1)
    right_out = jnp.concatenate([my_grads, swap(give_grads, "core", 1)], axis=0)

    grad_act = contract_cols(slot_grads, weight_out)
    slot_combine_grad = jnp.sum(hidden_act.astype(F32) * grad_act, axis=1).astype(BF16)
    grad_pre = (gates * grad_act * act_slope).astype(BF16)

    half_hidden = grad_pre.shape[1] // 2
    my_pre = lax.dynamic_slice_in_dim(grad_pre, core * half_hidden, half_hidden, axis=1)
    give_pre = lax.dynamic_slice_in_dim(grad_pre, (1 - core) * half_hidden, half_hidden, axis=1)
    right_in = jnp.concatenate([my_pre, swap(give_pre, "core", 1)], axis=0)

    flat_combine = exchange(slot_combine_grad.reshape(experts, capacity), GROUP).reshape(
        slot_count
    )
    grad_slots = contract_cols(grad_pre, weight_in).astype(BF16)
    flat_grads = exchange(
        grad_slots.reshape(experts, capacity, model_width), GROUP
    ).reshape(slot_count, model_width)

    outer_share = reduce_share(left_out, right_out, grad_scale)
    inner_share = reduce_share(left_in, right_in, grad_scale)

    combine_wide = flat_combine.astype(F32)[:, None]
    combine_grad = jnp.stack(
        [
            jnp.sum(jnp.where(first_hit, combine_wide, 0.0), axis=0),
            jnp.sum(jnp.where(second_hit, combine_wide, 0.0), axis=0),
        ],
        axis=1,
    )
    weighted_sum = jnp.sum(combine_grad * combine, axis=1)
    chosen_grad = keep_float * (combine_grad - weighted_sum[:, None]) / denominator[:, None]
    probs_grad = jnp.sum(jnp.where(picked, chosen_grad[:, :, None], 0.0), axis=1)
    logit_grad = router_probs * (
        probs_grad - jnp.sum(probs_grad * router_probs, axis=1, keepdims=True)
    )
    logit_b = logit_grad.astype(BF16)

    router_part = contract_rows(logit_b, tokens) * grad_scale
    router_part = router_part + swap(router_part, "core", 1)
    router_row = jnp.sum(exchange(router_part, GROUP), axis=0, keepdims=True)
    rows = exchange(jnp.broadcast_to(router_row, (16, model_width)), ("y", "zh"))
    router_row = jnp.sum(rows, axis=0, keepdims=True)
    grad_router = exchange(jnp.broadcast_to(router_row, (experts, model_width)), GROUP)

    expert_grad = contract_rows(dispatch, flat_grads)
    grad_tokens = (expert_grad + contract_cols(logit_b, router_weight)).astype(BF16)
    return (grad_tokens, grad_router.T, inner_share, outer_share)


def solution(mesh):
    fine = Mesh(mesh.devices.reshape(FINE_SHAPE), FINE)
    placed = (
        P(FINE, None),
        P(FINE, None),
        P(),
        P(GROUP, None, None),
        P(GROUP, None, None),
        P(FINE, None),
        P(FINE, None),
        P(FINE, None),
    )
    return jax.shard_map(
        per_device,
        mesh=fine,
        in_specs=placed,
        out_specs=(
            P(FINE, None),
            P(),
            P(GROUP, ("y", "zh", "core"), None),
            P(GROUP, ("y", "zh", "core"), None),
        ),
        check_vma=False,
    )
```

```python
import jax
import jax.numpy as jnp
from jax import lax
from jax.sharding import Mesh, PartitionSpec as P

FINE = ("y", "zh", "core", "x", "zl")
FINE_SHAPE = (4, 4, 2, 4, 2)
GROUP = ("x", "zl")
EXTRA = 128
ROUTER_STEPS = (
    ("core", 1),
    ("x", 1),
    ("x", 3),
    ("zl", 1),
    ("y", 1),
    ("y", 3),
    ("zh", 1),
    ("zh", 3),
)
F32 = jnp.float32
BF16 = jnp.bfloat16


def gelu_parts(hidden_pre):
    normal_cdf = 0.5 * (1.0 + jax.scipy.special.erf(hidden_pre * 0.7071067811865476))
    normal_pdf = jnp.exp(-0.5 * hidden_pre * hidden_pre) * 0.3989422804014327
    return (normal_cdf, normal_pdf)


def contract_rows(left, right):
    return lax.dot_general(left, right, (((0,), (0,)), ((), ())), preferred_element_type=F32)


def contract_cols(left, right):
    return lax.dot_general(left, right, (((1,), (1,)), ((), ())), preferred_element_type=F32)


def swap(values, axis, mask):
    size = lax.axis_size(axis)
    return lax.ppermute(values, axis, [(i, i ^ mask) for i in range(size)])


def exchange(values, axes):
    return lax.all_to_all(values, axes, split_axis=0, concat_axis=0, tiled=True)


def xor_blocks(values, me, blocks):
    width = values.shape[1] // blocks
    parts = [
        lax.dynamic_slice_in_dim(values, (me ^ r) * width, width, axis=1) for r in range(blocks)
    ]
    return jnp.concatenate(parts, axis=1)


def tie(*values):
    return lax.optimization_barrier(values)


def first_parts(left, right):
    rows = left.shape[1] // 4
    half = right.shape[1] // 2
    part_a = contract_rows(left[:, rows : 3 * rows], right[:, :half]).astype(BF16)
    part_b = contract_rows(left[:, 2 * rows :], right[:, half:]).astype(BF16)
    return part_a, part_b


def second_parts(left, right, got_a, got_b):
    rows = left.shape[1] // 4
    half = right.shape[1] // 2
    part_a = contract_rows(left[:, 3 * rows :], right[:, :half]) + got_a[rows:].astype(F32)
    part_b = contract_rows(left[:, rows : 2 * rows], right[:, half:]) + got_b[:rows].astype(F32)
    return part_a.astype(BF16), part_b.astype(BF16)


def own_parts(left, right, got_a, got_b, far_a, far_b):
    rows = left.shape[1] // 4
    half = right.shape[1] // 2
    near_a = contract_rows(left[:, :rows], right[:, :half]) + got_a[:rows].astype(F32)
    near_b = contract_rows(left[:, :rows], right[:, half:]) + got_b[rows:].astype(F32)
    near_a = near_a + far_a.astype(F32)
    near_b = near_b + far_b.astype(F32)
    return jnp.concatenate([near_a, near_b], axis=1)


def finish(near, scale):
    zh = lax.axis_index("zh")
    block = near.shape[0] // 4
    mine = lax.dynamic_slice_in_dim(near, zh * block, block, axis=0)
    near_b16 = near.astype(BF16)
    for r in (1, 2, 3):
        piece = lax.dynamic_slice_in_dim(near_b16, (zh ^ r) * block, block, axis=0)
        mine = mine + swap(piece, "zh", r).astype(F32)
    core = lax.axis_index("core")
    share = block // 2
    mine = mine * scale
    keep = lax.dynamic_slice_in_dim(mine, core * share, share, axis=0)
    give = lax.dynamic_slice_in_dim(mine, (1 - core) * share, share, axis=0)
    got = swap(give, "core", 1)
    first = jnp.where(core == 0, keep, got)
    second = jnp.where(core == 0, got, keep)
    return jnp.concatenate([first, second], axis=1)[None]


def per_device(
    tokens, grad_out, router_weight, weight_in, weight_out, expert_ids, slot_index, keep_mask
):
    tok_rows, model_width = tokens.shape
    experts = 8
    weight_in = weight_in[0]
    weight_out = weight_out[0]
    capacity = tok_rows * expert_ids.shape[1] // experts
    slot_count = experts * capacity
    grad_scale = float(tok_rows * 256) ** (-0.5)
    core = lax.axis_index("core")
    my_y = lax.axis_index("y")

    target = expert_ids * capacity + slot_index
    slot_iota = jnp.arange(slot_count, dtype=jnp.int32)[:, None]
    first_hit = (slot_iota == target[None, :, 0]) & (keep_mask[None, :, 0] == 1)
    second_hit = (slot_iota == target[None, :, 1]) & (keep_mask[None, :, 1] == 1)
    dispatch = (first_hit | second_hit).astype(BF16)

    send_tokens = jnp.dot(dispatch, tokens, preferred_element_type=F32).astype(BF16)
    slot_tokens = exchange(
        send_tokens.reshape(experts, capacity, model_width), GROUP
    ).reshape(slot_count, model_width)

    logits = jnp.dot(tokens, router_weight, preferred_element_type=F32)
    exp_logits = jnp.exp(logits)
    router_probs = exp_logits / jnp.sum(exp_logits, axis=1, keepdims=True)
    picked = expert_ids[:, :, None] == jnp.arange(experts, dtype=jnp.int32)[None, None, :]
    chosen = jnp.sum(jnp.where(picked, router_probs[:, None, :], 0.0), axis=2)
    keep_float = keep_mask.astype(F32)
    denominator = jnp.sum(keep_float * chosen, axis=1) + (1.0 - jnp.max(keep_float, axis=1))
    combine = keep_float * chosen / denominator[:, None]
    gate_lanes = jnp.sum(jnp.where(picked, combine[:, :, None], 0.0), axis=1).astype(BF16)
    gate_lanes = jnp.pad(gate_lanes, ((0, 0), (0, EXTRA - experts)))
    send_grads = jnp.dot(dispatch, grad_out, preferred_element_type=F32).astype(BF16)
    send_gates = jnp.dot(dispatch, gate_lanes, preferred_element_type=F32).astype(BF16)
    received = exchange(
        jnp.concatenate([send_grads, send_gates], axis=1).reshape(
            experts, capacity, model_width + EXTRA
        ),
        GROUP,
    ).reshape(slot_count, model_width + EXTRA)
    other_tokens = swap(slot_tokens, "core", 1)
    hidden_pre = jnp.dot(slot_tokens, weight_in, preferred_element_type=F32)
    normal_cdf, normal_pdf = gelu_parts(hidden_pre)
    hidden_act = (hidden_pre * normal_cdf).astype(BF16)
    act_slope = normal_cdf + hidden_pre * normal_pdf
    other_act = swap(hidden_act, "core", 1)
    left_in = xor_blocks(jnp.concatenate([slot_tokens, other_tokens], axis=0), my_y, 4)
    left_out = xor_blocks(jnp.concatenate([hidden_act, other_act], axis=0), my_y, 4)

    received, left_in, left_out, hidden_act, act_slope = lax.optimization_barrier(
        (received, left_in, left_out, hidden_act, act_slope)
    )
    slot_grads = received[:, :model_width]
    lane = jnp.arange(EXTRA, dtype=jnp.int32)[None, :]
    gates = jnp.sum(
        jnp.where(lane == lax.axis_index(GROUP), received[:, model_width:].astype(F32), 0.0),
        axis=1,
        keepdims=True,
    )

    half_width = model_width // 2
    scaled_grads = (gates * slot_grads.astype(F32)).astype(BF16)
    my_grads = lax.dynamic_slice_in_dim(scaled_grads, core * half_width, half_width, axis=1)
    give_grads = lax.dynamic_slice_in_dim(scaled_grads, (1 - core) * half_width, half_width, axis=1)
    slot_grads, give_grads = tie(slot_grads, give_grads)
    other_grads = swap(give_grads, "core", 1)

    grad_act = contract_cols(slot_grads, weight_out)
    slot_combine_grad = jnp.sum(hidden_act.astype(F32) * grad_act, axis=1).astype(BF16)
    grad_pre = (gates * grad_act * act_slope).astype(BF16)
    grad_pre, slot_combine_grad, other_grads = tie(grad_pre, slot_combine_grad, other_grads)
    flat_combine = exchange(slot_combine_grad.reshape(experts, capacity), GROUP).reshape(
        slot_count
    )

    half_hidden = grad_pre.shape[1] // 2
    my_pre = lax.dynamic_slice_in_dim(grad_pre, core * half_hidden, half_hidden, axis=1)
    give_pre = lax.dynamic_slice_in_dim(grad_pre, (1 - core) * half_hidden, half_hidden, axis=1)
    other_pre = swap(give_pre, "core", 1)

    right_out = jnp.concatenate([my_grads, other_grads], axis=0)
    out_a, out_b = first_parts(left_out, right_out)
    _, _, grad_pre, other_pre = tie(out_a, out_b, grad_pre, other_pre)
    out_a, out_b = swap(out_a, "y", 1), swap(out_b, "y", 3)

    right_in = jnp.concatenate([my_pre, other_pre], axis=0)
    in_a, in_b = first_parts(left_in, right_in)
    _, _, grad_pre = tie(in_a, in_b, grad_pre)
    in_a, in_b = swap(in_a, "y", 1), swap(in_b, "y", 3)

    grad_slots = contract_cols(grad_pre, weight_in).astype(BF16)
    grad_slots, flat_combine = tie(grad_slots, flat_combine)
    flat_grads = exchange(
        grad_slots.reshape(experts, capacity, model_width), GROUP
    ).reshape(slot_count, model_width)

    far_a, far_b = second_parts(left_out, right_out, out_a, out_b)
    _, _, flat_combine = tie(far_a, far_b, flat_combine)
    far_a, far_b = swap(far_a, "y", 3), swap(far_b, "y", 1)

    combine_wide = flat_combine.astype(F32)[:, None]
    combine_grad = jnp.stack(
        [
            jnp.sum(jnp.where(first_hit, combine_wide, 0.0), axis=0),
            jnp.sum(jnp.where(second_hit, combine_wide, 0.0), axis=0),
        ],
        axis=1,
    )
    weighted_sum = jnp.sum(combine_grad * combine, axis=1)
    chosen_grad = keep_float * (combine_grad - weighted_sum[:, None]) / denominator[:, None]
    probs_grad = jnp.sum(jnp.where(picked, chosen_grad[:, :, None], 0.0), axis=1)
    logit_grad = router_probs * (
        probs_grad - jnp.sum(probs_grad * router_probs, axis=1, keepdims=True)
    )
    logit_b = logit_grad.astype(BF16)

    router_part = contract_rows(logit_b, tokens) * grad_scale
    for axis, mask in ROUTER_STEPS:
        router_part = router_part + swap(router_part, axis, mask)

    near_in_far = second_parts(left_in, right_in, in_a, in_b)
    in_far_a, in_far_b = swap(near_in_far[0], "y", 3), swap(near_in_far[1], "y", 1)
    outer = own_parts(left_out, right_out, out_a, out_b, far_a, far_b)
    outer_share = finish(outer, grad_scale)
    inner = own_parts(left_in, right_in, in_a, in_b, in_far_a, in_far_b)
    inner_share = finish(inner, grad_scale)

    expert_grad = contract_rows(dispatch, flat_grads)
    grad_tokens = (expert_grad + contract_cols(logit_b, router_weight)).astype(BF16)
    return (grad_tokens, router_part.T, inner_share, outer_share)


def solution(mesh):
    fine = Mesh(mesh.devices.reshape(FINE_SHAPE), FINE)
    placed = (
        P(FINE, None),
        P(FINE, None),
        P(),
        P(GROUP, None, None),
        P(GROUP, None, None),
        P(FINE, None),
        P(FINE, None),
        P(FINE, None),
    )
    return jax.shard_map(
        per_device,
        mesh=fine,
        in_specs=placed,
        out_specs=(
            P(FINE, None),
            P(),
            P(GROUP, ("y", "zh", "core"), None),
            P(GROUP, ("y", "zh", "core"), None),
        ),
        check_vma=False,
    )
```

```python
import jax
import jax.numpy as jnp
from jax import lax
from jax.experimental import pallas as pl
from jax.experimental.pallas import tpu as pltpu
from jax.sharding import Mesh, PartitionSpec as P

FINE = ("y", "zh", "core", "x", "zl")
FINE_SHAPE = (4, 4, 2, 4, 2)
GROUP = ("x", "zl")
EXTRA = 128
ROUTER_STEPS = (
    ("core", 1),
    ("x", 1),
    ("x", 3),
    ("zl", 1),
    ("y", 1),
    ("y", 3),
    ("zh", 1),
    ("zh", 3),
)
F32 = jnp.float32
BF16 = jnp.bfloat16


def gelu_parts(hidden_pre):
    normal_cdf = 0.5 * (1.0 + jax.scipy.special.erf(hidden_pre * 0.7071067811865476))
    normal_pdf = jnp.exp(-0.5 * hidden_pre * hidden_pre) * 0.3989422804014327
    return (normal_cdf, normal_pdf)


def contract_rows(left, right):
    return lax.dot_general(left, right, (((0,), (0,)), ((), ())), preferred_element_type=F32)


def contract_cols(left, right):
    return lax.dot_general(left, right, (((1,), (1,)), ((), ())), preferred_element_type=F32)


def swap(values, axis, mask):
    size = lax.axis_size(axis)
    return lax.ppermute(values, axis, [(i, i ^ mask) for i in range(size)])


def exchange(values, axes):
    return lax.all_to_all(values, axes, split_axis=0, concat_axis=0, tiled=True)


def tie(*values):
    return lax.optimization_barrier(values)


def call(body, pos, grid, inputs, in_blocks, outputs, out_blocks):
    return pl.pallas_call(
        body,
        grid_spec=pltpu.PrefetchScalarGridSpec(
            num_scalar_prefetch=1,
            grid=(grid,),
            in_specs=[pl.BlockSpec(shape, index) for shape, index in in_blocks],
            out_specs=[pl.BlockSpec(shape, index) for shape, index in out_blocks],
        ),
        out_shape=[jax.ShapeDtypeStruct(shape, dtype) for shape, dtype in outputs],
        cost_estimate=pl.CostEstimate(flops=1000, bytes_accessed=1000, transcendentals=0),
        compiler_params=pltpu.CompilerParams(vmem_limit_bytes=40 * 1024 * 1024),
    )(pos, *inputs)


def gate_of(pos, lanes):
    lane = lax.broadcasted_iota(jnp.int32, lanes.shape, 1)
    return jnp.sum(jnp.where(lane == pos[2], lanes.astype(F32), 0.0), axis=1, keepdims=True)


def scale_grads(pos, received):
    slots, wide = received.shape
    width = wide - EXTRA
    half = width // 2
    rows = slots // 4

    def body(pos_ref, rec, mine, give):
        gate = gate_of(pos_ref, rec[:, width:])
        core = pos_ref[1]
        for out, which in ((mine, core), (give, 1 - core)):
            start = pl.multiple_of(which * half, half)
            out[...] = (gate * rec[:, pl.ds(start, half)].astype(F32)).astype(BF16)

    block = ((rows, half), lambda i, pos: (i, 0))
    return call(
        body,
        pos,
        4,
        [received],
        [((rows, wide), lambda i, pos: (i, 0))],
        [((slots, half), BF16)] * 2,
        [block, block],
    )


def pre_grads(pos, received, weight_out, act, slope):
    slots, wide = received.shape
    hidden, width = weight_out.shape
    step = hidden // 4

    def body(pos_ref, rec, weight, act_ref, slope_ref, grad_pre, give, gate_grad):
        i = pl.program_id(0)
        grad_act = lax.dot_general(
            rec[:, :width], weight[...], (((1,), (1,)), ((), ())), preferred_element_type=F32
        )
        gate = gate_of(pos_ref, rec[:, width:])
        part = jnp.sum(act_ref[...].astype(F32) * grad_act, axis=1, keepdims=True)
        value = (gate * grad_act * slope_ref[...]).astype(BF16)
        grad_pre[...] = value

        @pl.when(i < 2)
        def _():
            give[...] = value

        @pl.when(i == 0)
        def _():
            gate_grad[...] = part

        @pl.when(i > 0)
        def _():
            gate_grad[...] += part

    order = lambda i, pos: i ^ (2 * (1 - pos[1]))
    column = ((slots, step), lambda i, pos: (0, order(i, pos)))
    return call(
        body,
        pos,
        4,
        [received, weight_out, act, slope],
        [
            ((slots, wide), lambda i, pos: (0, 0)),
            ((step, width), lambda i, pos: (order(i, pos), 0)),
            column,
            column,
        ],
        [((slots, hidden), BF16), ((slots, hidden // 2), BF16), ((slots, 1), F32)],
        [
            column,
            ((slots, step), lambda i, pos: (0, jnp.minimum(i, 1))),
            ((slots, 1), lambda i, pos: (0, 0)),
        ],
    )


def parts(pos, left, right, own_offset, kept):
    left_mine, left_other = left
    right_mine, right_other = right
    slots = left_mine.shape[0]
    width = left_mine.shape[1] // 4
    cols = right_other.shape[1] // 2
    dtype = F32 if kept else BF16

    def mask(i):
        if kept:
            return jnp.where(i == 1, 3, jnp.where(i == 3, 1, 0))
        return jnp.where(i == 0, 1, jnp.where(i == 2, 3, 2))

    def body(pos_ref, lm, lo, rm, ro, out_a, out_b):
        dims = (((0,), (0,)), ((), ()))
        value = lax.dot_general(lm[...], rm[...], dims, preferred_element_type=F32)
        value = value + lax.dot_general(lo[...], ro[...], dims, preferred_element_type=F32)
        value = value.astype(dtype)
        i = pl.program_id(0)

        @pl.when(i < 2)
        def _():
            out_a[...] = value

        @pl.when(i >= 2)
        def _():
            out_b[...] = value

    left_block = ((slots, width), lambda i, pos: (0, pos[0] ^ mask(i)))
    return call(
        body,
        pos,
        4,
        [left_mine, left_other, right_mine, right_other],
        [
            left_block,
            left_block,
            ((slots, cols), lambda i, pos: (0, own_offset * pos[1] + i // 2)),
            ((slots, cols), lambda i, pos: (0, i // 2)),
        ],
        [((2 * width, cols), dtype)] * 2,
        [
            ((width, cols), lambda i, pos: (jnp.minimum(i, 1), 0)),
            ((width, cols), lambda i, pos: (jnp.maximum(i, 2) - 2, 0)),
        ],
    )


def slot_grads_of(pos, grad_pre, weight_in):
    slots, hidden = grad_pre.shape
    width = weight_in.shape[0]
    step = width // 4

    def body(pos_ref, grad, weight, out):
        out[...] = lax.dot_general(
            grad[...], weight[...], (((1,), (1,)), ((), ())), preferred_element_type=F32
        ).astype(BF16)

    return call(
        body,
        pos,
        4,
        [grad_pre, weight_in],
        [((slots, hidden), lambda i, pos: (0, 0)), ((step, hidden), lambda i, pos: (i, 0))],
        [((slots, width), BF16)],
        [((slots, step), lambda i, pos: (0, i))],
    )[0]


def zh_sum(near_a, near_b):
    zh = lax.axis_index("zh")
    block = near_a.shape[0] // 4

    def rows_of(r):
        return jnp.concatenate(
            [
                lax.dynamic_slice_in_dim(near, (zh ^ r) * block, block, axis=0)
                for near in (near_a, near_b)
            ],
            axis=1,
        )

    return rows_of(0), [swap(rows_of(r).astype(BF16), "zh", r) for r in (1, 2, 3)]


def zh_total(mine, got, scale):
    for piece in got:
        mine = mine + piece.astype(F32)
    return mine * scale


def core_total(mine):
    core = lax.axis_index("core")
    share = mine.shape[0] // 2
    keep = lax.dynamic_slice_in_dim(mine, core * share, share, axis=0)
    give = lax.dynamic_slice_in_dim(mine, (1 - core) * share, share, axis=0)
    got = swap(give, "core", 1)
    first = jnp.where(core == 0, keep, got)
    second = jnp.where(core == 0, got, keep)
    return jnp.concatenate([first, second], axis=1)[None]


def per_device(
    tokens, grad_out, router_weight, weight_in, weight_out, expert_ids, slot_index, keep_mask
):
    tok_rows, model_width = tokens.shape
    experts = 8
    weight_in = weight_in[0]
    weight_out = weight_out[0]
    capacity = tok_rows * expert_ids.shape[1] // experts
    slot_count = experts * capacity
    grad_scale = float(tok_rows * 256) ** (-0.5)
    core = lax.axis_index("core")
    my_y = lax.axis_index("y")

    target = expert_ids * capacity + slot_index
    slot_iota = jnp.arange(slot_count, dtype=jnp.int32)[:, None]
    first_hit = (slot_iota == target[None, :, 0]) & (keep_mask[None, :, 0] == 1)
    second_hit = (slot_iota == target[None, :, 1]) & (keep_mask[None, :, 1] == 1)
    dispatch = (first_hit | second_hit).astype(BF16)

    send_tokens = jnp.dot(dispatch, tokens, preferred_element_type=F32).astype(BF16)
    slot_tokens = exchange(
        send_tokens.reshape(experts, capacity, model_width), GROUP
    ).reshape(slot_count, model_width)

    logits = jnp.dot(tokens, router_weight, preferred_element_type=F32)
    exp_logits = jnp.exp(logits)
    router_probs = exp_logits / jnp.sum(exp_logits, axis=1, keepdims=True)
    picked = expert_ids[:, :, None] == jnp.arange(experts, dtype=jnp.int32)[None, None, :]
    chosen = jnp.sum(jnp.where(picked, router_probs[:, None, :], 0.0), axis=2)
    keep_float = keep_mask.astype(F32)
    denominator = jnp.sum(keep_float * chosen, axis=1) + (1.0 - jnp.max(keep_float, axis=1))
    combine = keep_float * chosen / denominator[:, None]
    gate_lanes = jnp.sum(jnp.where(picked, combine[:, :, None], 0.0), axis=1).astype(BF16)
    gate_lanes = jnp.pad(gate_lanes, ((0, 0), (0, EXTRA - experts)))
    send_grads = jnp.dot(dispatch, grad_out, preferred_element_type=F32).astype(BF16)
    send_gates = jnp.dot(dispatch, gate_lanes, preferred_element_type=F32).astype(BF16)
    received = exchange(
        jnp.concatenate([send_grads, send_gates], axis=1).reshape(
            experts, capacity, model_width + EXTRA
        ),
        GROUP,
    ).reshape(slot_count, model_width + EXTRA)
    other_tokens = swap(slot_tokens, "core", 1)
    hidden_pre = jnp.dot(slot_tokens, weight_in, preferred_element_type=F32)
    normal_cdf, normal_pdf = gelu_parts(hidden_pre)
    hidden_act = (hidden_pre * normal_cdf).astype(BF16)
    act_slope = normal_cdf + hidden_pre * normal_pdf
    other_act = swap(hidden_act, "core", 1)
    left_in = (slot_tokens, other_tokens)
    left_out = (hidden_act, other_act)
    pos = jnp.stack([my_y, core, lax.axis_index(GROUP)]).astype(jnp.int32)

    received, left_in, left_out, act_slope = tie(received, left_in, left_out, act_slope)
    my_out, give_out = scale_grads(pos, received)
    other_out = swap(give_out, "core", 1)
    received, _ = tie(received, give_out)
    grad_pre, give_in, slot_combine_grad = pre_grads(
        pos, received, weight_out, hidden_act, act_slope
    )
    other_in = swap(give_in, "core", 1)
    flat_combine = exchange(
        slot_combine_grad.astype(BF16).reshape(experts, capacity), GROUP
    ).reshape(slot_count)

    send_out_a, send_out_b = parts(pos, left_out, (my_out, other_out), 0, False)
    got_out_a, got_out_b = swap(send_out_a, "y", 1), swap(send_out_b, "y", 3)
    grad_pre, _ = tie(grad_pre, send_out_a)
    send_in_a, send_in_b = parts(pos, left_in, (grad_pre, other_in), 2, False)
    got_in_a, got_in_b = swap(send_in_a, "y", 1), swap(send_in_b, "y", 3)

    grad_pre, _ = tie(grad_pre, send_in_a)
    grad_slots = slot_grads_of(pos, grad_pre, weight_in)
    grad_slots, flat_combine = tie(grad_slots, flat_combine)
    flat_grads = exchange(
        grad_slots.reshape(experts, capacity, model_width), GROUP
    ).reshape(slot_count, model_width)

    my_out, grad_pre, flat_combine, _ = tie(my_out, grad_pre, flat_combine, grad_slots)
    keep_out_a, keep_out_b = parts(pos, left_out, (my_out, other_out), 0, True)
    grad_pre, _ = tie(grad_pre, keep_out_a)
    keep_in_a, keep_in_b = parts(pos, left_in, (grad_pre, other_in), 2, True)
    flat_combine, _ = tie(flat_combine, keep_in_a)

    combine_wide = flat_combine.astype(F32)[:, None]
    combine_grad = jnp.stack(
        [
            jnp.sum(jnp.where(first_hit, combine_wide, 0.0), axis=0),
            jnp.sum(jnp.where(second_hit, combine_wide, 0.0), axis=0),
        ],
        axis=1,
    )
    weighted_sum = jnp.sum(combine_grad * combine, axis=1)
    chosen_grad = keep_float * (combine_grad - weighted_sum[:, None]) / denominator[:, None]
    probs_grad = jnp.sum(jnp.where(picked, chosen_grad[:, :, None], 0.0), axis=1)
    logit_grad = router_probs * (
        probs_grad - jnp.sum(probs_grad * router_probs, axis=1, keepdims=True)
    )
    logit_b = logit_grad.astype(BF16)

    def router_steps(value, steps):
        for axis, mask in steps:
            value = value + swap(value, axis, mask)
        return value

    router_part = contract_rows(logit_b, tokens) * grad_scale

    def far_of(keep, got):
        rows = keep.shape[0] // 2
        return (keep[rows:] + got[rows:].astype(F32)).astype(BF16)

    def near_of(keep, got, got_far):
        rows = keep.shape[0] // 2
        return keep[:rows] + got[:rows].astype(F32) + got_far.astype(F32)

    got_out_a, got_out_b, _ = tie(got_out_a, got_out_b, router_part)
    far_a, far_b = far_of(keep_out_a, got_out_a), far_of(keep_out_b, got_out_b)
    far_out_a, far_out_b = swap(far_a, "y", 3), swap(far_b, "y", 1)

    got_in_a, got_in_b, _, _ = tie(got_in_a, got_in_b, far_a, far_b)
    far_a, far_b = far_of(keep_in_a, got_in_a), far_of(keep_in_b, got_in_b)
    far_in_a, far_in_b = swap(far_a, "y", 3), swap(far_b, "y", 1)
    router_part, _, _ = tie(router_part, far_a, far_b)
    router_part = router_steps(router_part, ROUTER_STEPS[:1])

    far_out_a, far_out_b, _ = tie(far_out_a, far_out_b, router_part)
    near_a = near_of(keep_out_a, got_out_a, far_out_a)
    near_b = near_of(keep_out_b, got_out_b, far_out_b)
    mine_out, zh_out = zh_sum(near_a, near_b)
    flat_grads, _, _ = tie(flat_grads, near_a, near_b)

    expert_grad = contract_rows(dispatch, flat_grads)
    grad_tokens = (expert_grad + contract_cols(logit_b, router_weight)).astype(BF16)
    router_part, _ = tie(router_part, grad_tokens)
    router_part = router_steps(router_part, ROUTER_STEPS[1:2])

    far_in_a, far_in_b, _ = tie(far_in_a, far_in_b, router_part)
    near_a = near_of(keep_in_a, got_in_a, far_in_a)
    near_b = near_of(keep_in_b, got_in_b, far_in_b)
    mine_in, zh_in = zh_sum(near_a, near_b)
    router_part, _, _ = tie(router_part, near_a, near_b)
    router_part = router_steps(router_part, ROUTER_STEPS[2:5])

    mine_out, zh_out, _ = tie(mine_out, zh_out, router_part)
    mine_out = zh_total(mine_out, zh_out, grad_scale)
    router_part, _ = tie(router_part, mine_out)
    router_part = router_steps(router_part, ROUTER_STEPS[5:6])
    mine_in, zh_in, _ = tie(mine_in, zh_in, router_part)
    mine_in = zh_total(mine_in, zh_in, grad_scale)
    router_part, _ = tie(router_part, mine_in)
    router_part = router_steps(router_part, ROUTER_STEPS[6:])
    return (grad_tokens, router_part.T, core_total(mine_in), core_total(mine_out))


def solution(mesh):
    fine = Mesh(mesh.devices.reshape(FINE_SHAPE), FINE)
    placed = (
        P(FINE, None),
        P(FINE, None),
        P(),
        P(GROUP, None, None),
        P(GROUP, None, None),
        P(FINE, None),
        P(FINE, None),
        P(FINE, None),
    )
    return jax.shard_map(
        per_device,
        mesh=fine,
        in_specs=placed,
        out_specs=(
            P(FINE, None),
            P(),
            P(GROUP, ("y", "zh", "core"), None),
            P(GROUP, ("y", "zh", "core"), None),
        ),
        check_vma=False,
    )
```

```python
import jax
import jax.numpy as jnp
from jax import lax
from jax.experimental import pallas as pl
from jax.experimental.pallas import tpu as pltpu
from jax.sharding import Mesh, PartitionSpec as P

FINE = ("y", "zh", "core", "x", "zl")
FINE_SHAPE = (4, 4, 2, 4, 2)
GROUP = ("x", "zl")
EXTRA = 128
ROUTER_STEPS = (
    ("core", 1),
    ("x", 1),
    ("x", 3),
    ("zl", 1),
    ("y", 1),
    ("y", 3),
    ("zh", 1),
    ("zh", 3),
)
COST_IN = 1000
COST_SLOTS = 1000
F32 = jnp.float32
BF16 = jnp.bfloat16


def gelu_parts(hidden_pre):
    normal_cdf = 0.5 * (1.0 + jax.scipy.special.erf(hidden_pre * 0.7071067811865476))
    normal_pdf = jnp.exp(-0.5 * hidden_pre * hidden_pre) * 0.3989422804014327
    return (normal_cdf, normal_pdf)


def contract_rows(left, right):
    return lax.dot_general(left, right, (((0,), (0,)), ((), ())), preferred_element_type=F32)


def contract_cols(left, right):
    return lax.dot_general(left, right, (((1,), (1,)), ((), ())), preferred_element_type=F32)


def swap(values, axis, mask):
    size = lax.axis_size(axis)
    return lax.ppermute(values, axis, [(i, i ^ mask) for i in range(size)])


def exchange(values, axes):
    return lax.all_to_all(values, axes, split_axis=0, concat_axis=0, tiled=True)


def tie(*values):
    return lax.optimization_barrier(values)


def call(body, pos, inputs, outputs, cost=1000):
    vmem = pl.BlockSpec(memory_space=pltpu.VMEM)
    return pl.pallas_call(
        body,
        in_specs=[pl.BlockSpec(memory_space=pltpu.SMEM)] + [vmem] * len(inputs),
        out_specs=[vmem] * len(outputs),
        out_shape=[jax.ShapeDtypeStruct(shape, dtype) for shape, dtype in outputs],
        cost_estimate=pl.CostEstimate(flops=cost, bytes_accessed=1000, transcendentals=0),
        compiler_params=pltpu.CompilerParams(vmem_limit_bytes=20 * 1024 * 1024),
    )(pos, *inputs)


def gate_of(pos, lanes):
    lane = lax.broadcasted_iota(jnp.int32, lanes.shape, 1)
    return jnp.sum(jnp.where(lane == pos[2], lanes.astype(F32), 0.0), axis=1, keepdims=True)


def scale_grads(pos, received, expert_out):
    slots, wide = received.shape
    width = wide - EXTRA
    half = width // 2
    rows = slots // 4

    def body(pos_ref, rec, expert, mine, give, gate_grad):
        core = pos_ref[1]
        for r in range(0, slots, rows):
            at = slice(r, r + rows)
            gate = gate_of(pos_ref, rec[at, width:])
            for out, which in ((mine, core), (give, 1 - core)):
                start = pl.multiple_of(which * half, half)
                out[at, :] = (gate * rec[at, pl.ds(start, half)].astype(F32)).astype(BF16)
            gate_grad[at, :] = jnp.sum(
                expert[at, :] * rec[at, :width].astype(F32), axis=1, keepdims=True
            )

    return call(
        body,
        pos,
        [received, expert_out],
        [((slots, half), BF16), ((slots, half), BF16), ((slots, 1), F32)],
    )


def pre_grads(pos, received, weight_out, slope):
    slots, wide = received.shape
    hidden, width = weight_out.shape
    step = hidden // 4

    def body(pos_ref, rec, weight, slope_ref, grad_pre, give):
        gate = gate_of(pos_ref, rec[:, width:])
        for i in range(4):
            at = slice(i * step, (i + 1) * step)
            grad_act = lax.dot_general(
                rec[:, :width], weight[at, :], (((1,), (1,)), ((), ())), preferred_element_type=F32
            )
            grad_pre[:, at] = (gate * grad_act * slope_ref[:, at]).astype(BF16)
        start = pl.multiple_of((1 - pos_ref[1]) * (hidden // 2), hidden // 2)
        give[...] = grad_pre[:, pl.ds(start, hidden // 2)]

    return call(
        body,
        pos,
        [received, weight_out, slope],
        [((slots, hidden), BF16), ((slots, hidden // 2), BF16)],
    )


def parts(pos, left, right, own_offset, kept, cost=1000):
    left_mine, left_other = left
    right_mine, right_other = right
    width = left_mine.shape[1] // 4
    cols = right_other.shape[1] // 2
    dtype = F32 if kept else BF16
    masks = ((0, 3), (0, 1)) if kept else ((1, 2), (3, 2))

    def body(pos_ref, lm, lo, rm, ro, *outs):
        dims = (((0,), (0,)), ((), ()))
        for i in range(2):
            own = pl.multiple_of((own_offset * pos_ref[1] + i) * cols, cols)
            for j in range(2):
                start = pl.multiple_of((pos_ref[0] ^ masks[i][j]) * width, width)
                value = lax.dot_general(
                    lm[:, pl.ds(start, width)],
                    rm[:, pl.ds(own, cols)],
                    dims,
                    preferred_element_type=F32,
                )
                value = value + lax.dot_general(
                    lo[:, pl.ds(start, width)],
                    ro[:, i * cols : (i + 1) * cols],
                    dims,
                    preferred_element_type=F32,
                )
                outs[i][j * width : (j + 1) * width, :] = value.astype(dtype)

    return call(
        body,
        pos,
        [left_mine, left_other, right_mine, right_other],
        [((2 * width, cols), dtype)] * 2,
        cost,
    )


def slot_grads_of(pos, grad_pre, weight_in, cost=1000):
    slots, hidden = grad_pre.shape
    width = weight_in.shape[0]
    step = width // 4

    def body(pos_ref, grad, weight, out):
        for i in range(4):
            at = slice(i * step, (i + 1) * step)
            out[:, at] = lax.dot_general(
                grad[...], weight[at, :], (((1,), (1,)), ((), ())), preferred_element_type=F32
            ).astype(BF16)

    return call(body, pos, [grad_pre, weight_in], [((slots, width), BF16)], cost)[0]


def zh_sum(near_a, near_b):
    zh = lax.axis_index("zh")
    block = near_a.shape[0] // 4

    def rows_of(r):
        return jnp.concatenate(
            [
                lax.dynamic_slice_in_dim(near, (zh ^ r) * block, block, axis=0)
                for near in (near_a, near_b)
            ],
            axis=1,
        )

    return rows_of(0), [swap(rows_of(r).astype(BF16), "zh", r) for r in (1, 2, 3)]


def zh_total(mine, got, scale):
    for piece in got:
        mine = mine + piece.astype(F32)
    return mine * scale


def core_total(mine):
    core = lax.axis_index("core")
    share = mine.shape[0] // 2
    keep = lax.dynamic_slice_in_dim(mine, core * share, share, axis=0)
    give = lax.dynamic_slice_in_dim(mine, (1 - core) * share, share, axis=0)
    got = swap(give, "core", 1)
    first = jnp.where(core == 0, keep, got)
    second = jnp.where(core == 0, got, keep)
    return jnp.concatenate([first, second], axis=1)[None]


def per_device(
    tokens, grad_out, router_weight, weight_in, weight_out, expert_ids, slot_index, keep_mask
):
    tok_rows, model_width = tokens.shape
    experts = 8
    weight_in = weight_in[0]
    weight_out = weight_out[0]
    capacity = tok_rows * expert_ids.shape[1] // experts
    slot_count = experts * capacity
    grad_scale = float(tok_rows * 256) ** (-0.5)
    core = lax.axis_index("core")
    my_y = lax.axis_index("y")

    target = expert_ids * capacity + slot_index
    slot_iota = jnp.arange(slot_count, dtype=jnp.int32)[:, None]
    first_hit = (slot_iota == target[None, :, 0]) & (keep_mask[None, :, 0] == 1)
    second_hit = (slot_iota == target[None, :, 1]) & (keep_mask[None, :, 1] == 1)
    dispatch = (first_hit | second_hit).astype(BF16)

    send_tokens = jnp.dot(dispatch, tokens, preferred_element_type=F32).astype(BF16)
    slot_tokens = exchange(
        send_tokens.reshape(experts, capacity, model_width), GROUP
    ).reshape(slot_count, model_width)

    logits = jnp.dot(tokens, router_weight, preferred_element_type=F32)
    exp_logits = jnp.exp(logits)
    router_probs = exp_logits / jnp.sum(exp_logits, axis=1, keepdims=True)
    picked = expert_ids[:, :, None] == jnp.arange(experts, dtype=jnp.int32)[None, None, :]
    chosen = jnp.sum(jnp.where(picked, router_probs[:, None, :], 0.0), axis=2)
    keep_float = keep_mask.astype(F32)
    denominator = jnp.sum(keep_float * chosen, axis=1) + (1.0 - jnp.max(keep_float, axis=1))
    combine = keep_float * chosen / denominator[:, None]
    gate_lanes = jnp.sum(jnp.where(picked, combine[:, :, None], 0.0), axis=1).astype(BF16)
    gate_lanes = jnp.pad(gate_lanes, ((0, 0), (0, EXTRA - experts)))
    send_grads = jnp.dot(dispatch, grad_out, preferred_element_type=F32).astype(BF16)
    send_gates = jnp.dot(dispatch, gate_lanes, preferred_element_type=F32).astype(BF16)
    received = exchange(
        jnp.concatenate([send_grads, send_gates], axis=1).reshape(
            experts, capacity, model_width + EXTRA
        ),
        GROUP,
    ).reshape(slot_count, model_width + EXTRA)
    other_tokens = swap(slot_tokens, "core", 1)
    hidden_pre = jnp.dot(slot_tokens, weight_in, preferred_element_type=F32)
    normal_cdf, normal_pdf = gelu_parts(hidden_pre)
    hidden_act = (hidden_pre * normal_cdf).astype(BF16)
    act_slope = normal_cdf + hidden_pre * normal_pdf
    other_act = swap(hidden_act, "core", 1)
    left_in = (slot_tokens, other_tokens)
    left_out = (hidden_act, other_act)
    pos = jnp.stack([my_y, core, lax.axis_index(GROUP)]).astype(jnp.int32)

    expert_out = jnp.dot(hidden_act, weight_out, preferred_element_type=F32)

    received, left_in, left_out, act_slope, expert_out = tie(
        received, left_in, left_out, act_slope, expert_out
    )
    my_out, give_out, slot_combine_grad = scale_grads(pos, received, expert_out)
    other_out = swap(give_out, "core", 1)
    received, _ = tie(received, give_out)
    grad_pre, give_in = pre_grads(pos, received, weight_out, act_slope)
    other_in = swap(give_in, "core", 1)

    send_out_a, send_out_b = parts(pos, left_out, (my_out, other_out), 0, False)
    got_out_a, got_out_b = swap(send_out_a, "y", 1), swap(send_out_b, "y", 3)
    grad_pre, slot_combine_grad, _, _ = tie(grad_pre, slot_combine_grad, send_out_a, send_out_b)
    flat_combine = exchange(
        slot_combine_grad.astype(BF16).reshape(experts, capacity), GROUP
    ).reshape(slot_count)
    send_in_a, send_in_b = parts(pos, left_in, (grad_pre, other_in), 2, False, COST_IN)
    got_in_a, got_in_b = swap(send_in_a, "y", 1), swap(send_in_b, "y", 3)

    grad_pre, _, _ = tie(grad_pre, send_in_a, send_in_b)
    grad_slots = slot_grads_of(pos, grad_pre, weight_in, COST_SLOTS)
    grad_slots, flat_combine = tie(grad_slots, flat_combine)
    flat_grads = exchange(
        grad_slots.reshape(experts, capacity, model_width), GROUP
    ).reshape(slot_count, model_width)

    my_out, grad_pre, flat_combine, _ = tie(my_out, grad_pre, flat_combine, grad_slots)
    keep_out_a, keep_out_b = parts(pos, left_out, (my_out, other_out), 0, True)
    grad_pre, _ = tie(grad_pre, keep_out_a)
    keep_in_a, keep_in_b = parts(pos, left_in, (grad_pre, other_in), 2, True)

    def router_steps(value, steps):
        for axis, mask in steps:
            value = value + swap(value, axis, mask)
        return value

    def far_of(keep, got):
        rows = keep.shape[0] // 2
        return (keep[rows:] + got[rows:].astype(F32)).astype(BF16)

    def near_of(keep, got, got_far):
        rows = keep.shape[0] // 2
        return keep[:rows] + got[:rows].astype(F32) + got_far.astype(F32)

    got_out_a, got_out_b, _ = tie(got_out_a, got_out_b, keep_in_a)
    far_a, far_b = far_of(keep_out_a, got_out_a), far_of(keep_out_b, got_out_b)
    far_out_a, far_out_b = swap(far_a, "y", 3), swap(far_b, "y", 1)

    got_in_a, got_in_b, _, _ = tie(got_in_a, got_in_b, far_a, far_b)
    far_a, far_b = far_of(keep_in_a, got_in_a), far_of(keep_in_b, got_in_b)
    far_in_a, far_in_b = swap(far_a, "y", 3), swap(far_b, "y", 1)
    flat_combine, _, _ = tie(flat_combine, far_a, far_b)

    combine_wide = flat_combine.astype(F32)[:, None]
    combine_grad = jnp.stack(
        [
            jnp.sum(jnp.where(first_hit, combine_wide, 0.0), axis=0),
            jnp.sum(jnp.where(second_hit, combine_wide, 0.0), axis=0),
        ],
        axis=1,
    )
    weighted_sum = jnp.sum(combine_grad * combine, axis=1)
    chosen_grad = keep_float * (combine_grad - weighted_sum[:, None]) / denominator[:, None]
    probs_grad = jnp.sum(jnp.where(picked, chosen_grad[:, :, None], 0.0), axis=1)
    logit_grad = router_probs * (
        probs_grad - jnp.sum(probs_grad * router_probs, axis=1, keepdims=True)
    )
    logit_b = logit_grad.astype(BF16)

    router_part = contract_rows(logit_b, tokens) * grad_scale
    router_part = router_steps(router_part, ROUTER_STEPS[:1])

    far_out_a, far_out_b, _ = tie(far_out_a, far_out_b, router_part)
    near_a = near_of(keep_out_a, got_out_a, far_out_a)
    near_b = near_of(keep_out_b, got_out_b, far_out_b)
    mine_out, zh_out = zh_sum(near_a, near_b)
    flat_grads, _, _ = tie(flat_grads, near_a, near_b)

    expert_grad = contract_rows(dispatch, flat_grads)
    grad_tokens = (expert_grad + contract_cols(logit_b, router_weight)).astype(BF16)
    router_part, _ = tie(router_part, grad_tokens)
    router_part = router_steps(router_part, ROUTER_STEPS[1:2])

    far_in_a, far_in_b, _ = tie(far_in_a, far_in_b, router_part)
    near_a = near_of(keep_in_a, got_in_a, far_in_a)
    near_b = near_of(keep_in_b, got_in_b, far_in_b)
    mine_in, zh_in = zh_sum(near_a, near_b)
    router_part, _, _ = tie(router_part, near_a, near_b)
    router_part = router_steps(router_part, ROUTER_STEPS[2:5])

    mine_out, zh_out, _ = tie(mine_out, zh_out, router_part)
    mine_out = zh_total(mine_out, zh_out, grad_scale)
    router_part, _ = tie(router_part, mine_out)
    router_part = router_steps(router_part, ROUTER_STEPS[5:6])
    mine_in, zh_in, _ = tie(mine_in, zh_in, router_part)
    mine_in = zh_total(mine_in, zh_in, grad_scale)
    router_part, _ = tie(router_part, mine_in)
    router_part = router_steps(router_part, ROUTER_STEPS[6:])
    return (grad_tokens, router_part.T, core_total(mine_in), core_total(mine_out))


def solution(mesh):
    fine = Mesh(mesh.devices.reshape(FINE_SHAPE), FINE)
    placed = (
        P(FINE, None),
        P(FINE, None),
        P(),
        P(GROUP, None, None),
        P(GROUP, None, None),
        P(FINE, None),
        P(FINE, None),
        P(FINE, None),
    )
    return jax.shard_map(
        per_device,
        mesh=fine,
        in_specs=placed,
        out_specs=(
            P(FINE, None),
            P(),
            P(GROUP, ("y", "zh", "core"), None),
            P(GROUP, ("y", "zh", "core"), None),
        ),
        check_vma=False,
    )
```

```python
import jax
import jax.numpy as jnp
from jax import lax
from jax.experimental import pallas as pl
from jax.experimental.pallas import tpu as pltpu
from jax.sharding import Mesh, PartitionSpec as P

FINE = ("y", "zh", "core", "x", "zl")
FINE_SHAPE = (4, 4, 2, 4, 2)
GROUP = ("x", "zl")
EXTRA = 128
ROUTER_STEPS = (
    ("core", 1),
    ("x", 1),
    ("x", 3),
    ("zl", 1),
    ("y", 1),
    ("y", 3),
    ("zh", 1),
    ("zh", 3),
)
VMEM_LIMIT = 14 * 1024 * 1024
F32 = jnp.float32
BF16 = jnp.bfloat16


def gelu_parts(hidden_pre):
    normal_cdf = 0.5 * (1.0 + jax.scipy.special.erf(hidden_pre * 0.7071067811865476))
    normal_pdf = jnp.exp(-0.5 * hidden_pre * hidden_pre) * 0.3989422804014327
    return (normal_cdf, normal_pdf)


def contract_rows(left, right):
    return lax.dot_general(left, right, (((0,), (0,)), ((), ())), preferred_element_type=F32)


def contract_cols(left, right):
    return lax.dot_general(left, right, (((1,), (1,)), ((), ())), preferred_element_type=F32)


def swap(values, axis, mask):
    size = lax.axis_size(axis)
    return lax.ppermute(values, axis, [(i, i ^ mask) for i in range(size)])


def exchange(values, axes):
    return lax.all_to_all(values, axes, split_axis=0, concat_axis=0, tiled=True)


def tie(*values):
    return lax.optimization_barrier(values)


def call(body, pos, inputs, outputs):
    vmem = pl.BlockSpec(memory_space=pltpu.VMEM)
    return pl.pallas_call(
        body,
        in_specs=[pl.BlockSpec(memory_space=pltpu.SMEM)] + [vmem] * len(inputs),
        out_specs=[vmem] * len(outputs),
        out_shape=[jax.ShapeDtypeStruct(shape, dtype) for shape, dtype in outputs],
        cost_estimate=pl.CostEstimate(flops=1000, bytes_accessed=1000, transcendentals=0),
        compiler_params=pltpu.CompilerParams(vmem_limit_bytes=VMEM_LIMIT),
    )(pos, *inputs)


def gate_of(pos, lanes):
    lane = lax.broadcasted_iota(jnp.int32, lanes.shape, 1)
    return jnp.sum(jnp.where(lane == pos[2], lanes.astype(F32), 0.0), axis=1, keepdims=True)


def scale_grads(pos, received, expert_out):
    slots, wide = received.shape
    width = wide - EXTRA
    half = width // 2
    rows = slots // 4

    def body(pos_ref, rec, expert, mine, give, gate_grad):
        core = pos_ref[1]
        for r in range(0, slots, rows):
            at = slice(r, r + rows)
            gate = gate_of(pos_ref, rec[at, width:])
            for out, which in ((mine, core), (give, 1 - core)):
                start = pl.multiple_of(which * half, half)
                out[at, :] = (gate * rec[at, pl.ds(start, half)].astype(F32)).astype(BF16)
            gate_grad[at, :] = jnp.sum(
                expert[at, :].astype(F32) * rec[at, :width].astype(F32),
                axis=1,
                keepdims=True,
            )

    return call(
        body,
        pos,
        [received, expert_out],
        [((slots, half), BF16), ((slots, half), BF16), ((slots, 1), F32)],
    )


def pre_grads(pos, received, weight_out, slope):
    slots, wide = received.shape
    hidden, width = weight_out.shape
    step = hidden // 4

    def body(pos_ref, rec, weight, slope_ref, grad_pre, give):
        gate = gate_of(pos_ref, rec[:, width:])
        for i in range(4):
            at = slice(i * step, (i + 1) * step)
            grad_act = lax.dot_general(
                rec[:, :width], weight[at, :], (((1,), (1,)), ((), ())), preferred_element_type=F32
            )
            grad_pre[:, at] = (gate * grad_act * slope_ref[:, at]).astype(BF16)
        start = pl.multiple_of((1 - pos_ref[1]) * (hidden // 2), hidden // 2)
        give[...] = grad_pre[:, pl.ds(start, hidden // 2)]

    return call(
        body,
        pos,
        [received, weight_out, slope],
        [((slots, hidden), BF16), ((slots, hidden // 2), BF16)],
    )


def row_products(pos_ref, refs, own_offset, masks, width, cols):
    lm, lo, rm, ro = refs
    dims = (((0,), (0,)), ((), ()))
    for i in range(2):
        own = pl.multiple_of((own_offset * pos_ref[1] + i) * cols, cols)
        for j in range(2):
            start = pl.multiple_of((pos_ref[0] ^ masks[i][j]) * width, width)
            value = lax.dot_general(
                lm[:, pl.ds(start, width)],
                rm[:, pl.ds(own, cols)],
                dims,
                preferred_element_type=F32,
            )
            value = value + lax.dot_general(
                lo[:, pl.ds(start, width)],
                ro[:, i * cols : (i + 1) * cols],
                dims,
                preferred_element_type=F32,
            )
            yield i, j, value


def sent_parts(pos, left, right, own_offset):
    width = left[0].shape[1] // 4
    cols = right[1].shape[1] // 2

    def body(pos_ref, lm, lo, rm, ro, *outs):
        refs = (lm, lo, rm, ro)
        for i, j, value in row_products(
            pos_ref, refs, own_offset, ((1, 2), (3, 2)), width, cols
        ):
            outs[i][j * width : (j + 1) * width, :] = value.astype(BF16)

    return call(body, pos, [*left, *right], [((2 * width, cols), BF16)] * 2)


def kept_parts(pos, left, right, own_offset, got):
    width = left[0].shape[1] // 4
    cols = right[1].shape[1] // 2

    def body(pos_ref, lm, lo, rm, ro, got_a, got_b, near_a, near_b, far_a, far_b):
        refs = (lm, lo, rm, ro)
        for i, j, value in row_products(
            pos_ref, refs, own_offset, ((0, 3), (0, 1)), width, cols
        ):
            value = value + (got_a, got_b)[i][j * width : (j + 1) * width, :].astype(F32)
            if j == 0:
                (near_a, near_b)[i][...] = value
            else:
                (far_a, far_b)[i][...] = value.astype(BF16)

    return call(
        body,
        pos,
        [*left, *right, *got],
        [((width, cols), F32)] * 2 + [((width, cols), BF16)] * 2,
    )


def zh_pieces(pos, near, far, scale):
    rows, cols = near[0].shape
    block = rows // 4

    def body(pos_ref, near_a, near_b, far_a, far_b, mine, *pieces):
        for r in range(4):
            at = pl.ds(pl.multiple_of((pos_ref[3] ^ r) * block, block), block)
            for i, (n, f) in enumerate(((near_a, far_a), (near_b, far_b))):
                value = (n[at, :] + f[at, :].astype(F32)) * scale
                here = slice(i * cols, (i + 1) * cols)
                if r == 0:
                    mine[:, here] = value
                else:
                    pieces[r - 1][:, here] = value.astype(BF16)

    shape = (block, 2 * cols)
    return call(body, pos, [*near, *far], [(shape, F32)] + [(shape, BF16)] * 3)


def zh_total(pos, mine, got):
    rows, cols = mine.shape
    share = rows // 2

    def body(pos_ref, own, one, two, three, keep, give):
        core = pos_ref[1]
        for out, which in ((keep, core), (give, 1 - core)):
            at = pl.ds(pl.multiple_of(which * share, share), share)
            value = own[at, :] + one[at, :].astype(F32)
            out[...] = value + two[at, :].astype(F32) + three[at, :].astype(F32)

    return call(body, pos, [mine, *got], [((share, cols), F32)] * 2)


def both_halves(pos, keep, got):
    rows, cols = keep.shape

    def body(pos_ref, own, other, out):
        core = pos_ref[1]
        out[:, pl.ds(pl.multiple_of(core * cols, cols), cols)] = own[...]
        out[:, pl.ds(pl.multiple_of((1 - core) * cols, cols), cols)] = other[...]

    return call(body, pos, [keep, got], [((rows, 2 * cols), F32)])[0][None]


def token_grads(pos, dispatch, flat_grads, logit_lanes, weight_lanes):
    rows, width = dispatch.shape[1], flat_grads.shape[1]
    step = width // 4

    def body(pos_ref, disp, flat, logit, weight, out):
        for i in range(4):
            at = slice(i * step, (i + 1) * step)
            value = lax.dot_general(
                disp[...], flat[:, at], (((0,), (0,)), ((), ())), preferred_element_type=F32
            )
            value = value + lax.dot_general(
                logit[...], weight[at, :], (((1,), (1,)), ((), ())), preferred_element_type=F32
            )
            out[:, at] = value.astype(BF16)

    return call(
        body, pos, [dispatch, flat_grads, logit_lanes, weight_lanes], [((rows, width), BF16)]
    )[0]


def slot_grads_of(pos, grad_pre, weight_in):
    slots, hidden = grad_pre.shape
    width = weight_in.shape[0]
    step = width // 4

    def body(pos_ref, grad, weight, out):
        for i in range(4):
            at = slice(i * step, (i + 1) * step)
            out[:, at] = lax.dot_general(
                grad[...], weight[at, :], (((1,), (1,)), ((), ())), preferred_element_type=F32
            ).astype(BF16)

    return call(body, pos, [grad_pre, weight_in], [((slots, width), BF16)])[0]


def per_device(
    tokens, grad_out, router_weight, weight_in, weight_out, expert_ids, slot_index, keep_mask
):
    tok_rows, model_width = tokens.shape
    experts = 8
    weight_in = weight_in[0]
    weight_out = weight_out[0]
    capacity = tok_rows * expert_ids.shape[1] // experts
    slot_count = experts * capacity
    grad_scale = float(tok_rows * 256) ** (-0.5)
    core = lax.axis_index("core")
    my_y = lax.axis_index("y")

    target = expert_ids * capacity + slot_index
    slot_iota = jnp.arange(slot_count, dtype=jnp.int32)[:, None]
    first_hit = (slot_iota == target[None, :, 0]) & (keep_mask[None, :, 0] == 1)
    second_hit = (slot_iota == target[None, :, 1]) & (keep_mask[None, :, 1] == 1)
    dispatch = (first_hit | second_hit).astype(BF16)

    send_tokens = jnp.dot(dispatch, tokens, preferred_element_type=F32).astype(BF16)
    slot_tokens = exchange(
        send_tokens.reshape(experts, capacity, model_width), GROUP
    ).reshape(slot_count, model_width)

    logits = jnp.dot(tokens, router_weight, preferred_element_type=F32)
    exp_logits = jnp.exp(logits)
    router_probs = exp_logits / jnp.sum(exp_logits, axis=1, keepdims=True)
    picked = expert_ids[:, :, None] == jnp.arange(experts, dtype=jnp.int32)[None, None, :]
    chosen = jnp.sum(jnp.where(picked, router_probs[:, None, :], 0.0), axis=2)
    keep_float = keep_mask.astype(F32)
    denominator = jnp.sum(keep_float * chosen, axis=1) + (1.0 - jnp.max(keep_float, axis=1))
    combine = keep_float * chosen / denominator[:, None]
    gate_lanes = jnp.sum(jnp.where(picked, combine[:, :, None], 0.0), axis=1).astype(BF16)
    gate_lanes = jnp.pad(gate_lanes, ((0, 0), (0, EXTRA - experts)))
    send_grads = jnp.dot(dispatch, grad_out, preferred_element_type=F32).astype(BF16)
    send_gates = jnp.dot(dispatch, gate_lanes, preferred_element_type=F32).astype(BF16)
    received = exchange(
        jnp.concatenate([send_grads, send_gates], axis=1).reshape(
            experts, capacity, model_width + EXTRA
        ),
        GROUP,
    ).reshape(slot_count, model_width + EXTRA)
    other_tokens = swap(slot_tokens, "core", 1)
    hidden_pre = jnp.dot(slot_tokens, weight_in, preferred_element_type=F32)
    normal_cdf, normal_pdf = gelu_parts(hidden_pre)
    hidden_act = (hidden_pre * normal_cdf).astype(BF16)
    act_slope = normal_cdf + hidden_pre * normal_pdf
    other_act = swap(hidden_act, "core", 1)
    left_in = (slot_tokens, other_tokens)
    left_out = (hidden_act, other_act)
    pos = jnp.stack([my_y, core, lax.axis_index(GROUP), lax.axis_index("zh")]).astype(jnp.int32)

    expert_out = jnp.dot(hidden_act, weight_out, preferred_element_type=F32).astype(BF16)
    weight_lanes = jnp.pad(router_weight, ((0, 0), (0, EXTRA - experts)))

    received, left_in, left_out, act_slope, expert_out = tie(
        received, left_in, left_out, act_slope, expert_out
    )
    my_out, give_out, slot_combine_grad = scale_grads(pos, received, expert_out)
    other_out = swap(give_out, "core", 1)
    flat_combine = exchange(
        slot_combine_grad.astype(BF16).reshape(experts, capacity), GROUP
    ).reshape(slot_count)
    received, _ = tie(received, give_out)
    grad_pre, give_in = pre_grads(pos, received, weight_out, act_slope)
    other_in = swap(give_in, "core", 1)

    sent = sent_parts(pos, left_out, (my_out, other_out), 0)
    got_out = (swap(sent[0], "y", 1), swap(sent[1], "y", 3))
    pre_for_slots, _ = tie(grad_pre, sent)
    grad_slots = slot_grads_of(pos, pre_for_slots, weight_in)
    grad_slots, flat_combine = tie(grad_slots, flat_combine)
    flat_grads = exchange(
        grad_slots.reshape(experts, capacity, model_width), GROUP
    ).reshape(slot_count, model_width)
    grad_pre, flat_combine, _ = tie(grad_pre, flat_combine, grad_slots)
    sent = sent_parts(pos, left_in, (grad_pre, other_in), 2)
    got_in = (swap(sent[0], "y", 1), swap(sent[1], "y", 3))
    my_out, flat_combine, _ = tie(my_out, flat_combine, sent)

    combine_wide = flat_combine.astype(F32)[:, None]
    combine_grad = jnp.stack(
        [
            jnp.sum(jnp.where(first_hit, combine_wide, 0.0), axis=0),
            jnp.sum(jnp.where(second_hit, combine_wide, 0.0), axis=0),
        ],
        axis=1,
    )
    weighted_sum = jnp.sum(combine_grad * combine, axis=1)
    chosen_grad = keep_float * (combine_grad - weighted_sum[:, None]) / denominator[:, None]
    probs_grad = jnp.sum(jnp.where(picked, chosen_grad[:, :, None], 0.0), axis=1)
    logit_grad = router_probs * (
        probs_grad - jnp.sum(probs_grad * router_probs, axis=1, keepdims=True)
    )
    logit_b = logit_grad.astype(BF16)

    logit_lanes = jnp.pad(logit_b, ((0, 0), (0, EXTRA - experts)))

    router_part = contract_rows(logit_b, tokens) * grad_scale

    def router_step(step, value, *until):
        got = swap(value, *ROUTER_STEPS[step])
        value, got, _ = tie(value, got, until)
        return value + got

    my_out, _ = tie(my_out, router_part)
    *near_out, far_a, far_b = kept_parts(pos, left_out, (my_out, other_out), 0, got_out)
    far_out = (swap(far_a, "y", 3), swap(far_b, "y", 1))
    router_part = router_step(0, router_part, far_a)

    grad_pre, router_part, _ = tie(grad_pre, router_part, far_a)
    *near_in, far_a, far_b = kept_parts(pos, left_in, (grad_pre, other_in), 2, got_in)
    far_in = (swap(far_a, "y", 3), swap(far_b, "y", 1))
    router_part = router_step(1, router_part, far_a)

    near_out, router_part, _ = tie(near_out, router_part, far_a)
    mine_out, *pieces = zh_pieces(pos, near_out, far_out, grad_scale)
    zh_out = [swap(piece, "zh", r + 1) for r, piece in enumerate(pieces)]
    router_part = router_step(2, router_part, mine_out)

    near_in, router_part, _ = tie(near_in, router_part, mine_out)
    mine_in, *pieces = zh_pieces(pos, near_in, far_in, grad_scale)
    zh_in = [swap(piece, "zh", r + 1) for r, piece in enumerate(pieces)]
    router_part = router_step(3, router_part, mine_in)

    mine_out, router_part, _ = tie(mine_out, router_part, mine_in)
    keep_out, give = zh_total(pos, mine_out, zh_out)
    other_half_out = swap(give, "core", 1)
    router_part = router_step(4, router_part, keep_out)

    mine_in, router_part, _ = tie(mine_in, router_part, keep_out)
    keep_in, give = zh_total(pos, mine_in, zh_in)
    other_half_in = swap(give, "core", 1)
    router_part = router_step(5, router_part, keep_in)

    dispatch, router_part, _ = tie(dispatch, router_part, keep_in)
    grad_tokens = token_grads(pos, dispatch, flat_grads, logit_lanes, weight_lanes)
    router_part = router_step(6, router_part, grad_tokens)
    router_part = router_step(7, router_part)
    outer_share = both_halves(pos, keep_out, other_half_out)
    inner_share = both_halves(pos, keep_in, other_half_in)
    return (grad_tokens, router_part.T, inner_share, outer_share)


def solution(mesh):
    fine = Mesh(mesh.devices.reshape(FINE_SHAPE), FINE)
    placed = (
        P(FINE, None),
        P(FINE, None),
        P(),
        P(GROUP, None, None),
        P(GROUP, None, None),
        P(FINE, None),
        P(FINE, None),
        P(FINE, None),
    )
    return jax.shard_map(
        per_device,
        mesh=fine,
        in_specs=placed,
        out_specs=(
            P(FINE, None),
            P(),
            P(GROUP, ("y", "zh", "core"), None),
            P(GROUP, ("y", "zh", "core"), None),
        ),
        check_vma=False,
    )
```

```python
import jax
import jax.numpy as jnp
from jax import lax
from jax.experimental import pallas as pl
from jax.experimental.pallas import tpu as pltpu
from jax.sharding import Mesh, PartitionSpec as P

FINE = ("y", "zh", "core", "x", "zl")
FINE_SHAPE = (4, 4, 2, 4, 2)
GROUP = ("x", "zl")
EXTRA = 128
ROUTER_STEPS = (
    ("core", 1),
    ("x", 1),
    ("x", 3),
    ("zl", 1),
    ("y", 1),
    ("y", 3),
    ("zh", 1),
    ("zh", 3),
)
VMEM_LIMIT = 14 * 1024 * 1024
LONG = 60_000_000_000
F32 = jnp.float32
BF16 = jnp.bfloat16


def gelu_parts(hidden_pre):
    normal_cdf = 0.5 * (1.0 + jax.scipy.special.erf(hidden_pre * 0.7071067811865476))
    normal_pdf = jnp.exp(-0.5 * hidden_pre * hidden_pre) * 0.3989422804014327
    return (normal_cdf, normal_pdf)


def contract_rows(left, right):
    return lax.dot_general(left, right, (((0,), (0,)), ((), ())), preferred_element_type=F32)


def contract_cols(left, right):
    return lax.dot_general(left, right, (((1,), (1,)), ((), ())), preferred_element_type=F32)


def swap(values, axis, mask):
    size = lax.axis_size(axis)
    return lax.ppermute(values, axis, [(i, i ^ mask) for i in range(size)])


def exchange(values, axes):
    return lax.all_to_all(values, axes, split_axis=0, concat_axis=0, tiled=True)


def tie(*values):
    return lax.optimization_barrier(values)


def call(body, pos, inputs, outputs, flops=1000):
    vmem = pl.BlockSpec(memory_space=pltpu.VMEM)
    return pl.pallas_call(
        body,
        in_specs=[pl.BlockSpec(memory_space=pltpu.SMEM)] + [vmem] * len(inputs),
        out_specs=[vmem] * len(outputs),
        out_shape=[jax.ShapeDtypeStruct(shape, dtype) for shape, dtype in outputs],
        cost_estimate=pl.CostEstimate(flops=flops, bytes_accessed=1000, transcendentals=0),
        compiler_params=pltpu.CompilerParams(vmem_limit_bytes=VMEM_LIMIT),
    )(pos, *inputs)


def gate_of(pos, lanes):
    lane = lax.broadcasted_iota(jnp.int32, lanes.shape, 1)
    return jnp.sum(jnp.where(lane == pos[2], lanes.astype(F32), 0.0), axis=1, keepdims=True)


def scale_grads(pos, received):
    slots, wide = received.shape
    half = (wide - EXTRA) // 2
    rows = slots // 4

    def body(pos_ref, rec, mine, give):
        core = pos_ref[1]
        for r in range(0, slots, rows):
            at = slice(r, r + rows)
            gate = gate_of(pos_ref, rec[at, 2 * half :])
            for out, which in ((mine, core), (give, 1 - core)):
                start = pl.multiple_of(which * half, half)
                out[at, :] = (gate * rec[at, pl.ds(start, half)].astype(F32)).astype(BF16)

    return call(body, pos, [received], [((slots, half), BF16)] * 2)


def pre_grads(pos, received, weight_out, act, slope):
    slots, wide = received.shape
    hidden, width = weight_out.shape
    step = hidden // 4

    def body(pos_ref, rec, weight, act_ref, slope_ref, grad_pre, give, gate_grad):
        gate = gate_of(pos_ref, rec[:, width:])
        total = None
        for i in range(4):
            at = slice(i * step, (i + 1) * step)
            grad_act = lax.dot_general(
                rec[:, :width], weight[at, :], (((1,), (1,)), ((), ())), preferred_element_type=F32
            )
            part = jnp.sum(act_ref[:, at].astype(F32) * grad_act, axis=1, keepdims=True)
            total = part if total is None else total + part
            grad_pre[:, at] = (gate * grad_act * slope_ref[:, at]).astype(BF16)
        gate_grad[...] = total
        start = pl.multiple_of((1 - pos_ref[1]) * (hidden // 2), hidden // 2)
        give[...] = grad_pre[:, pl.ds(start, hidden // 2)]

    return call(
        body,
        pos,
        [received, weight_out, act, slope],
        [((slots, hidden), BF16), ((slots, hidden // 2), BF16), ((slots, 1), F32)],
    )


def row_products(pos_ref, refs, own_offset, masks, width, cols):
    lm, lo, rm, ro = refs
    dims = (((0,), (0,)), ((), ()))
    for i in range(2):
        own = pl.multiple_of((own_offset * pos_ref[1] + i) * cols, cols)
        for j in range(2):
            start = pl.multiple_of((pos_ref[0] ^ masks[i][j]) * width, width)
            value = lax.dot_general(
                lm[:, pl.ds(start, width)],
                rm[:, pl.ds(own, cols)],
                dims,
                preferred_element_type=F32,
            )
            value = value + lax.dot_general(
                lo[:, pl.ds(start, width)],
                ro[:, i * cols : (i + 1) * cols],
                dims,
                preferred_element_type=F32,
            )
            yield i, j, value


def sent_parts(pos, left_out, right_out, left_in, right_in):
    width_out, width_in = left_out[0].shape[1] // 4, left_in[0].shape[1] // 4
    cols_out, cols_in = right_out[1].shape[1] // 2, right_in[1].shape[1] // 2
    masks = ((1, 2), (3, 2))

    def body(pos_ref, *refs):
        outs = refs[8:]
        for i, j, value in row_products(pos_ref, refs[:4], 0, masks, width_out, cols_out):
            outs[i][j * width_out : (j + 1) * width_out, :] = value.astype(BF16)
        for i, j, value in row_products(pos_ref, refs[4:8], 2, masks, width_in, cols_in):
            outs[i][2 * width_out :, j * cols_in : (j + 1) * cols_in] = value.astype(BF16)

    return call(
        body,
        pos,
        [*left_out, *right_out, *left_in, *right_in],
        [((2 * width_out + width_in, cols_out), BF16)] * 2,
    )


def kept_parts(pos, left_out, right_out, left_in, right_in, got):
    width_out, width_in = left_out[0].shape[1] // 4, left_in[0].shape[1] // 4
    cols_out, cols_in = right_out[1].shape[1] // 2, right_in[1].shape[1] // 2
    masks = ((0, 3), (0, 1))
    half = width_in // 2

    def body(pos_ref, *refs):
        arrived = refs[8:10]
        near_out, near_in, far = refs[10:12], refs[12:14], refs[14:16]
        for i, j, value in row_products(pos_ref, refs[:4], 0, masks, width_out, cols_out):
            at = slice(j * width_out, (j + 1) * width_out)
            value = value + arrived[i][at, :].astype(F32)
            if j == 0:
                near_out[i][...] = value
            else:
                far[i][:width_out, :] = value.astype(BF16)
        for i, j, value in row_products(pos_ref, refs[4:8], 2, masks, width_in, cols_in):
            at = slice(j * cols_in, (j + 1) * cols_in)
            value = value + arrived[i][2 * width_out :, at].astype(F32)
            if j == 0:
                near_in[i][...] = value
            else:
                value = value.astype(BF16)
                far[i][width_out:, :cols_in] = value[:half, :]
                far[i][width_out:, cols_in:] = value[half:, :]

    return call(
        body,
        pos,
        [*left_out, *right_out, *left_in, *right_in, *got],
        [((width_out, cols_out), F32)] * 2
        + [((width_in, cols_in), F32)] * 2
        + [((width_out + half, cols_out), BF16)] * 2,
        LONG,
    )


def zh_pieces(pos, near_out, near_in, far, scale):
    rows_out, cols_out = near_out[0].shape
    rows_in, cols_in = near_in[0].shape
    half = rows_in // 2
    share_out, share_in = rows_out // 8, rows_in // 8

    def body(pos_ref, out_a, out_b, in_a, in_b, far_a, far_b, pieces):
        for i, (out, inner, arrived) in enumerate(((out_a, in_a, far_a), (out_b, in_b, far_b))):
            value = (out[...] + arrived[:rows_out, :].astype(F32)) * scale
            value = value.astype(BF16).reshape(8, share_out, cols_out)
            pieces[:, :share_out, i * cols_out : (i + 1) * cols_out] = value
            for k in range(2):
                value = inner[k * half : (k + 1) * half, :]
                value = value + arrived[rows_out:, k * cols_in : (k + 1) * cols_in].astype(F32)
                value = (value * scale).astype(BF16).reshape(4, 2, share_in // 2, cols_in)
                for m in range(2):
                    start = m * 2 * cols_in + i * cols_in
                    pieces[4 * k : 4 * k + 4, share_out:, start : start + cols_in] = value[:, m]

    return call(
        body,
        pos,
        [*near_out, *near_in, *far],
        [((8, share_out + share_in // 2, 2 * cols_out), BF16)],
    )[0]


def shares(pos, pieces, share_out):
    rows, cols = pieces.shape[1:]
    rows_in = rows - share_out
    cols_in = cols // 2

    def body(pos_ref, got, outer, inner):
        for c in range(2):
            value = sum(got[2 * z + c].astype(F32) for z in range(4))
            outer[:, c * cols : (c + 1) * cols] = value[:share_out]
            at = slice(c * cols_in, (c + 1) * cols_in)
            inner[:rows_in, at] = value[share_out:, :cols_in]
            inner[rows_in:, at] = value[share_out:, cols_in:]

    outer, inner = call(
        body, pos, [pieces], [((share_out, 2 * cols), F32), ((2 * rows_in, cols), F32)]
    )
    return outer[None], inner[None]


def slot_grads_of(pos, grad_pre, weight_in, gate_grad):
    slots, hidden = grad_pre.shape
    width = weight_in.shape[0]
    step = width // 4

    def body(pos_ref, grad, weight, gate, out):
        for i in range(4):
            at = slice(i * step, (i + 1) * step)
            out[:, at] = lax.dot_general(
                grad[...], weight[at, :], (((1,), (1,)), ((), ())), preferred_element_type=F32
            ).astype(BF16)
        lane = lax.broadcasted_iota(jnp.int32, (slots, EXTRA), 1)
        out[:, width:] = jnp.where(lane == pos_ref[2], gate[...], 0.0).astype(BF16)

    return call(
        body, pos, [grad_pre, weight_in, gate_grad], [((slots, width + EXTRA), BF16)]
    )[0]


def token_grads(pos, dispatch, back, tokens, weight_lanes, probs, combine, keep, denominator, scale):
    rows, width = tokens.shape
    experts = 8
    step = width // 4

    def body(pos_ref, disp, flat, tok, weight, p_ref, c_ref, k_ref, d_ref, out, router):
        dims = (((0,), (0,)), ((), ()))
        combine_grad = lax.dot_general(
            disp[...], flat[:, width:], dims, preferred_element_type=F32
        )
        weighted = jnp.sum(combine_grad * c_ref[...], axis=1, keepdims=True)
        probs_grad = k_ref[...] * (combine_grad - weighted) / d_ref[...]
        probs = p_ref[...]
        inner = jnp.sum(probs_grad * probs, axis=1, keepdims=True)
        logit_b = (probs * (probs_grad - inner)).astype(BF16)
        for i in range(4):
            at = slice(i * step, (i + 1) * step)
            part = lax.dot_general(logit_b, tok[:, at], dims, preferred_element_type=F32)
            router[:, at] = part[:experts] * scale
            value = lax.dot_general(disp[...], flat[:, at], dims, preferred_element_type=F32)
            value = value + lax.dot_general(
                logit_b, weight[at, :], (((1,), (1,)), ((), ())), preferred_element_type=F32
            )
            out[:, at] = value.astype(BF16)

    return call(
        body,
        pos,
        [dispatch, back, tokens, weight_lanes, probs, combine, keep, denominator],
        [((rows, width), BF16), ((experts, width), F32)],
    )


def per_device(
    tokens, grad_out, router_weight, weight_in, weight_out, expert_ids, slot_index, keep_mask
):
    tok_rows, model_width = tokens.shape
    experts = 8
    weight_in = weight_in[0]
    weight_out = weight_out[0]
    capacity = tok_rows * expert_ids.shape[1] // experts
    slot_count = experts * capacity
    grad_scale = float(tok_rows * 256) ** (-0.5)
    core = lax.axis_index("core")
    my_y = lax.axis_index("y")

    target = expert_ids * capacity + slot_index
    slot_iota = jnp.arange(slot_count, dtype=jnp.int32)[:, None]
    first_hit = (slot_iota == target[None, :, 0]) & (keep_mask[None, :, 0] == 1)
    second_hit = (slot_iota == target[None, :, 1]) & (keep_mask[None, :, 1] == 1)
    dispatch = (first_hit | second_hit).astype(BF16)

    send_tokens = jnp.dot(dispatch, tokens, preferred_element_type=F32).astype(BF16)
    slot_tokens = exchange(
        send_tokens.reshape(experts, capacity, model_width), GROUP
    ).reshape(slot_count, model_width)

    logits = jnp.dot(tokens, router_weight, preferred_element_type=F32)
    exp_logits = jnp.exp(logits)
    router_probs = exp_logits / jnp.sum(exp_logits, axis=1, keepdims=True)
    picked = expert_ids[:, :, None] == jnp.arange(experts, dtype=jnp.int32)[None, None, :]
    chosen = jnp.sum(jnp.where(picked, router_probs[:, None, :], 0.0), axis=2)
    keep_float = keep_mask.astype(F32)
    denominator = jnp.sum(keep_float * chosen, axis=1) + (1.0 - jnp.max(keep_float, axis=1))
    combine = keep_float * chosen / denominator[:, None]
    def lanes(values, fill=0.0):
        return jnp.pad(values, ((0, 0), (0, EXTRA - experts)), constant_values=fill)

    probs_lanes = lanes(router_probs)
    combine_lanes = lanes(jnp.sum(jnp.where(picked, combine[:, :, None], 0.0), axis=1))
    keep_lanes = lanes(jnp.sum(jnp.where(picked, keep_float[:, :, None], 0.0), axis=1))
    denominator_lanes = jnp.broadcast_to(denominator[:, None], (tok_rows, EXTRA))
    weight_lanes = lanes(router_weight)
    gate_lanes = combine_lanes.astype(BF16)
    send_grads = jnp.dot(dispatch, grad_out, preferred_element_type=F32).astype(BF16)
    send_gates = jnp.dot(dispatch, gate_lanes, preferred_element_type=F32).astype(BF16)
    received = exchange(
        jnp.concatenate([send_grads, send_gates], axis=1).reshape(
            experts, capacity, model_width + EXTRA
        ),
        GROUP,
    ).reshape(slot_count, model_width + EXTRA)
    other_tokens = swap(slot_tokens, "core", 1)
    hidden_pre = jnp.dot(slot_tokens, weight_in, preferred_element_type=F32)
    normal_cdf, normal_pdf = gelu_parts(hidden_pre)
    hidden_act = (hidden_pre * normal_cdf).astype(BF16)
    act_slope = normal_cdf + hidden_pre * normal_pdf
    other_act = swap(hidden_act, "core", 1)
    left_in = (slot_tokens, other_tokens)
    left_out = (hidden_act, other_act)
    pos = jnp.stack([my_y, core, lax.axis_index(GROUP), lax.axis_index("zh")]).astype(jnp.int32)


    (received, left_in, left_out, act_slope, dispatch, weight_lanes) = tie(
        received, left_in, left_out, act_slope, dispatch, weight_lanes
    )
    probs_lanes, combine_lanes, keep_lanes, denominator_lanes, _ = tie(
        probs_lanes, combine_lanes, keep_lanes, denominator_lanes, act_slope
    )
    my_out, give_out = scale_grads(pos, received)
    right_out = (my_out, swap(give_out, "core", 1))
    received, _ = tie(received, give_out)
    grad_pre, give_in, gate_grad = pre_grads(
        pos, received, weight_out, left_out[0], act_slope
    )
    right_in = (grad_pre, swap(give_in, "core", 1))

    sent = sent_parts(pos, left_out, right_out, left_in, right_in)
    got = (swap(sent[0], "y", 1), swap(sent[1], "y", 3))
    pre_for_slots, _ = tie(grad_pre, sent)
    grad_slots = slot_grads_of(pos, pre_for_slots, weight_in, gate_grad)
    back = exchange(
        grad_slots.reshape(experts, capacity, model_width + EXTRA), GROUP
    ).reshape(slot_count, model_width + EXTRA)

    left_in, left_out, right_in, right_out, _ = tie(
        left_in, left_out, right_in, right_out, grad_slots
    )
    *near, far_a, far_b = kept_parts(pos, left_out, right_out, left_in, right_in, got)
    far = (swap(far_a, "y", 3), swap(far_b, "y", 1))

    back, _ = tie(back, far_a)
    grad_tokens, router_part = token_grads(
        pos,
        dispatch,
        back,
        tokens,
        weight_lanes,
        probs_lanes,
        combine_lanes,
        keep_lanes,
        denominator_lanes,
        grad_scale,
    )

    def router_steps(value, first, last):
        for axis, mask in ROUTER_STEPS[first:last]:
            value = value + swap(value, axis, mask)
        return value

    router_part = router_steps(router_part, 0, 2)
    near, _ = tie(near, router_part)
    pieces = zh_pieces(pos, near[:2], near[2:], far, grad_scale)
    router_part, _ = tie(router_part, pieces)
    got = exchange(pieces, ("zh", "core"))
    router_part = router_steps(router_part, 2, 8)
    got, router_part = tie(got, router_part)
    outer_share, inner_share = shares(pos, got, near[0].shape[0] // 8)
    return (grad_tokens, router_part.T, inner_share, outer_share)


def solution(mesh):
    fine = Mesh(mesh.devices.reshape(FINE_SHAPE), FINE)
    placed = (
        P(FINE, None),
        P(FINE, None),
        P(),
        P(GROUP, None, None),
        P(GROUP, None, None),
        P(FINE, None),
        P(FINE, None),
        P(FINE, None),
    )
    return jax.shard_map(
        per_device,
        mesh=fine,
        in_specs=placed,
        out_specs=(
            P(FINE, None),
            P(),
            P(GROUP, ("y", "zh", "core"), None),
            P(GROUP, ("y", "zh", "core"), None),
        ),
        check_vma=False,
    )
```

```python
import jax
import jax.numpy as jnp
from jax import lax
from jax.experimental import pallas as pl
from jax.experimental.pallas import tpu as pltpu
from jax.sharding import Mesh, PartitionSpec as P

FINE = ("y", "zh", "core", "x", "zl")
FINE_SHAPE = (4, 4, 2, 4, 2)
GROUP = ("x", "zl")
EXTRA = 128
VMEM_LIMIT = 16 * 1024 * 1024
COST_SLOTS = 1000
LONG = 26_000_000_000
F32 = jnp.float32
BF16 = jnp.bfloat16


def gelu_parts(hidden_pre):
    normal_cdf = 0.5 * (1.0 + jax.scipy.special.erf(hidden_pre * 0.7071067811865476))
    normal_pdf = jnp.exp(-0.5 * hidden_pre * hidden_pre) * 0.3989422804014327
    return (normal_cdf, normal_pdf)


def contract_rows(left, right):
    return lax.dot_general(left, right, (((0,), (0,)), ((), ())), preferred_element_type=F32)


def contract_cols(left, right):
    return lax.dot_general(left, right, (((1,), (1,)), ((), ())), preferred_element_type=F32)


def swap(values, axis, mask):
    size = lax.axis_size(axis)
    return lax.ppermute(values, axis, [(i, i ^ mask) for i in range(size)])


def exchange(values, axes):
    return lax.all_to_all(values, axes, split_axis=0, concat_axis=0, tiled=True)


def tie(*values):
    return lax.optimization_barrier(values)


def call(body, pos, inputs, outputs, flops=1000, far=(), scratch=()):
    vmem = pl.BlockSpec(memory_space=pltpu.VMEM)
    return pl.pallas_call(
        body,
        in_specs=[pl.BlockSpec(memory_space=pltpu.SMEM)]
        + [vmem] * len(inputs)
        + [pl.BlockSpec(memory_space=pl.ANY)] * len(far),
        out_specs=[vmem] * len(outputs),
        out_shape=[jax.ShapeDtypeStruct(shape, dtype) for shape, dtype in outputs],
        scratch_shapes=scratch,
        cost_estimate=pl.CostEstimate(flops=flops, bytes_accessed=1000, transcendentals=0),
        compiler_params=pltpu.CompilerParams(vmem_limit_bytes=VMEM_LIMIT),
    )(pos, *inputs, *far)


def gate_of(pos, lanes):
    lane = lax.broadcasted_iota(jnp.int32, lanes.shape, 1)
    return jnp.sum(jnp.where(lane == pos[2], lanes.astype(F32), 0.0), axis=1, keepdims=True)


def scale_grads(pos, received):
    slots, wide = received.shape
    half = (wide - EXTRA) // 2
    rows = slots // 4

    def body(pos_ref, rec, mine, give):
        core = pos_ref[1]
        for r in range(0, slots, rows):
            at = slice(r, r + rows)
            gate = gate_of(pos_ref, rec[at, 2 * half :])
            for out, which in ((mine, core), (give, 1 - core)):
                start = pl.multiple_of(which * half, half)
                out[at, :] = (gate * rec[at, pl.ds(start, half)].astype(F32)).astype(BF16)

    return call(body, pos, [received], [((slots, half), BF16)] * 2)


def pre_grads(pos, received, weight_out, act, slope):
    slots, wide = received.shape
    hidden, width = weight_out.shape
    step = hidden // 4

    def body(pos_ref, rec, weight, act_ref, slope_ref, grad_pre, give, gate_grad, w, a, g, sems):
        copies = []
        for i in range(4):
            at = slice(i * step, (i + 1) * step)
            moves = (
                (weight.at[at, :], w.at[at, :]),
                (act_ref.at[:, at], a.at[i]),
                (slope_ref.at[:, at], g.at[i]),
            )
            copies.append(
                [pltpu.make_async_copy(x, y, sems.at[i, k]) for k, (x, y) in enumerate(moves)]
            )
            for copy in copies[i]:
                copy.start()
        gate = gate_of(pos_ref, rec[:, width:])
        total = None
        for i in range(4):
            at = slice(i * step, (i + 1) * step)
            for copy in copies[i]:
                copy.wait()
            grad_act = lax.dot_general(
                rec[:, :width], w[at, :], (((1,), (1,)), ((), ())), preferred_element_type=F32
            )
            part = jnp.sum(a[i].astype(F32) * grad_act, axis=1, keepdims=True)
            total = part if total is None else total + part
            grad_pre[:, at] = (gate * grad_act * g[i]).astype(BF16)
        start = pl.multiple_of((1 - pos_ref[1]) * (hidden // 2), hidden // 2)
        give[...] = grad_pre[:, pl.ds(start, hidden // 2)]
        lane = lax.broadcasted_iota(jnp.int32, (slots, EXTRA), 1)
        gate_grad[...] = jnp.where(lane == pos_ref[2], total, 0.0).astype(BF16)

    return call(
        body,
        pos,
        [received],
        [((slots, hidden), BF16), ((slots, hidden // 2), BF16), ((slots, EXTRA), BF16)],
        far=[weight_out, act, slope],
        scratch=[
            pltpu.VMEM((hidden, width), BF16),
            pltpu.VMEM((4, slots, step), BF16),
            pltpu.VMEM((4, slots, step), F32),
            pltpu.SemaphoreType.DMA((4, 3)),
        ],
    )


def row_products(pos_ref, refs, own_offset, masks, width, cols):
    lm, lo, rm, ro = refs
    dims = (((0,), (0,)), ((), ()))
    for i in range(2):
        own = pl.multiple_of((own_offset * pos_ref[1] + i) * cols, cols)
        for j in range(2):
            start = pl.multiple_of((pos_ref[0] ^ masks[i][j]) * width, width)
            value = lax.dot_general(
                lm[:, pl.ds(start, width)],
                rm[:, pl.ds(own, cols)],
                dims,
                preferred_element_type=F32,
            )
            value = value + lax.dot_general(
                lo[:, pl.ds(start, width)],
                ro[:, i * cols : (i + 1) * cols],
                dims,
                preferred_element_type=F32,
            )
            yield i, j, value


def sent_parts(pos, left_out, right_out, left_in, right_in):
    slots = left_in[0].shape[0]
    width_out, width_in = left_out[0].shape[1] // 4, left_in[0].shape[1] // 4
    cols_out, cols_in = right_out[1].shape[1] // 2, right_in[1].shape[1] // 2
    masks = ((1, 2), (3, 2))

    def body(pos_ref, *refs):
        out_refs, right_refs = refs[:4], refs[4:6]
        lefts, outs, (buffer, sems) = refs[6:8], refs[8:10], refs[10:]
        copies = []
        for k in range(2):
            for r in (1, 2, 3):
                start = pl.multiple_of((pos_ref[0] ^ r) * width_in, width_in)
                copy = pltpu.make_async_copy(
                    lefts[k].at[:, pl.ds(start, width_in)], buffer.at[k, r - 1], sems.at[k, r - 1]
                )
                copy.start()
                copies.append(copy)
        for i, j, value in row_products(pos_ref, out_refs, 0, masks, width_out, cols_out):
            outs[i][j * width_out : (j + 1) * width_out, :] = value.astype(BF16)
        for copy in copies:
            copy.wait()
        dims = (((0,), (0,)), ((), ()))
        for i in range(2):
            own = pl.multiple_of((2 * pos_ref[1] + i) * cols_in, cols_in)
            for j in range(2):
                r = masks[i][j] - 1
                value = lax.dot_general(
                    buffer[0, r],
                    right_refs[0][:, pl.ds(own, cols_in)],
                    dims,
                    preferred_element_type=F32,
                )
                value = value + lax.dot_general(
                    buffer[1, r],
                    right_refs[1][:, i * cols_in : (i + 1) * cols_in],
                    dims,
                    preferred_element_type=F32,
                )
                outs[i][2 * width_out :, j * cols_in : (j + 1) * cols_in] = value.astype(BF16)

    return call(
        body,
        pos,
        [*left_out, *right_out, *right_in],
        [((2 * width_out + width_in, cols_out), BF16)] * 2,
        far=[*left_in],
        scratch=[pltpu.VMEM((2, 3, slots, width_in), BF16), pltpu.SemaphoreType.DMA((2, 3))],
    )


def kept_parts(pos, left_out, right_out, left_in, right_in):
    width_out, width_in = left_out[0].shape[1] // 4, left_in[0].shape[1] // 4
    cols_out, cols_in = right_out[1].shape[1] // 2, right_in[1].shape[1] // 2
    masks = ((0, 3), (0, 1))
    half = width_in // 2

    def body(pos_ref, *refs):
        near_out, near_in, far = refs[8:10], refs[10:12], refs[12:14]
        for i, j, value in row_products(pos_ref, refs[:4], 0, masks, width_out, cols_out):
            if j == 0:
                near_out[i][...] = value
            else:
                far[i][:width_out, :] = value
        for i, j, value in row_products(pos_ref, refs[4:8], 2, masks, width_in, cols_in):
            if j == 0:
                near_in[i][...] = value
            else:
                far[i][width_out:, :cols_in] = value[:half, :]
                far[i][width_out:, cols_in:] = value[half:, :]

    return call(
        body,
        pos,
        [*left_out, *right_out, *left_in, *right_in],
        [((width_out, cols_out), F32)] * 2
        + [((width_in, cols_in), F32)] * 2
        + [((width_out + half, cols_out), F32)] * 2,
    )


def far_sums(pos, far, got):
    rows, cols = far[0].shape
    half, wide = rows // 2, cols // 2

    def body(pos_ref, far_a, far_b, got_a, got_b, out_a, out_b):
        for mine, arrived, out in ((far_a, got_a, out_a), (far_b, got_b, out_b)):
            out[:half, :] = (mine[:half, :] + arrived[half:rows, :].astype(F32)).astype(BF16)
            for k in range(2):
                at = slice(k * wide, (k + 1) * wide)
                value = arrived[rows + k * half : rows + (k + 1) * half, wide:].astype(F32)
                out[half:, at] = (mine[half:, at] + value).astype(BF16)

    return call(body, pos, [*far, *got], [((rows, cols), BF16)] * 2, LONG)


def zh_pieces(pos, near_out, near_in, got, far, scale):
    rows_out, cols_out = near_out[0].shape
    rows_in, cols_in = near_in[0].shape
    half = rows_in // 2
    share_out, share_in = rows_out // 8, rows_in // 8

    def body(pos_ref, out_a, out_b, in_a, in_b, got_a, got_b, far_a, far_b, pieces):
        sets = ((out_a, in_a, got_a, far_a), (out_b, in_b, got_b, far_b))
        for i, (out, inner, first, second) in enumerate(sets):
            value = out[...] + first[:rows_out, :].astype(F32) + second[:rows_out, :].astype(F32)
            value = (value * scale).astype(BF16).reshape(8, share_out, cols_out)
            pieces[:, :share_out, i * cols_out : (i + 1) * cols_out] = value
            for k in range(2):
                at = slice(2 * rows_out + k * half, 2 * rows_out + (k + 1) * half)
                value = inner[k * half : (k + 1) * half, :] + first[at, :cols_in].astype(F32)
                value = value + second[rows_out:, k * cols_in : (k + 1) * cols_in].astype(F32)
                value = (value * scale).astype(BF16).reshape(4, 2, share_in // 2, cols_in)
                for m in range(2):
                    start = m * 2 * cols_in + i * cols_in
                    pieces[4 * k : 4 * k + 4, share_out:, start : start + cols_in] = value[:, m]

    return call(
        body,
        pos,
        [*near_out, *near_in, *got, *far],
        [((8, share_out + share_in // 2, 2 * cols_out), BF16)],
    )[0]


def shares(pos, pieces, share_out):
    rows, cols = pieces.shape[1:]
    rows_in = rows - share_out
    cols_in = cols // 2

    def body(pos_ref, got, outer, inner):
        for c in range(2):
            value = sum(got[2 * z + c].astype(F32) for z in range(4))
            outer[:, c * cols : (c + 1) * cols] = value[:share_out]
            at = slice(c * cols_in, (c + 1) * cols_in)
            inner[:rows_in, at] = value[share_out:, :cols_in]
            inner[rows_in:, at] = value[share_out:, cols_in:]

    outer, inner = call(
        body, pos, [pieces], [((share_out, 2 * cols), F32), ((2 * rows_in, cols), F32)]
    )
    return outer[None], inner[None]


def slot_grads_of(pos, grad_pre, weight_in):
    slots, hidden = grad_pre.shape
    width = weight_in.shape[0]
    step = width // 4

    def body(pos_ref, grad, weight, out):
        for i in range(4):
            at = slice(i * step, (i + 1) * step)
            out[:, at] = lax.dot_general(
                grad[...], weight[at, :], (((1,), (1,)), ((), ())), preferred_element_type=F32
            ).astype(BF16)

    return call(body, pos, [grad_pre, weight_in], [((slots, width), BF16)], COST_SLOTS)[0]


def router_grads(pos, dispatch, gate_back, tokens, probs, combine, keep, denominator, scale):
    rows, width = tokens.shape
    experts = 8
    step = width // 4

    def body(pos_ref, disp, back, tok, p_ref, c_ref, k_ref, d_ref, logit, router):
        dims = (((0,), (0,)), ((), ()))
        combine_grad = lax.dot_general(disp[...], back[...], dims, preferred_element_type=F32)
        weighted = jnp.sum(combine_grad * c_ref[...], axis=1, keepdims=True)
        probs_grad = k_ref[...] * (combine_grad - weighted) / d_ref[...]
        probs = p_ref[...]
        inner = jnp.sum(probs_grad * probs, axis=1, keepdims=True)
        logit_b = (probs * (probs_grad - inner)).astype(BF16)
        logit[...] = logit_b
        for i in range(4):
            at = slice(i * step, (i + 1) * step)
            part = lax.dot_general(logit_b, tok[:, at], dims, preferred_element_type=F32)
            router[:, at] = part[:experts] * scale

    return call(
        body,
        pos,
        [dispatch, gate_back, tokens, probs, combine, keep, denominator],
        [((rows, EXTRA), BF16), ((experts, width), F32)],
    )


def token_grads(pos, dispatch, back, logit_lanes, weight_lanes):
    rows, width = dispatch.shape[1], back.shape[1]
    step = width // 4

    def body(pos_ref, disp, flat, logit, weight, out):
        for i in range(4):
            at = slice(i * step, (i + 1) * step)
            value = lax.dot_general(
                disp[...], flat[:, at], (((0,), (0,)), ((), ())), preferred_element_type=F32
            )
            value = value + lax.dot_general(
                logit[...], weight[at, :], (((1,), (1,)), ((), ())), preferred_element_type=F32
            )
            out[:, at] = value.astype(BF16)

    return call(
        body, pos, [dispatch, back, logit_lanes, weight_lanes], [((rows, width), BF16)]
    )[0]


def per_device(
    tokens, grad_out, router_weight, weight_in, weight_out, expert_ids, slot_index, keep_mask
):
    tok_rows, model_width = tokens.shape
    experts = 8
    weight_in = weight_in[0]
    weight_out = weight_out[0]
    capacity = tok_rows * expert_ids.shape[1] // experts
    slot_count = experts * capacity
    grad_scale = float(tok_rows * 256) ** (-0.5)
    core = lax.axis_index("core")
    my_y = lax.axis_index("y")

    target = expert_ids * capacity + slot_index
    slot_iota = jnp.arange(slot_count, dtype=jnp.int32)[:, None]
    first_hit = (slot_iota == target[None, :, 0]) & (keep_mask[None, :, 0] == 1)
    second_hit = (slot_iota == target[None, :, 1]) & (keep_mask[None, :, 1] == 1)
    dispatch = (first_hit | second_hit).astype(BF16)

    send_tokens = jnp.dot(dispatch, tokens, preferred_element_type=F32).astype(BF16)
    slot_tokens = exchange(
        send_tokens.reshape(experts, capacity, model_width), GROUP
    ).reshape(slot_count, model_width)

    logits = jnp.dot(tokens, router_weight, preferred_element_type=F32)
    exp_logits = jnp.exp(logits)
    router_probs = exp_logits / jnp.sum(exp_logits, axis=1, keepdims=True)
    picked = expert_ids[:, :, None] == jnp.arange(experts, dtype=jnp.int32)[None, None, :]
    chosen = jnp.sum(jnp.where(picked, router_probs[:, None, :], 0.0), axis=2)
    keep_float = keep_mask.astype(F32)
    denominator = jnp.sum(keep_float * chosen, axis=1) + (1.0 - jnp.max(keep_float, axis=1))
    combine = keep_float * chosen / denominator[:, None]
    def lanes(values, fill=0.0):
        return jnp.pad(values, ((0, 0), (0, EXTRA - experts)), constant_values=fill)

    probs_lanes = lanes(router_probs)
    combine_lanes = lanes(jnp.sum(jnp.where(picked, combine[:, :, None], 0.0), axis=1))
    keep_lanes = lanes(jnp.sum(jnp.where(picked, keep_float[:, :, None], 0.0), axis=1))
    denominator_lanes = jnp.broadcast_to(denominator[:, None], (tok_rows, EXTRA))
    weight_lanes = lanes(router_weight)
    gate_lanes = combine_lanes.astype(BF16)
    send_grads = jnp.dot(dispatch, grad_out, preferred_element_type=F32).astype(BF16)
    send_gates = jnp.dot(dispatch, gate_lanes, preferred_element_type=F32).astype(BF16)
    received = exchange(
        jnp.concatenate([send_grads, send_gates], axis=1).reshape(
            experts, capacity, model_width + EXTRA
        ),
        GROUP,
    ).reshape(slot_count, model_width + EXTRA)
    other_tokens = swap(slot_tokens, "core", 1)
    hidden_pre = jnp.dot(slot_tokens, weight_in, preferred_element_type=F32)
    normal_cdf, normal_pdf = gelu_parts(hidden_pre)
    hidden_act = (hidden_pre * normal_cdf).astype(BF16)
    act_slope = normal_cdf + hidden_pre * normal_pdf
    other_act = swap(hidden_act, "core", 1)
    left_in = (slot_tokens, other_tokens)
    left_out = (hidden_act, other_act)
    pos = jnp.stack([my_y, core, lax.axis_index(GROUP), lax.axis_index("zh")]).astype(jnp.int32)


    token_side = (dispatch, weight_lanes, probs_lanes, combine_lanes, keep_lanes, denominator_lanes)
    received, left_in, left_out, act_slope, token_side = tie(
        received, left_in, left_out, act_slope, token_side
    )
    dispatch, weight_lanes, probs_lanes, combine_lanes, keep_lanes, denominator_lanes = token_side
    my_out, give_out = scale_grads(pos, received)
    right_out = (my_out, swap(give_out, "core", 1))
    received, _ = tie(received, give_out)
    grad_pre, give_in, gate_grad = pre_grads(
        pos, received, weight_out, left_out[0], act_slope
    )
    right_in = (grad_pre, swap(give_in, "core", 1))

    sent = sent_parts(pos, left_out, right_out, left_in, right_in)
    got = (swap(sent[0], "y", 1), swap(sent[1], "y", 3))
    gate_grad, grad_pre, _ = tie(gate_grad, grad_pre, sent)
    gate_back = exchange(gate_grad.reshape(experts, capacity, EXTRA), GROUP).reshape(
        slot_count, EXTRA
    )
    grad_slots = slot_grads_of(pos, grad_pre, weight_in)
    grad_slots, gate_back = tie(grad_slots, gate_back)
    back = exchange(
        grad_slots.reshape(experts, capacity, model_width), GROUP
    ).reshape(slot_count, model_width)

    gate_back, _ = tie(gate_back, grad_slots)
    logit_lanes, router_part = router_grads(
        pos,
        dispatch,
        gate_back,
        tokens,
        probs_lanes,
        combine_lanes,
        keep_lanes,
        denominator_lanes,
        grad_scale,
    )

    def router_round(value, axes, one, two):
        near, far, both = (swap(value, axes, mask) for mask in (one, two, one ^ two))
        return (value + near) + (far + both)

    left_in, left_out, right_in, right_out, _ = tie(
        left_in, left_out, right_in, right_out, router_part
    )
    *near, far_a, far_b = kept_parts(pos, left_out, right_out, left_in, right_in)
    router_part, _ = tie(router_part, far_a)
    router_part = router_round(router_part, ("core", "zl"), 1, 2)
    got, far_a, far_b, router_part = tie(got, far_a, far_b, router_part)
    far_a, far_b = far_sums(pos, (far_a, far_b), got)
    far = (swap(far_a, "y", 3), swap(far_b, "y", 1))

    router_part, _ = tie(router_part, far_a)
    router_part = router_round(router_part, "zh", 1, 3)
    near, far, router_part = tie(near, far, router_part)
    pieces = zh_pieces(pos, near[:2], near[2:], got, far, grad_scale)
    got = exchange(pieces, ("zh", "core"))

    back, router_part, _ = tie(back, router_part, pieces)
    grad_tokens = token_grads(pos, dispatch, back, logit_lanes, weight_lanes)
    router_part, _ = tie(router_part, grad_tokens)
    router_part = router_round(router_part, "x", 1, 3)
    router_part = router_round(router_part, "y", 1, 3)
    got, router_part = tie(got, router_part)
    outer_share, inner_share = shares(pos, got, near[0].shape[0] // 8)
    return (grad_tokens, router_part.T, inner_share, outer_share)


def solution(mesh):
    fine = Mesh(mesh.devices.reshape(FINE_SHAPE), FINE)
    placed = (
        P(FINE, None),
        P(FINE, None),
        P(),
        P(GROUP, None, None),
        P(GROUP, None, None),
        P(FINE, None),
        P(FINE, None),
        P(FINE, None),
    )
    return jax.shard_map(
        per_device,
        mesh=fine,
        in_specs=placed,
        out_specs=(
            P(FINE, None),
            P(),
            P(GROUP, ("y", "zh", "core"), None),
            P(GROUP, ("y", "zh", "core"), None),
        ),
        check_vma=False,
    )
```

```python
import jax
import jax.numpy as jnp
from jax import lax
from jax.experimental import pallas as pl
from jax.experimental.pallas import tpu as pltpu
from jax.sharding import Mesh, PartitionSpec as P

FINE = ("y", "zh", "core", "x", "zl")
FINE_SHAPE = (4, 4, 2, 4, 2)
GROUP = ("x", "zl")
EXTRA = 128
VMEM_LIMIT = 16 * 1024 * 1024
LONG = 50_000_000_000
F32 = jnp.float32
BF16 = jnp.bfloat16


def gelu_parts(hidden_pre):
    normal_cdf = 0.5 * (1.0 + jax.scipy.special.erf(hidden_pre * 0.7071067811865476))
    normal_pdf = jnp.exp(-0.5 * hidden_pre * hidden_pre) * 0.3989422804014327
    return (normal_cdf, normal_pdf)


def contract_rows(left, right):
    return lax.dot_general(left, right, (((0,), (0,)), ((), ())), preferred_element_type=F32)


def contract_cols(left, right):
    return lax.dot_general(left, right, (((1,), (1,)), ((), ())), preferred_element_type=F32)


def swap(values, axis, mask):
    size = lax.axis_size(axis)
    return lax.ppermute(values, axis, [(i, i ^ mask) for i in range(size)])


def exchange(values, axes):
    return lax.all_to_all(values, axes, split_axis=0, concat_axis=0, tiled=True)


def tie(*values):
    return lax.optimization_barrier(values)


def call(body, pos, inputs, outputs, flops=1000, far=(), scratch=()):
    vmem = pl.BlockSpec(memory_space=pltpu.VMEM)
    return pl.pallas_call(
        body,
        in_specs=[pl.BlockSpec(memory_space=pltpu.SMEM)]
        + [vmem] * len(inputs)
        + [pl.BlockSpec(memory_space=pltpu.HBM)] * len(far),
        out_specs=[vmem] * len(outputs),
        out_shape=[jax.ShapeDtypeStruct(shape, dtype) for shape, dtype in outputs],
        scratch_shapes=scratch,
        cost_estimate=pl.CostEstimate(flops=flops, bytes_accessed=1000, transcendentals=0),
        compiler_params=pltpu.CompilerParams(vmem_limit_bytes=VMEM_LIMIT),
    )(pos, *inputs, *far)


def gate_of(pos, lanes):
    lane = lax.broadcasted_iota(jnp.int32, lanes.shape, 1)
    return jnp.sum(jnp.where(lane == pos[2], lanes.astype(F32), 0.0), axis=1, keepdims=True)


def scale_grads(pos, received):
    slots, wide = received.shape
    half = (wide - EXTRA) // 2
    rows = slots // 4

    def body(pos_ref, rec, mine, give):
        core = pos_ref[1]
        for r in range(0, slots, rows):
            at = slice(r, r + rows)
            gate = gate_of(pos_ref, rec[at, 2 * half :])
            for out, which in ((mine, core), (give, 1 - core)):
                start = pl.multiple_of(which * half, half)
                out[at, :] = (gate * rec[at, pl.ds(start, half)].astype(F32)).astype(BF16)

    return call(body, pos, [received], [((slots, half), BF16)] * 2)


def pre_grads(pos, received, weight_out, act, slope):
    slots, wide = received.shape
    hidden, width = weight_out.shape
    step = hidden // 4

    def body(pos_ref, rec, weight, act_ref, slope_ref, grad_pre, give, gate_grad, w, a, g, sems):
        copies = []
        for i in range(4):
            at = slice(i * step, (i + 1) * step)
            moves = (
                (weight.at[at, :], w.at[at, :]),
                (act_ref.at[:, at], a.at[i]),
                (slope_ref.at[:, at], g.at[i]),
            )
            copies.append(
                [pltpu.make_async_copy(x, y, sems.at[i, k]) for k, (x, y) in enumerate(moves)]
            )
            for copy in copies[i]:
                copy.start()
        gate = gate_of(pos_ref, rec[:, width:])
        total = None
        for i in range(4):
            at = slice(i * step, (i + 1) * step)
            for copy in copies[i]:
                copy.wait()
            grad_act = lax.dot_general(
                rec[:, :width], w[at, :], (((1,), (1,)), ((), ())), preferred_element_type=F32
            )
            part = jnp.sum(a[i].astype(F32) * grad_act, axis=1, keepdims=True)
            total = part if total is None else total + part
            grad_pre[:, at] = (gate * grad_act * g[i]).astype(BF16)
        start = pl.multiple_of((1 - pos_ref[1]) * (hidden // 2), hidden // 2)
        give[...] = grad_pre[:, pl.ds(start, hidden // 2)]
        lane = lax.broadcasted_iota(jnp.int32, (slots, EXTRA), 1)
        gate_grad[...] = jnp.where(lane == pos_ref[2], total, 0.0).astype(BF16)

    return call(
        body,
        pos,
        [received],
        [((slots, hidden), BF16), ((slots, hidden // 2), BF16), ((slots, EXTRA), BF16)],
        far=[weight_out, act, slope],
        scratch=[
            pltpu.VMEM((hidden, width), BF16),
            pltpu.VMEM((4, slots, step), BF16),
            pltpu.VMEM((4, slots, step), F32),
            pltpu.SemaphoreType.DMA((4, 3)),
        ],
    )


def row_products(pos_ref, refs, own_offset, masks, width, cols):
    lm, lo, rm, ro = refs
    dims = (((0,), (0,)), ((), ()))
    for i in range(2):
        own = pl.multiple_of((own_offset * pos_ref[1] + i) * cols, cols)
        for j in range(2):
            start = pl.multiple_of((pos_ref[0] ^ masks[i][j]) * width, width)
            value = lax.dot_general(
                lm[:, pl.ds(start, width)],
                rm[:, pl.ds(own, cols)],
                dims,
                preferred_element_type=F32,
            )
            value = value + lax.dot_general(
                lo[:, pl.ds(start, width)],
                ro[:, i * cols : (i + 1) * cols],
                dims,
                preferred_element_type=F32,
            )
            yield i, j, value


def sent_parts(pos, left_out, right_out, left_in, right_in):
    slots = left_in[0].shape[0]
    width_out, width_in = left_out[0].shape[1] // 4, left_in[0].shape[1] // 4
    cols_out, cols_in = right_out[1].shape[1] // 2, right_in[1].shape[1] // 2
    masks = ((1, 2), (3, 2))

    def body(pos_ref, *refs):
        rights, lefts, outs = refs[:4], refs[4:8], refs[8:10]
        buffer_out, buffer_in, sems = refs[10:]
        copies = []
        for k in range(4):
            buffer, width = (buffer_out, width_out) if k < 2 else (buffer_in, width_in)
            for r in (1, 2, 3):
                start = pl.multiple_of((pos_ref[0] ^ r) * width, width)
                copy = pltpu.make_async_copy(
                    lefts[k].at[:, pl.ds(start, width)],
                    buffer.at[k % 2, r - 1],
                    sems.at[k, r - 1],
                )
                copy.start()
                copies.append(copy)
        dims = (((0,), (0,)), ((), ()))
        for part in range(2):
            buffer, cols = (buffer_in, cols_in) if part else (buffer_out, cols_out)
            mine, other = rights[2 * part : 2 * part + 2]
            for copy in copies[6 * part : 6 * part + 6]:
                copy.wait()
            for i in range(2):
                own = i * cols
                if part:
                    own = pl.multiple_of((2 * pos_ref[1] + i) * cols, cols)
                for j in range(2):
                    r = masks[i][j] - 1
                    value = lax.dot_general(
                        buffer[0, r], mine[:, pl.ds(own, cols)], dims, preferred_element_type=F32
                    )
                    value = value + lax.dot_general(
                        buffer[1, r],
                        other[:, i * cols : (i + 1) * cols],
                        dims,
                        preferred_element_type=F32,
                    )
                    value = value.astype(BF16)
                    if part:
                        outs[i][2 * width_out :, j * cols : (j + 1) * cols] = value
                    else:
                        outs[i][j * width_out : (j + 1) * width_out, :] = value

    return call(
        body,
        pos,
        [*right_out, *right_in],
        [((2 * width_out + width_in, cols_out), BF16)] * 2,
        far=[*left_out, *left_in],
        scratch=[
            pltpu.VMEM((2, 3, slots, width_out), BF16),
            pltpu.VMEM((2, 3, slots, width_in), BF16),
            pltpu.SemaphoreType.DMA((4, 3)),
        ],
    )


def kept_parts(pos, left_out, right_out, left_in, right_in):
    width_out, width_in = left_out[0].shape[1] // 4, left_in[0].shape[1] // 4
    cols_out, cols_in = right_out[1].shape[1] // 2, right_in[1].shape[1] // 2
    masks = ((0, 3), (0, 1))
    half = width_in // 2

    def body(pos_ref, *refs):
        near_out, near_in, far = refs[8:10], refs[10:12], refs[12:14]
        for i, j, value in row_products(pos_ref, refs[:4], 0, masks, width_out, cols_out):
            if j == 0:
                near_out[i][...] = value
            else:
                far[i][:width_out, :] = value
        for i, j, value in row_products(pos_ref, refs[4:8], 2, masks, width_in, cols_in):
            if j == 0:
                near_in[i][...] = value
            else:
                far[i][width_out:, :cols_in] = value[:half, :]
                far[i][width_out:, cols_in:] = value[half:, :]

    return call(
        body,
        pos,
        [*left_out, *right_out, *left_in, *right_in],
        [((width_out, cols_out), F32)] * 2
        + [((width_in, cols_in), F32)] * 2
        + [((width_out + half, cols_out), F32)] * 2,
    )


def far_sums(pos, far, got):
    rows, cols = far[0].shape
    half, wide = rows // 2, cols // 2

    def body(pos_ref, far_a, far_b, got_a, got_b, out_a, out_b):
        for mine, arrived, out in ((far_a, got_a, out_a), (far_b, got_b, out_b)):
            out[:half, :] = (mine[:half, :] + arrived[half:rows, :].astype(F32)).astype(BF16)
            for k in range(2):
                at = slice(k * wide, (k + 1) * wide)
                value = arrived[rows + k * half : rows + (k + 1) * half, wide:].astype(F32)
                out[half:, at] = (mine[half:, at] + value).astype(BF16)

    return call(body, pos, [*far, *got], [((rows, cols), BF16)] * 2, LONG)


def zh_pieces(pos, near_out, near_in, got, far, scale):
    rows_out, cols_out = near_out[0].shape
    rows_in, cols_in = near_in[0].shape
    half = rows_in // 2
    share_out, share_in = rows_out // 8, rows_in // 8

    def body(pos_ref, out_a, out_b, in_a, in_b, got_a, got_b, far_a, far_b, pieces):
        sets = ((out_a, in_a, got_a, far_a), (out_b, in_b, got_b, far_b))
        for i, (out, inner, first, second) in enumerate(sets):
            value = out[...] + first[:rows_out, :].astype(F32) + second[:rows_out, :].astype(F32)
            value = (value * scale).astype(BF16).reshape(8, share_out, cols_out)
            pieces[:, :share_out, i * cols_out : (i + 1) * cols_out] = value
            for k in range(2):
                at = slice(2 * rows_out + k * half, 2 * rows_out + (k + 1) * half)
                value = inner[k * half : (k + 1) * half, :] + first[at, :cols_in].astype(F32)
                value = value + second[rows_out:, k * cols_in : (k + 1) * cols_in].astype(F32)
                value = (value * scale).astype(BF16).reshape(4, 2, share_in // 2, cols_in)
                for m in range(2):
                    start = m * 2 * cols_in + i * cols_in
                    pieces[4 * k : 4 * k + 4, share_out:, start : start + cols_in] = value[:, m]

    return call(
        body,
        pos,
        [*near_out, *near_in, *got, *far],
        [((8, share_out + share_in // 2, 2 * cols_out), BF16)],
    )[0]


def shares(pos, pieces, share_out):
    rows, cols = pieces.shape[1:]
    rows_in = rows - share_out
    cols_in = cols // 2

    def body(pos_ref, got, outer, inner):
        for c in range(2):
            value = sum(got[2 * z + c].astype(F32) for z in range(4))
            outer[:, c * cols : (c + 1) * cols] = value[:share_out]
            at = slice(c * cols_in, (c + 1) * cols_in)
            inner[:rows_in, at] = value[share_out:, :cols_in]
            inner[rows_in:, at] = value[share_out:, cols_in:]

    outer, inner = call(
        body, pos, [pieces], [((share_out, 2 * cols), F32), ((2 * rows_in, cols), F32)]
    )
    return outer[None], inner[None]


def slot_grads_of(pos, grad_pre, weight_in, gate_grad):
    slots, hidden = grad_pre.shape
    width = weight_in.shape[0]
    step = width // 4

    def body(pos_ref, grad, weight, gate, out):
        for i in range(4):
            at = slice(i * step, (i + 1) * step)
            out[:, at] = lax.dot_general(
                grad[...], weight[at, :], (((1,), (1,)), ((), ())), preferred_element_type=F32
            ).astype(BF16)
        out[:, width:] = gate[...]

    return call(
        body, pos, [grad_pre, weight_in, gate_grad], [((slots, width + EXTRA), BF16)]
    )[0]


def router_grads(pos, dispatch, back, tokens, probs, combine, keep, denominator, scale):
    rows, width = tokens.shape
    experts = 8
    step = width // 4

    def body(pos_ref, disp, flat, tok, p_ref, c_ref, k_ref, d_ref, logit, router):
        dims = (((0,), (0,)), ((), ()))
        combine_grad = lax.dot_general(
            disp[...], flat[:, width:], dims, preferred_element_type=F32
        )
        weighted = jnp.sum(combine_grad * c_ref[...], axis=1, keepdims=True)
        probs_grad = k_ref[...] * (combine_grad - weighted) / d_ref[...]
        probs = p_ref[...]
        inner = jnp.sum(probs_grad * probs, axis=1, keepdims=True)
        logit_b = (probs * (probs_grad - inner)).astype(BF16)
        logit[...] = logit_b
        for i in range(4):
            at = slice(i * step, (i + 1) * step)
            part = lax.dot_general(logit_b, tok[:, at], dims, preferred_element_type=F32)
            router[:, at] = part[:experts] * scale

    return call(
        body,
        pos,
        [dispatch, back, tokens, probs, combine, keep, denominator],
        [((rows, EXTRA), BF16), ((experts, width), F32)],
    )


def token_grads(pos, dispatch, back, logit_lanes, weight_lanes):
    rows, width = dispatch.shape[1], back.shape[1] - EXTRA
    step = width // 4

    def body(pos_ref, disp, flat, logit, weight, out):
        for i in range(4):
            at = slice(i * step, (i + 1) * step)
            value = lax.dot_general(
                disp[...], flat[:, at], (((0,), (0,)), ((), ())), preferred_element_type=F32
            )
            value = value + lax.dot_general(
                logit[...], weight[at, :], (((1,), (1,)), ((), ())), preferred_element_type=F32
            )
            out[:, at] = value.astype(BF16)

    return call(
        body, pos, [dispatch, back, logit_lanes, weight_lanes], [((rows, width), BF16)]
    )[0]


def per_device(
    tokens, grad_out, router_weight, weight_in, weight_out, expert_ids, slot_index, keep_mask
):
    tok_rows, model_width = tokens.shape
    experts = 8
    weight_in = weight_in[0]
    weight_out = weight_out[0]
    capacity = tok_rows * expert_ids.shape[1] // experts
    slot_count = experts * capacity
    grad_scale = float(tok_rows * 256) ** (-0.5)
    core = lax.axis_index("core")
    my_y = lax.axis_index("y")

    target = expert_ids * capacity + slot_index
    slot_iota = jnp.arange(slot_count, dtype=jnp.int32)[:, None]
    first_hit = (slot_iota == target[None, :, 0]) & (keep_mask[None, :, 0] == 1)
    second_hit = (slot_iota == target[None, :, 1]) & (keep_mask[None, :, 1] == 1)
    dispatch = (first_hit | second_hit).astype(BF16)

    send_tokens = jnp.dot(dispatch, tokens, preferred_element_type=F32).astype(BF16)
    slot_tokens = exchange(
        send_tokens.reshape(experts, capacity, model_width), GROUP
    ).reshape(slot_count, model_width)

    logits = jnp.dot(tokens, router_weight, preferred_element_type=F32)
    exp_logits = jnp.exp(logits)
    router_probs = exp_logits / jnp.sum(exp_logits, axis=1, keepdims=True)
    picked = expert_ids[:, :, None] == jnp.arange(experts, dtype=jnp.int32)[None, None, :]
    chosen = jnp.sum(jnp.where(picked, router_probs[:, None, :], 0.0), axis=2)
    keep_float = keep_mask.astype(F32)
    denominator = jnp.sum(keep_float * chosen, axis=1) + (1.0 - jnp.max(keep_float, axis=1))
    combine = keep_float * chosen / denominator[:, None]
    def lanes(values, fill=0.0):
        return jnp.pad(values, ((0, 0), (0, EXTRA - experts)), constant_values=fill)

    probs_lanes = lanes(router_probs)
    combine_lanes = lanes(jnp.sum(jnp.where(picked, combine[:, :, None], 0.0), axis=1))
    keep_lanes = lanes(jnp.sum(jnp.where(picked, keep_float[:, :, None], 0.0), axis=1))
    denominator_lanes = jnp.broadcast_to(denominator[:, None], (tok_rows, EXTRA))
    weight_lanes = lanes(router_weight)
    gate_lanes = combine_lanes.astype(BF16)
    send_grads = jnp.dot(dispatch, grad_out, preferred_element_type=F32).astype(BF16)
    send_gates = jnp.dot(dispatch, gate_lanes, preferred_element_type=F32).astype(BF16)
    received = exchange(
        jnp.concatenate([send_grads, send_gates], axis=1).reshape(
            experts, capacity, model_width + EXTRA
        ),
        GROUP,
    ).reshape(slot_count, model_width + EXTRA)
    other_tokens = swap(slot_tokens, "core", 1)
    hidden_pre = jnp.dot(slot_tokens, weight_in, preferred_element_type=F32)
    normal_cdf, normal_pdf = gelu_parts(hidden_pre)
    hidden_act = (hidden_pre * normal_cdf).astype(BF16)
    act_slope = normal_cdf + hidden_pre * normal_pdf
    other_act = swap(hidden_act, "core", 1)
    left_in = (slot_tokens, other_tokens)
    left_out = (hidden_act, other_act)
    pos = jnp.stack([my_y, core, lax.axis_index(GROUP), lax.axis_index("zh")]).astype(jnp.int32)


    token_side = (dispatch, weight_lanes, probs_lanes, combine_lanes, keep_lanes, denominator_lanes)
    received, left_in, left_out, act_slope, token_side = tie(
        received, left_in, left_out, act_slope, token_side
    )
    dispatch, weight_lanes, probs_lanes, combine_lanes, keep_lanes, denominator_lanes = token_side
    my_out, give_out = scale_grads(pos, received)
    right_out = (my_out, swap(give_out, "core", 1))
    received, _ = tie(received, give_out)
    grad_pre, give_in, gate_grad = pre_grads(
        pos, received, weight_out, left_out[0], act_slope
    )
    right_in = (grad_pre, swap(give_in, "core", 1))

    sent = sent_parts(pos, left_out, right_out, left_in, right_in)
    got = (swap(sent[0], "y", 1), swap(sent[1], "y", 3))
    pre_for_slots, _ = tie(grad_pre, sent)
    grad_slots = slot_grads_of(pos, pre_for_slots, weight_in, gate_grad)
    back = exchange(
        grad_slots.reshape(experts, capacity, model_width + EXTRA), GROUP
    ).reshape(slot_count, model_width + EXTRA)

    left_in, left_out, right_in, right_out, _ = tie(
        left_in, left_out, right_in, right_out, grad_slots
    )
    *near, far_a, far_b = kept_parts(pos, left_out, right_out, left_in, right_in)
    got, far_a, far_b = tie(got, far_a, far_b)
    far_a, far_b = far_sums(pos, (far_a, far_b), got)
    far = (swap(far_a, "y", 3), swap(far_b, "y", 1))

    back, _ = tie(back, far_a)
    logit_lanes, router_part = router_grads(
        pos,
        dispatch,
        back,
        tokens,
        probs_lanes,
        combine_lanes,
        keep_lanes,
        denominator_lanes,
        grad_scale,
    )

    def router_round(value, axes, one, two):
        near, far, both = (swap(value, axes, mask) for mask in (one, two, one ^ two))
        return (value + near) + (far + both)

    router_part = router_round(router_part, "zh", 1, 3)
    near, far, router_part = tie(near, far, router_part)
    pieces = zh_pieces(pos, near[:2], near[2:], got, far, grad_scale)
    got = exchange(pieces, ("zh", "core"))

    back, router_part, _ = tie(back, router_part, pieces)
    grad_tokens = token_grads(pos, dispatch, back, logit_lanes, weight_lanes)
    router_part, _ = tie(router_part, grad_tokens)
    router_part = router_round(router_part, "x", 1, 3)
    router_part = router_round(router_part, "y", 1, 3)
    router_part = router_round(router_part, ("core", "zl"), 1, 2)
    got, router_part = tie(got, router_part)
    outer_share, inner_share = shares(pos, got, near[0].shape[0] // 8)
    return (grad_tokens, router_part.T, inner_share, outer_share)


def solution(mesh):
    fine = Mesh(mesh.devices.reshape(FINE_SHAPE), FINE)
    placed = (
        P(FINE, None),
        P(FINE, None),
        P(),
        P(GROUP, None, None),
        P(GROUP, None, None),
        P(FINE, None),
        P(FINE, None),
        P(FINE, None),
    )
    return jax.shard_map(
        per_device,
        mesh=fine,
        in_specs=placed,
        out_specs=(
            P(FINE, None),
            P(),
            P(GROUP, ("y", "zh", "core"), None),
            P(GROUP, ("y", "zh", "core"), None),
        ),
        check_vma=False,
    )
```

```python
import jax
import jax.numpy as jnp
from jax import lax
from jax.experimental import pallas as pl
from jax.experimental.pallas import tpu as pltpu
from jax.sharding import Mesh, PartitionSpec as P

FINE = ("y", "zh", "core", "x", "zl")
FINE_SHAPE = (4, 4, 2, 4, 2)
GROUP = ("x", "zl")
EXTRA = 128
VMEM_LIMIT = 20 * 1024 * 1024
LONG = 30_000_000_000
F32 = jnp.float32
BF16 = jnp.bfloat16


def gelu_parts(hidden_pre):
    normal_cdf = 0.5 * (1.0 + jax.scipy.special.erf(hidden_pre * 0.7071067811865476))
    normal_pdf = jnp.exp(-0.5 * hidden_pre * hidden_pre) * 0.3989422804014327
    return (normal_cdf, normal_pdf)


def contract_rows(left, right):
    return lax.dot_general(left, right, (((0,), (0,)), ((), ())), preferred_element_type=F32)


def contract_cols(left, right):
    return lax.dot_general(left, right, (((1,), (1,)), ((), ())), preferred_element_type=F32)


def swap(values, axis, mask):
    size = lax.axis_size(axis)
    return lax.ppermute(values, axis, [(i, i ^ mask) for i in range(size)])


def exchange(values, axes):
    return lax.all_to_all(values, axes, split_axis=0, concat_axis=0, tiled=True)


def tie(*values):
    return lax.optimization_barrier(values)


def call(body, pos, inputs, outputs, flops=1000, far=(), scratch=()):
    vmem = pl.BlockSpec(memory_space=pltpu.VMEM)
    return pl.pallas_call(
        body,
        in_specs=[pl.BlockSpec(memory_space=pltpu.SMEM)]
        + [vmem] * len(inputs)
        + [pl.BlockSpec(memory_space=pltpu.HBM)] * len(far),
        out_specs=[vmem] * len(outputs),
        out_shape=[jax.ShapeDtypeStruct(shape, dtype) for shape, dtype in outputs],
        scratch_shapes=scratch,
        cost_estimate=pl.CostEstimate(flops=flops, bytes_accessed=1000, transcendentals=0),
        compiler_params=pltpu.CompilerParams(vmem_limit_bytes=VMEM_LIMIT),
    )(pos, *inputs, *far)


def gate_of(pos, lanes):
    lane = lax.broadcasted_iota(jnp.int32, lanes.shape, 1)
    return jnp.sum(jnp.where(lane == pos[2], lanes.astype(F32), 0.0), axis=1, keepdims=True)


def scale_grads(pos, received):
    slots, wide = received.shape
    half = (wide - EXTRA) // 2
    rows = slots // 4

    def body(pos_ref, rec, mine, give):
        core = pos_ref[1]
        for r in range(0, slots, rows):
            at = slice(r, r + rows)
            gate = gate_of(pos_ref, rec[at, 2 * half :])
            for out, which in ((mine, core), (give, 1 - core)):
                start = pl.multiple_of(which * half, half)
                out[at, :] = (gate * rec[at, pl.ds(start, half)].astype(F32)).astype(BF16)

    return call(body, pos, [received], [((slots, half), BF16)] * 2)


def pre_grads(pos, received, weight_out, act, slope):
    slots, wide = received.shape
    hidden, width = weight_out.shape
    step = hidden // 4

    def body(pos_ref, rec, weight, act_ref, slope_ref, grad_pre, give, gate_grad):
        gate = gate_of(pos_ref, rec[:, width:])
        total = None
        for i in range(4):
            at = slice(i * step, (i + 1) * step)
            grad_act = lax.dot_general(
                rec[:, :width], weight[at, :], (((1,), (1,)), ((), ())), preferred_element_type=F32
            )
            part = jnp.sum(act_ref[:, at].astype(F32) * grad_act, axis=1, keepdims=True)
            total = part if total is None else total + part
            grad_pre[:, at] = (gate * grad_act * slope_ref[:, at]).astype(BF16)
        start = pl.multiple_of((1 - pos_ref[1]) * (hidden // 2), hidden // 2)
        give[...] = grad_pre[:, pl.ds(start, hidden // 2)]
        lane = lax.broadcasted_iota(jnp.int32, (slots, EXTRA), 1)
        gate_grad[...] = jnp.where(lane == pos_ref[2], total, 0.0).astype(BF16)

    return call(
        body,
        pos,
        [received, weight_out, act, slope],
        [((slots, hidden), BF16), ((slots, hidden // 2), BF16), ((slots, EXTRA), BF16)],
    )


def products(pos, left_out, right_out, left_in, right_in, masks, store, outputs, near):
    slots = left_in[0].shape[0]
    widths = left_out[0].shape[1] // 4, left_in[0].shape[1] // 4
    cols = right_out[1].shape[1] // 2, right_in[1].shape[1] // 2
    blocks = sorted({r for pair in masks for r in pair})

    def body(pos_ref, *refs):
        count = len(outputs)
        refs = list(refs)
        scratch = refs[8 + count :]
        outs = refs[8 : 8 + count]
        rights, lefts = (refs[:4], refs[4:8]) if near else (refs[4:8], refs[:4])
        buffers, sems = scratch[:2], scratch[2]
        held = scratch[3:7]
        copies = []
        for part in range(2):
            width = widths[part]
            for k in range(2):
                for n, r in enumerate(blocks):
                    start = pl.multiple_of((pos_ref[0] ^ r) * width, width)
                    copies.append(
                        pltpu.make_async_copy(
                            lefts[2 * part + k].at[:, pl.ds(start, width)],
                            buffers[part].at[k, n],
                            sems.at[2 * part + k, n],
                        )
                    )
            if not near:
                for k in range(2):
                    source = rights[2 * part + k]
                    if part == 1 and k == 0:
                        start = pl.multiple_of(pos_ref[1] * 2 * cols[1], 2 * cols[1])
                        source = source.at[:, pl.ds(start, 2 * cols[1])]
                    copies.append(
                        pltpu.make_async_copy(
                            source, held[2 * part + k], sems.at[2 * part + k, len(blocks)]
                        )
                    )
        for copy in copies:
            copy.start()
        dims = (((0,), (0,)), ((), ()))
        for part in range(2):
            each = len(copies) // 2
            for copy in copies[part * each : (part + 1) * each]:
                copy.wait()
            wide = cols[part]
            mine, other = (rights if near else held)[2 * part : 2 * part + 2]
            for i in range(2):
                own = i * wide
                if part and near:
                    own = pl.multiple_of((2 * pos_ref[1] + i) * wide, wide)
                for j in range(2):
                    n = blocks.index(masks[i][j])
                    value = lax.dot_general(
                        buffers[part][0, n],
                        mine[:, pl.ds(own, wide)],
                        dims,
                        preferred_element_type=F32,
                    )
                    value = value + lax.dot_general(
                        buffers[part][1, n],
                        other[:, i * wide : (i + 1) * wide],
                        dims,
                        preferred_element_type=F32,
                    )
                    store(outs, part, i, j, value)

    rights = [*right_out, *right_in]
    lefts = [*left_out, *left_in]
    scratch = [pltpu.VMEM((2, len(blocks), slots, width), BF16) for width in widths]
    scratch.append(pltpu.SemaphoreType.DMA((4, len(blocks) + 1)))
    if not near:
        scratch += [pltpu.VMEM((slots, 2 * cols[k // 2]), BF16) for k in range(4)]
    return call(
        body,
        pos,
        rights if near else [],
        outputs,
        far=lefts if near else lefts + rights,
        scratch=scratch,
    )


def sent_parts(pos, left_out, right_out, left_in, right_in):
    width_out, width_in = left_out[0].shape[1] // 4, left_in[0].shape[1] // 4
    cols_out, cols_in = right_out[1].shape[1] // 2, right_in[1].shape[1] // 2

    def store(outs, part, i, j, value):
        if part:
            outs[i][2 * width_out :, j * cols_in : (j + 1) * cols_in] = value.astype(BF16)
        else:
            outs[i][j * width_out : (j + 1) * width_out, :] = value.astype(BF16)

    outputs = [((2 * width_out + width_in, cols_out), BF16)] * 2
    sides = (left_out, right_out, left_in, right_in)
    return products(pos, *sides, ((1, 2), (3, 2)), store, outputs, True)


def kept_parts(pos, left_out, right_out, left_in, right_in):
    width_out, width_in = left_out[0].shape[1] // 4, left_in[0].shape[1] // 4
    cols_out, cols_in = right_out[1].shape[1] // 2, right_in[1].shape[1] // 2
    half = width_in // 2

    def store(outs, part, i, j, value):
        near_out, near_in, far = outs[:2], outs[2:4], outs[4:]
        if j == 0:
            (near_in if part else near_out)[i][...] = value
        elif part:
            far[i][width_out:, :cols_in] = value[:half, :]
            far[i][width_out:, cols_in:] = value[half:, :]
        else:
            far[i][:width_out, :] = value

    outputs = (
        [((width_out, cols_out), F32)] * 2
        + [((width_in, cols_in), F32)] * 2
        + [((width_out + half, cols_out), F32)] * 2
    )
    sides = (left_out, right_out, left_in, right_in)
    return products(pos, *sides, ((0, 3), (0, 1)), store, outputs, False)


def far_sums(pos, far, got):
    rows, cols = far[0].shape
    half, wide = rows // 2, cols // 2

    def body(pos_ref, far_a, far_b, got_a, got_b, out_a, out_b):
        for mine, arrived, out in ((far_a, got_a, out_a), (far_b, got_b, out_b)):
            out[:half, :] = (mine[:half, :] + arrived[half:rows, :].astype(F32)).astype(BF16)
            for k in range(2):
                at = slice(k * wide, (k + 1) * wide)
                value = arrived[rows + k * half : rows + (k + 1) * half, wide:].astype(F32)
                out[half:, at] = (mine[half:, at] + value).astype(BF16)

    return call(body, pos, [*far, *got], [((rows, cols), BF16)] * 2)


def zh_pieces(pos, near_out, near_in, got, far, scale):
    rows_out, cols_out = near_out[0].shape
    rows_in, cols_in = near_in[0].shape
    half = rows_in // 2
    share_out, share_in = rows_out // 8, rows_in // 8

    def body(pos_ref, out_a, out_b, in_a, in_b, got_a, got_b, far_a, far_b, pieces):
        sets = ((out_a, in_a, got_a, far_a), (out_b, in_b, got_b, far_b))
        for i, (out, inner, first, second) in enumerate(sets):
            value = out[...] + first[:rows_out, :].astype(F32) + second[:rows_out, :].astype(F32)
            value = (value * scale).astype(BF16).reshape(8, share_out, cols_out)
            pieces[:, :share_out, i * cols_out : (i + 1) * cols_out] = value
            for k in range(2):
                at = slice(2 * rows_out + k * half, 2 * rows_out + (k + 1) * half)
                value = inner[k * half : (k + 1) * half, :] + first[at, :cols_in].astype(F32)
                value = value + second[rows_out:, k * cols_in : (k + 1) * cols_in].astype(F32)
                value = (value * scale).astype(BF16).reshape(4, 2, share_in // 2, cols_in)
                for m in range(2):
                    start = m * 2 * cols_in + i * cols_in
                    pieces[4 * k : 4 * k + 4, share_out:, start : start + cols_in] = value[:, m]

    return call(
        body,
        pos,
        [*near_out, *near_in, *got, *far],
        [((8, share_out + share_in // 2, 2 * cols_out), BF16)],
        LONG,
    )[0]


def shares(pos, pieces, share_out):
    rows, cols = pieces.shape[1:]
    rows_in = rows - share_out
    cols_in = cols // 2

    def body(pos_ref, got, outer, inner):
        for c in range(2):
            value = sum(got[2 * z + c].astype(F32) for z in range(4))
            outer[:, c * cols : (c + 1) * cols] = value[:share_out]
            at = slice(c * cols_in, (c + 1) * cols_in)
            inner[:rows_in, at] = value[share_out:, :cols_in]
            inner[rows_in:, at] = value[share_out:, cols_in:]

    outer, inner = call(
        body, pos, [pieces], [((share_out, 2 * cols), F32), ((2 * rows_in, cols), F32)]
    )
    return outer[None], inner[None]


def slot_grads_of(pos, grad_pre, weight_in):
    slots, hidden = grad_pre.shape
    width = weight_in.shape[0]
    step = width // 4

    def body(pos_ref, grad, weight, out, held, sems):
        copies = []
        for i in range(4):
            at = pl.ds(i * step, step)
            copies.append(pltpu.make_async_copy(weight.at[at, :], held.at[at, :], sems.at[i]))
            copies[i].start()
        for i in range(4):
            at = slice(i * step, (i + 1) * step)
            copies[i].wait()
            out[:, at] = lax.dot_general(
                grad[...], held[at, :], (((1,), (1,)), ((), ())), preferred_element_type=F32
            ).astype(BF16)

    return call(
        body,
        pos,
        [grad_pre],
        [((slots, width), BF16)],
        far=[weight_in],
        scratch=[pltpu.VMEM((width, hidden), BF16), pltpu.SemaphoreType.DMA((4,))],
    )[0]


def router_grads(pos, dispatch, gate_back, token_lanes, tokens, scale):
    rows, width = tokens.shape
    experts = 8
    step = width // 4

    def body(pos_ref, disp, back, side, tok, logit, router, held, sem):
        copy = pltpu.make_async_copy(tok, held, sem)
        copy.start()
        dims = (((0,), (0,)), ((), ()))
        combine_grad = lax.dot_general(disp[...], back[...], dims, preferred_element_type=F32)
        probs, combine, keep, denominator = (side[k] for k in range(4))
        weighted = jnp.sum(combine_grad * combine, axis=1, keepdims=True)
        probs_grad = keep * (combine_grad - weighted) / denominator
        inner = jnp.sum(probs_grad * probs, axis=1, keepdims=True)
        logit_b = (probs * (probs_grad - inner)).astype(BF16)
        logit[...] = logit_b
        copy.wait()
        for i in range(4):
            at = slice(i * step, (i + 1) * step)
            part = lax.dot_general(logit_b, held[:, at], dims, preferred_element_type=F32)
            router[:, at] = part[:experts] * scale

    return call(
        body,
        pos,
        [dispatch, gate_back, token_lanes],
        [((rows, EXTRA), BF16), ((experts, width), F32)],
        far=[tokens],
        scratch=[pltpu.VMEM((rows, width), BF16), pltpu.SemaphoreType.DMA],
    )


def token_grads(pos, dispatch, back, logit_lanes, weight_lanes):
    rows, width = dispatch.shape[1], back.shape[1]
    step = width // 4

    def body(pos_ref, disp, flat, logit, weight, out):
        for i in range(4):
            at = slice(i * step, (i + 1) * step)
            value = lax.dot_general(
                disp[...], flat[:, at], (((0,), (0,)), ((), ())), preferred_element_type=F32
            )
            value = value + lax.dot_general(
                logit[...], weight[at, :], (((1,), (1,)), ((), ())), preferred_element_type=F32
            )
            out[:, at] = value.astype(BF16)

    return call(
        body, pos, [dispatch, back, logit_lanes, weight_lanes], [((rows, width), BF16)]
    )[0]


def per_device(
    tokens, grad_out, router_weight, weight_in, weight_out, expert_ids, slot_index, keep_mask
):
    tok_rows, model_width = tokens.shape
    experts = 8
    weight_in = weight_in[0]
    weight_out = weight_out[0]
    capacity = tok_rows * expert_ids.shape[1] // experts
    slot_count = experts * capacity
    grad_scale = float(tok_rows * 256) ** (-0.5)
    core = lax.axis_index("core")
    my_y = lax.axis_index("y")

    target = expert_ids * capacity + slot_index
    slot_iota = jnp.arange(slot_count, dtype=jnp.int32)[:, None]
    first_hit = (slot_iota == target[None, :, 0]) & (keep_mask[None, :, 0] == 1)
    second_hit = (slot_iota == target[None, :, 1]) & (keep_mask[None, :, 1] == 1)
    dispatch = (first_hit | second_hit).astype(BF16)

    send_tokens = jnp.dot(dispatch, tokens, preferred_element_type=F32).astype(BF16)
    slot_tokens = exchange(
        send_tokens.reshape(experts, capacity, model_width), GROUP
    ).reshape(slot_count, model_width)

    logits = jnp.dot(tokens, router_weight, preferred_element_type=F32)
    exp_logits = jnp.exp(logits)
    router_probs = exp_logits / jnp.sum(exp_logits, axis=1, keepdims=True)
    picked = expert_ids[:, :, None] == jnp.arange(experts, dtype=jnp.int32)[None, None, :]
    chosen = jnp.sum(jnp.where(picked, router_probs[:, None, :], 0.0), axis=2)
    keep_float = keep_mask.astype(F32)
    denominator = jnp.sum(keep_float * chosen, axis=1) + (1.0 - jnp.max(keep_float, axis=1))
    combine = keep_float * chosen / denominator[:, None]
    def lanes(values, fill=0.0):
        return jnp.pad(values, ((0, 0), (0, EXTRA - experts)), constant_values=fill)

    def per_expert(values):
        return jnp.sum(jnp.where(picked, values[:, :, None], 0.0), axis=1)

    combine_full = per_expert(combine)
    token_lanes = jnp.stack(
        [
            lanes(router_probs),
            lanes(combine_full),
            lanes(per_expert(keep_float)),
            lanes(jnp.broadcast_to(denominator[:, None], (tok_rows, experts)), 1.0),
        ]
    )
    weight_lanes = lanes(router_weight)
    gate_lanes = lanes(combine_full.astype(BF16))
    send_grads = jnp.dot(dispatch, grad_out, preferred_element_type=F32).astype(BF16)
    send_gates = jnp.dot(dispatch, gate_lanes, preferred_element_type=F32).astype(BF16)
    received = exchange(
        jnp.concatenate([send_grads, send_gates], axis=1).reshape(
            experts, capacity, model_width + EXTRA
        ),
        GROUP,
    ).reshape(slot_count, model_width + EXTRA)
    other_tokens = swap(slot_tokens, "core", 1)
    hidden_pre = jnp.dot(slot_tokens, weight_in, preferred_element_type=F32)
    normal_cdf, normal_pdf = gelu_parts(hidden_pre)
    hidden_act = (hidden_pre * normal_cdf).astype(BF16)
    act_slope = normal_cdf + hidden_pre * normal_pdf
    other_act = swap(hidden_act, "core", 1)
    left_in = (slot_tokens, other_tokens)
    left_out = (hidden_act, other_act)
    pos = jnp.stack([my_y, core, lax.axis_index(GROUP), lax.axis_index("zh")]).astype(jnp.int32)


    received, left_in, left_out, act_slope, dispatch, weight_lanes, token_lanes = tie(
        received, left_in, left_out, act_slope, dispatch, weight_lanes, token_lanes
    )
    my_out, give_out = scale_grads(pos, received)
    right_out = (my_out, swap(give_out, "core", 1))
    received, _ = tie(received, give_out)
    grad_pre, give_in, gate_grad = pre_grads(
        pos, received, weight_out, left_out[0], act_slope
    )
    right_in = (grad_pre, swap(give_in, "core", 1))

    sent = sent_parts(pos, left_out, right_out, left_in, right_in)
    got = (swap(sent[0], "y", 1), swap(sent[1], "y", 3))
    pre_for_slots, gate_grad, _ = tie(grad_pre, gate_grad, sent)
    gate_back = exchange(gate_grad.reshape(experts, capacity, EXTRA), GROUP).reshape(
        slot_count, EXTRA
    )
    grad_slots = slot_grads_of(pos, pre_for_slots, weight_in)
    grad_slots, gate_back = tie(grad_slots, gate_back)
    back = exchange(
        grad_slots.reshape(experts, capacity, model_width), GROUP
    ).reshape(slot_count, model_width)

    gate_back, _ = tie(gate_back, grad_slots)
    logit_lanes, router_part = router_grads(
        pos, dispatch, gate_back, token_lanes, tokens, grad_scale
    )

    def router_round(value, axes, one, two, *until):
        near, far, both = (swap(value, axes, mask) for mask in (one, two, one ^ two))
        value, near, far, both, _ = tie(value, near, far, both, until)
        return (value + near) + (far + both)

    left_in, left_out, right_in, right_out, _ = tie(
        left_in, left_out, right_in, right_out, router_part
    )
    *near, far_a, far_b = kept_parts(pos, left_out, right_out, left_in, right_in)
    got, far_a, far_b = tie(got, far_a, far_b)
    far_a, far_b = far_sums(pos, (far_a, far_b), got)
    far = (swap(far_a, "y", 3), swap(far_b, "y", 1))
    router_part = router_round(router_part, "zh", 1, 3, far_a)

    near, far, router_part = tie(near, far, router_part)
    pieces = zh_pieces(pos, near[:2], near[2:], got, far, grad_scale)
    got = exchange(pieces, ("zh", "core"))

    back, router_part, _ = tie(back, router_part, pieces)
    grad_tokens = token_grads(pos, dispatch, back, logit_lanes, weight_lanes)
    router_part, _ = tie(router_part, grad_tokens)
    router_part = router_round(router_part, "x", 1, 3)
    router_part = router_round(router_part, "y", 1, 3)
    router_part = router_round(router_part, ("core", "zl"), 1, 2)
    got, router_part = tie(got, router_part)
    outer_share, inner_share = shares(pos, got, near[0].shape[0] // 8)
    return (grad_tokens, router_part.T, inner_share, outer_share)


def solution(mesh):
    fine = Mesh(mesh.devices.reshape(FINE_SHAPE), FINE)
    placed = (
        P(FINE, None),
        P(FINE, None),
        P(),
        P(GROUP, None, None),
        P(GROUP, None, None),
        P(FINE, None),
        P(FINE, None),
        P(FINE, None),
    )
    return jax.shard_map(
        per_device,
        mesh=fine,
        in_specs=placed,
        out_specs=(
            P(FINE, None),
            P(),
            P(GROUP, ("y", "zh", "core"), None),
            P(GROUP, ("y", "zh", "core"), None),
        ),
        check_vma=False,
    )
```

```python
import jax
import jax.numpy as jnp
from jax import lax
from jax.experimental import pallas as pl
from jax.experimental.pallas import tpu as pltpu
from jax.sharding import Mesh, PartitionSpec as P

FINE = ("y", "zh", "core", "x", "zl")
FINE_SHAPE = (4, 4, 2, 4, 2)
GROUP = ("x", "zl")
EXTRA = 128
VMEM_LIMIT = 20 * 1024 * 1024
ALL_VMEM = 58 * 1024 * 1024
MOST_VMEM = 52 * 1024 * 1024
LONG = 28_000_000_000
F32 = jnp.float32
BF16 = jnp.bfloat16


def gelu_parts(hidden_pre):
    normal_cdf = 0.5 * (1.0 + jax.scipy.special.erf(hidden_pre * 0.7071067811865476))
    normal_pdf = jnp.exp(-0.5 * hidden_pre * hidden_pre) * 0.3989422804014327
    return (normal_cdf, normal_pdf)


def contract_rows(left, right):
    return lax.dot_general(left, right, (((0,), (0,)), ((), ())), preferred_element_type=F32)


def contract_cols(left, right):
    return lax.dot_general(left, right, (((1,), (1,)), ((), ())), preferred_element_type=F32)


def swap(values, axis, mask):
    size = lax.axis_size(axis)
    return lax.ppermute(values, axis, [(i, i ^ mask) for i in range(size)])


def exchange(values, axes):
    return lax.all_to_all(values, axes, split_axis=0, concat_axis=0, tiled=True)


def tie(*values):
    return lax.optimization_barrier(values)


def call(body, pos, inputs, outputs, flops=1000, far=(), scratch=(), vmem_limit=VMEM_LIMIT):
    vmem = pl.BlockSpec(memory_space=pltpu.VMEM)
    return pl.pallas_call(
        body,
        in_specs=[pl.BlockSpec(memory_space=pltpu.SMEM)]
        + [vmem] * len(inputs)
        + [pl.BlockSpec(memory_space=pltpu.HBM)] * len(far),
        out_specs=[vmem] * len(outputs),
        out_shape=[jax.ShapeDtypeStruct(shape, dtype) for shape, dtype in outputs],
        scratch_shapes=scratch,
        cost_estimate=pl.CostEstimate(flops=flops, bytes_accessed=1000, transcendentals=0),
        compiler_params=pltpu.CompilerParams(vmem_limit_bytes=vmem_limit),
    )(pos, *inputs, *far)


def gate_of(pos, lanes):
    lane = lax.broadcasted_iota(jnp.int32, lanes.shape, 1)
    return jnp.sum(jnp.where(lane == pos[2], lanes.astype(F32), 0.0), axis=1, keepdims=True)


def scale_grads(pos, received):
    slots, wide = received.shape
    half = (wide - EXTRA) // 2
    rows = slots // 4

    def body(pos_ref, rec, mine, give):
        core = pos_ref[1]
        for r in range(0, slots, rows):
            at = slice(r, r + rows)
            gate = gate_of(pos_ref, rec[at, 2 * half :])
            for out, which in ((mine, core), (give, 1 - core)):
                start = pl.multiple_of(which * half, half)
                out[at, :] = (gate * rec[at, pl.ds(start, half)].astype(F32)).astype(BF16)

    return call(body, pos, [received], [((slots, half), BF16)] * 2)


def pre_grads(pos, received, weight_out, act, slope):
    slots, wide = received.shape
    hidden, width = weight_out.shape
    step = hidden // 4

    def body(pos_ref, rec, weight, act_ref, slope_ref, grad_pre, give, gate_grad):
        gate = gate_of(pos_ref, rec[:, width:])
        total = None
        for i in range(4):
            at = slice(i * step, (i + 1) * step)
            grad_act = lax.dot_general(
                rec[:, :width], weight[at, :], (((1,), (1,)), ((), ())), preferred_element_type=F32
            )
            part = jnp.sum(act_ref[:, at].astype(F32) * grad_act, axis=1, keepdims=True)
            total = part if total is None else total + part
            grad_pre[:, at] = (gate * grad_act * slope_ref[:, at]).astype(BF16)
        start = pl.multiple_of((1 - pos_ref[1]) * (hidden // 2), hidden // 2)
        give[...] = grad_pre[:, pl.ds(start, hidden // 2)]
        lane = lax.broadcasted_iota(jnp.int32, (slots, EXTRA), 1)
        gate_grad[...] = jnp.where(lane == pos_ref[2], total, 0.0).astype(BF16)

    return call(
        body,
        pos,
        [received, weight_out, act, slope],
        [((slots, hidden), BF16), ((slots, hidden // 2), BF16), ((slots, EXTRA), BF16)],
    )


def products(pos, left_out, right_out, left_in, right_in, masks, store, outputs, near):
    slots = left_in[0].shape[0]
    widths = left_out[0].shape[1] // 4, left_in[0].shape[1] // 4
    cols = right_out[1].shape[1] // 2, right_in[1].shape[1] // 2
    blocks = sorted({r for pair in masks for r in pair})

    def body(pos_ref, *refs):
        count = len(outputs)
        refs = list(refs)
        scratch = refs[8 + count :]
        outs = refs[8 : 8 + count]
        rights, lefts = (refs[:4], refs[4:8]) if near else (refs[4:8], refs[:4])
        buffers, sems = scratch[:2], scratch[2]
        held = scratch[3:7]
        copies = []
        for part in range(2):
            width = widths[part]
            for k in range(2):
                for n, r in enumerate(blocks):
                    start = pl.multiple_of((pos_ref[0] ^ r) * width, width)
                    copies.append(
                        pltpu.make_async_copy(
                            lefts[2 * part + k].at[:, pl.ds(start, width)],
                            buffers[part].at[k, n],
                            sems.at[2 * part + k, n],
                        )
                    )
            if not near:
                for k in range(2):
                    source = rights[2 * part + k]
                    if part == 1 and k == 0:
                        start = pl.multiple_of(pos_ref[1] * 2 * cols[1], 2 * cols[1])
                        source = source.at[:, pl.ds(start, 2 * cols[1])]
                    copies.append(
                        pltpu.make_async_copy(
                            source, held[2 * part + k], sems.at[2 * part + k, len(blocks)]
                        )
                    )
        for copy in copies:
            copy.start()
        dims = (((0,), (0,)), ((), ()))
        for part in range(2):
            each = len(copies) // 2
            for copy in copies[part * each : (part + 1) * each]:
                copy.wait()
            wide = cols[part]
            mine, other = (rights if near else held)[2 * part : 2 * part + 2]
            for i in range(2):
                own = i * wide
                if part and near:
                    own = pl.multiple_of((2 * pos_ref[1] + i) * wide, wide)
                for j in range(2):
                    n = blocks.index(masks[i][j])
                    value = lax.dot_general(
                        buffers[part][0, n],
                        mine[:, pl.ds(own, wide)],
                        dims,
                        preferred_element_type=F32,
                    )
                    value = value + lax.dot_general(
                        buffers[part][1, n],
                        other[:, i * wide : (i + 1) * wide],
                        dims,
                        preferred_element_type=F32,
                    )
                    store(outs, part, i, j, value)

    rights = [*right_out, *right_in]
    lefts = [*left_out, *left_in]
    scratch = [pltpu.VMEM((2, len(blocks), slots, width), BF16) for width in widths]
    scratch.append(pltpu.SemaphoreType.DMA((4, len(blocks) + 1)))
    if not near:
        scratch += [pltpu.VMEM((slots, 2 * cols[k // 2]), BF16) for k in range(4)]
    return call(
        body,
        pos,
        rights if near else [],
        outputs,
        far=lefts if near else lefts + rights,
        scratch=scratch,
        vmem_limit=VMEM_LIMIT if near else MOST_VMEM,
    )


def sent_parts(pos, left_out, right_out, left_in, right_in):
    width_out, width_in = left_out[0].shape[1] // 4, left_in[0].shape[1] // 4
    cols_out, cols_in = right_out[1].shape[1] // 2, right_in[1].shape[1] // 2

    def store(outs, part, i, j, value):
        if part:
            outs[i][2 * width_out :, j * cols_in : (j + 1) * cols_in] = value.astype(BF16)
        else:
            outs[i][j * width_out : (j + 1) * width_out, :] = value.astype(BF16)

    outputs = [((2 * width_out + width_in, cols_out), BF16)] * 2
    sides = (left_out, right_out, left_in, right_in)
    return products(pos, *sides, ((1, 2), (3, 2)), store, outputs, True)


def kept_parts(pos, left_out, right_out, left_in, right_in):
    width_out, width_in = left_out[0].shape[1] // 4, left_in[0].shape[1] // 4
    cols_out, cols_in = right_out[1].shape[1] // 2, right_in[1].shape[1] // 2
    half = width_in // 2

    def store(outs, part, i, j, value):
        near_out, near_in, far = outs[:2], outs[2:4], outs[4:]
        if j == 0:
            (near_in if part else near_out)[i][...] = value
        elif part:
            far[i][width_out:, :cols_in] = value[:half, :]
            far[i][width_out:, cols_in:] = value[half:, :]
        else:
            far[i][:width_out, :] = value

    outputs = (
        [((width_out, cols_out), F32)] * 2
        + [((width_in, cols_in), F32)] * 2
        + [((width_out + half, cols_out), F32)] * 2
    )
    sides = (left_out, right_out, left_in, right_in)
    return products(pos, *sides, ((0, 3), (0, 1)), store, outputs, False)


def far_sums(pos, far, got):
    rows, cols = far[0].shape
    half, wide = rows // 2, cols // 2

    def body(pos_ref, far_a, far_b, got_a, got_b, out_a, out_b):
        for mine, arrived, out in ((far_a, got_a, out_a), (far_b, got_b, out_b)):
            out[:half, :] = (mine[:half, :] + arrived[half:rows, :].astype(F32)).astype(BF16)
            for k in range(2):
                at = slice(k * wide, (k + 1) * wide)
                value = arrived[rows + k * half : rows + (k + 1) * half, wide:].astype(F32)
                out[half:, at] = (mine[half:, at] + value).astype(BF16)

    return call(body, pos, [*far, *got], [((rows, cols), BF16)] * 2)


def zh_pieces(pos, near_out, near_in, got, far, scale):
    rows_out, cols_out = near_out[0].shape
    rows_in, cols_in = near_in[0].shape
    half = rows_in // 2
    share_out, share_in = rows_out // 8, rows_in // 8

    def body(pos_ref, out_a, out_b, in_a, in_b, got_a, got_b, far_a, far_b, pieces):
        sets = ((out_a, in_a, got_a, far_a), (out_b, in_b, got_b, far_b))
        for i, (out, inner, first, second) in enumerate(sets):
            value = out[...] + first[:rows_out, :].astype(F32) + second[:rows_out, :].astype(F32)
            value = (value * scale).astype(BF16).reshape(8, share_out, cols_out)
            pieces[:, :share_out, i * cols_out : (i + 1) * cols_out] = value
            for k in range(2):
                at = slice(2 * rows_out + k * half, 2 * rows_out + (k + 1) * half)
                value = inner[k * half : (k + 1) * half, :] + first[at, :cols_in].astype(F32)
                value = value + second[rows_out:, k * cols_in : (k + 1) * cols_in].astype(F32)
                value = (value * scale).astype(BF16).reshape(4, 2, share_in // 2, cols_in)
                for m in range(2):
                    start = m * 2 * cols_in + i * cols_in
                    pieces[4 * k : 4 * k + 4, share_out:, start : start + cols_in] = value[:, m]

    return call(
        body,
        pos,
        [*near_out, *near_in, *got, *far],
        [((8, share_out + share_in // 2, 2 * cols_out), BF16)],
        LONG,
    )[0]


def shares(pos, pieces, share_out):
    rows, cols = pieces.shape[1:]
    rows_in = rows - share_out
    cols_in = cols // 2

    def body(pos_ref, got, outer, inner):
        for c in range(2):
            value = sum(got[2 * z + c].astype(F32) for z in range(4))
            outer[:, c * cols : (c + 1) * cols] = value[:share_out]
            at = slice(c * cols_in, (c + 1) * cols_in)
            inner[:rows_in, at] = value[share_out:, :cols_in]
            inner[rows_in:, at] = value[share_out:, cols_in:]

    outer, inner = call(
        body, pos, [pieces], [((share_out, 2 * cols), F32), ((2 * rows_in, cols), F32)]
    )
    return outer[None], inner[None]


def slot_grads_of(pos, grad_pre, weight_in):
    slots, hidden = grad_pre.shape
    width = weight_in.shape[0]
    step = width // 4

    def body(pos_ref, grad, weight, out, held, sems):
        copies = []
        for i in range(4):
            at = pl.ds(i * step, step)
            copies.append(pltpu.make_async_copy(weight.at[at, :], held.at[at, :], sems.at[i]))
            copies[i].start()
        for i in range(4):
            at = slice(i * step, (i + 1) * step)
            copies[i].wait()
            out[:, at] = lax.dot_general(
                grad[...], held[at, :], (((1,), (1,)), ((), ())), preferred_element_type=F32
            ).astype(BF16)

    return call(
        body,
        pos,
        [grad_pre],
        [((slots, width), BF16)],
        far=[weight_in],
        scratch=[pltpu.VMEM((width, hidden), BF16), pltpu.SemaphoreType.DMA((4,))],
        vmem_limit=ALL_VMEM,
    )[0]


def router_grads(pos, dispatch, gate_back, token_lanes, tokens, scale):
    rows, width = tokens.shape
    experts = 8
    step = width // 4

    def body(pos_ref, disp, back, side, tok, logit, router, held, sem):
        copy = pltpu.make_async_copy(tok, held, sem)
        copy.start()
        dims = (((0,), (0,)), ((), ()))
        combine_grad = lax.dot_general(disp[...], back[...], dims, preferred_element_type=F32)
        probs, combine, keep, denominator = (side[k] for k in range(4))
        weighted = jnp.sum(combine_grad * combine, axis=1, keepdims=True)
        probs_grad = keep * (combine_grad - weighted) / denominator
        inner = jnp.sum(probs_grad * probs, axis=1, keepdims=True)
        logit_b = (probs * (probs_grad - inner)).astype(BF16)
        logit[...] = logit_b
        copy.wait()
        for i in range(4):
            at = slice(i * step, (i + 1) * step)
            part = lax.dot_general(logit_b, held[:, at], dims, preferred_element_type=F32)
            router[:, at] = part[:experts] * scale

    return call(
        body,
        pos,
        [dispatch, gate_back, token_lanes],
        [((rows, EXTRA), BF16), ((experts, width), F32)],
        far=[tokens],
        scratch=[pltpu.VMEM((rows, width), BF16), pltpu.SemaphoreType.DMA],
        vmem_limit=ALL_VMEM,
    )


def token_grads(pos, dispatch, back, logit_lanes, weight_lanes):
    rows, width = dispatch.shape[1], back.shape[1]
    step = width // 4

    def body(pos_ref, disp, flat, logit, weight, out):
        for i in range(4):
            at = slice(i * step, (i + 1) * step)
            value = lax.dot_general(
                disp[...], flat[:, at], (((0,), (0,)), ((), ())), preferred_element_type=F32
            )
            value = value + lax.dot_general(
                logit[...], weight[at, :], (((1,), (1,)), ((), ())), preferred_element_type=F32
            )
            out[:, at] = value.astype(BF16)

    return call(
        body, pos, [dispatch, back, logit_lanes, weight_lanes], [((rows, width), BF16)]
    )[0]


def per_device(
    tokens, grad_out, router_weight, weight_in, weight_out, expert_ids, slot_index, keep_mask
):
    tok_rows, model_width = tokens.shape
    experts = 8
    weight_in = weight_in[0]
    weight_out = weight_out[0]
    capacity = tok_rows * expert_ids.shape[1] // experts
    slot_count = experts * capacity
    grad_scale = float(tok_rows * 256) ** (-0.5)
    core = lax.axis_index("core")
    my_y = lax.axis_index("y")

    target = expert_ids * capacity + slot_index
    slot_iota = jnp.arange(slot_count, dtype=jnp.int32)[:, None]
    first_hit = (slot_iota == target[None, :, 0]) & (keep_mask[None, :, 0] == 1)
    second_hit = (slot_iota == target[None, :, 1]) & (keep_mask[None, :, 1] == 1)
    dispatch = (first_hit | second_hit).astype(BF16)

    send_tokens = jnp.dot(dispatch, tokens, preferred_element_type=F32).astype(BF16)
    slot_tokens = exchange(
        send_tokens.reshape(experts, capacity, model_width), GROUP
    ).reshape(slot_count, model_width)

    logits = jnp.dot(tokens, router_weight, preferred_element_type=F32)
    exp_logits = jnp.exp(logits)
    router_probs = exp_logits / jnp.sum(exp_logits, axis=1, keepdims=True)
    picked = expert_ids[:, :, None] == jnp.arange(experts, dtype=jnp.int32)[None, None, :]
    chosen = jnp.sum(jnp.where(picked, router_probs[:, None, :], 0.0), axis=2)
    keep_float = keep_mask.astype(F32)
    denominator = jnp.sum(keep_float * chosen, axis=1) + (1.0 - jnp.max(keep_float, axis=1))
    combine = keep_float * chosen / denominator[:, None]
    def lanes(values, fill=0.0):
        return jnp.pad(values, ((0, 0), (0, EXTRA - experts)), constant_values=fill)

    def per_expert(values):
        return jnp.sum(jnp.where(picked, values[:, :, None], 0.0), axis=1)

    combine_full = per_expert(combine)
    token_lanes = jnp.stack(
        [
            lanes(router_probs),
            lanes(combine_full),
            lanes(per_expert(keep_float)),
            lanes(jnp.broadcast_to(denominator[:, None], (tok_rows, experts)), 1.0),
        ]
    )
    weight_lanes = lanes(router_weight)
    gate_lanes = lanes(combine_full.astype(BF16))
    send_grads = jnp.dot(dispatch, grad_out, preferred_element_type=F32).astype(BF16)
    send_gates = jnp.dot(dispatch, gate_lanes, preferred_element_type=F32).astype(BF16)
    received = exchange(
        jnp.concatenate([send_grads, send_gates], axis=1).reshape(
            experts, capacity, model_width + EXTRA
        ),
        GROUP,
    ).reshape(slot_count, model_width + EXTRA)
    other_tokens = swap(slot_tokens, "core", 1)
    hidden_pre = jnp.dot(slot_tokens, weight_in, preferred_element_type=F32)
    normal_cdf, normal_pdf = gelu_parts(hidden_pre)
    hidden_act = (hidden_pre * normal_cdf).astype(BF16)
    act_slope = normal_cdf + hidden_pre * normal_pdf
    other_act = swap(hidden_act, "core", 1)
    left_in = (slot_tokens, other_tokens)
    left_out = (hidden_act, other_act)
    pos = jnp.stack([my_y, core, lax.axis_index(GROUP), lax.axis_index("zh")]).astype(jnp.int32)


    received, left_in, left_out, act_slope, dispatch, weight_lanes, token_lanes = tie(
        received, left_in, left_out, act_slope, dispatch, weight_lanes, token_lanes
    )
    my_out, give_out = scale_grads(pos, received)
    right_out = (my_out, swap(give_out, "core", 1))
    received, _ = tie(received, give_out)
    grad_pre, give_in, gate_grad = pre_grads(
        pos, received, weight_out, left_out[0], act_slope
    )
    right_in = (grad_pre, swap(give_in, "core", 1))

    sent = sent_parts(pos, left_out, right_out, left_in, right_in)
    got = (swap(sent[0], "y", 1), swap(sent[1], "y", 3))
    pre_for_slots, gate_grad, _ = tie(grad_pre, gate_grad, sent)
    gate_back = exchange(gate_grad.reshape(experts, capacity, EXTRA), GROUP).reshape(
        slot_count, EXTRA
    )
    grad_slots = slot_grads_of(pos, pre_for_slots, weight_in)
    grad_slots, gate_back = tie(grad_slots, gate_back)
    back = exchange(
        grad_slots.reshape(experts, capacity, model_width), GROUP
    ).reshape(slot_count, model_width)

    gate_back, _ = tie(gate_back, grad_slots)
    logit_lanes, router_part = router_grads(
        pos, dispatch, gate_back, token_lanes, tokens, grad_scale
    )

    def router_round(value, axes, one, two, *until):
        near, far, both = (swap(value, axes, mask) for mask in (one, two, one ^ two))
        value, near, far, both, _ = tie(value, near, far, both, until)
        return (value + near) + (far + both)

    left_in, left_out, right_in, right_out, _ = tie(
        left_in, left_out, right_in, right_out, router_part
    )
    *near, far_a, far_b = kept_parts(pos, left_out, right_out, left_in, right_in)
    got, far_a, far_b = tie(got, far_a, far_b)
    far_a, far_b = far_sums(pos, (far_a, far_b), got)
    far = (swap(far_a, "y", 3), swap(far_b, "y", 1))
    other_router = swap(router_part, "core", 1)
    router_part, other_router, _ = tie(router_part, other_router, far_a)
    router_part = router_part + other_router

    near, far, router_part = tie(near, far, router_part)
    pieces = zh_pieces(pos, near[:2], near[2:], got, far, grad_scale)
    got = exchange(pieces, ("zh", "core"))

    back, router_part, _ = tie(back, router_part, pieces)
    grad_tokens = token_grads(pos, dispatch, back, logit_lanes, weight_lanes)
    router_part = router_round(router_part, "x", 1, 3, grad_tokens)
    router_part = router_round(router_part, "y", 1, 3)
    router_part = router_part + swap(router_part, "zl", 1)
    router_part = router_round(router_part, "zh", 1, 3)
    got, router_part = tie(got, router_part)
    outer_share, inner_share = shares(pos, got, near[0].shape[0] // 8)
    return (grad_tokens, router_part.T, inner_share, outer_share)


def solution(mesh):
    fine = Mesh(mesh.devices.reshape(FINE_SHAPE), FINE)
    placed = (
        P(FINE, None),
        P(FINE, None),
        P(),
        P(GROUP, None, None),
        P(GROUP, None, None),
        P(FINE, None),
        P(FINE, None),
        P(FINE, None),
    )
    return jax.shard_map(
        per_device,
        mesh=fine,
        in_specs=placed,
        out_specs=(
            P(FINE, None),
            P(),
            P(GROUP, ("y", "zh", "core"), None),
            P(GROUP, ("y", "zh", "core"), None),
        ),
        check_vma=False,
    )
```

```python
import jax
import jax.numpy as jnp
from jax import lax
from jax.experimental import pallas as pl
from jax.experimental.pallas import tpu as pltpu
from jax.sharding import Mesh, PartitionSpec as P

FINE = ("y", "zh", "core", "x", "zl")
FINE_SHAPE = (4, 4, 2, 4, 2)
GROUP = ("x", "zl")
EXTRA = 128
VMEM_LIMIT = 20 * 1024 * 1024
ALL_VMEM = 58 * 1024 * 1024
MOST_VMEM = 52 * 1024 * 1024
LONG = 28_000_000_000
F32 = jnp.float32
BF16 = jnp.bfloat16


def gelu_parts(hidden_pre):
    normal_cdf = 0.5 * (1.0 + jax.scipy.special.erf(hidden_pre * 0.7071067811865476))
    normal_pdf = jnp.exp(-0.5 * hidden_pre * hidden_pre) * 0.3989422804014327
    return (normal_cdf, normal_pdf)


def contract_rows(left, right):
    return lax.dot_general(left, right, (((0,), (0,)), ((), ())), preferred_element_type=F32)


def contract_cols(left, right):
    return lax.dot_general(left, right, (((1,), (1,)), ((), ())), preferred_element_type=F32)


def swap(values, axis, mask):
    size = lax.axis_size(axis)
    return lax.ppermute(values, axis, [(i, i ^ mask) for i in range(size)])


def exchange(values, axes):
    return lax.all_to_all(values, axes, split_axis=0, concat_axis=0, tiled=True)


def tie(*values):
    return lax.optimization_barrier(values)


def call(body, pos, inputs, outputs, flops=1000, far=(), scratch=(), vmem_limit=VMEM_LIMIT):
    vmem = pl.BlockSpec(memory_space=pltpu.VMEM)
    return pl.pallas_call(
        body,
        in_specs=[pl.BlockSpec(memory_space=pltpu.SMEM)]
        + [vmem] * len(inputs)
        + [pl.BlockSpec(memory_space=pltpu.HBM)] * len(far),
        out_specs=[vmem] * len(outputs),
        out_shape=[jax.ShapeDtypeStruct(shape, dtype) for shape, dtype in outputs],
        scratch_shapes=scratch,
        cost_estimate=pl.CostEstimate(flops=flops, bytes_accessed=1000, transcendentals=0),
        compiler_params=pltpu.CompilerParams(vmem_limit_bytes=vmem_limit),
    )(pos, *inputs, *far)


def gate_of(pos, lanes):
    lane = lax.broadcasted_iota(jnp.int32, lanes.shape, 1)
    return jnp.sum(jnp.where(lane == pos[2], lanes.astype(F32), 0.0), axis=1, keepdims=True)


def scale_grads(pos, received):
    slots, wide = received.shape
    half = (wide - EXTRA) // 2
    rows = slots // 4

    def body(pos_ref, rec, mine, give):
        core = pos_ref[1]
        for r in range(0, slots, rows):
            at = slice(r, r + rows)
            gate = gate_of(pos_ref, rec[at, 2 * half :])
            for out, which in ((mine, core), (give, 1 - core)):
                start = pl.multiple_of(which * half, half)
                out[at, :] = (gate * rec[at, pl.ds(start, half)].astype(F32)).astype(BF16)

    return call(body, pos, [received], [((slots, half), BF16)] * 2)


def pre_grads(pos, received, weight_out, act, slope):
    slots, wide = received.shape
    hidden, width = weight_out.shape
    step = hidden // 4

    def body(pos_ref, rec, weight, act_ref, slope_ref, grad_pre, give, gate_grad):
        gate = gate_of(pos_ref, rec[:, width:])
        total = None
        for i in range(4):
            at = slice(i * step, (i + 1) * step)
            grad_act = lax.dot_general(
                rec[:, :width], weight[at, :], (((1,), (1,)), ((), ())), preferred_element_type=F32
            )
            part = jnp.sum(act_ref[:, at].astype(F32) * grad_act, axis=1, keepdims=True)
            total = part if total is None else total + part
            grad_pre[:, at] = (gate * grad_act * slope_ref[:, at]).astype(BF16)
        start = pl.multiple_of((1 - pos_ref[1]) * (hidden // 2), hidden // 2)
        give[...] = grad_pre[:, pl.ds(start, hidden // 2)]
        lane = lax.broadcasted_iota(jnp.int32, (slots, EXTRA), 1)
        gate_grad[...] = jnp.where(lane == pos_ref[2], total, 0.0).astype(BF16)

    return call(
        body,
        pos,
        [received, weight_out, act, slope],
        [((slots, hidden), BF16), ((slots, hidden // 2), BF16), ((slots, EXTRA), BF16)],
    )


def products(pos, left_out, right_out, left_in, right_in, masks, store, outputs, near):
    slots = left_in[0].shape[0]
    widths = left_out[0].shape[1] // 4, left_in[0].shape[1] // 4
    cols = right_out[1].shape[1] // 2, right_in[1].shape[1] // 2
    blocks = sorted({r for pair in masks for r in pair})

    def body(pos_ref, *refs):
        count = len(outputs)
        refs = list(refs)
        scratch = refs[8 + count :]
        outs = refs[8 : 8 + count]
        rights, lefts = (refs[:4], refs[4:8]) if near else (refs[4:8], refs[:4])
        buffers, sems = scratch[:2], scratch[2]
        held = scratch[3:7]
        copies = []
        for part in range(2):
            width = widths[part]
            for k in range(2):
                for n, r in enumerate(blocks):
                    start = pl.multiple_of((pos_ref[0] ^ r) * width, width)
                    copies.append(
                        pltpu.make_async_copy(
                            lefts[2 * part + k].at[:, pl.ds(start, width)],
                            buffers[part].at[k, n],
                            sems.at[2 * part + k, n],
                        )
                    )
            if not near:
                for k in range(2):
                    source = rights[2 * part + k]
                    if part == 1 and k == 0:
                        start = pl.multiple_of(pos_ref[1] * 2 * cols[1], 2 * cols[1])
                        source = source.at[:, pl.ds(start, 2 * cols[1])]
                    copies.append(
                        pltpu.make_async_copy(
                            source, held[2 * part + k], sems.at[2 * part + k, len(blocks)]
                        )
                    )
        for copy in copies:
            copy.start()
        dims = (((0,), (0,)), ((), ()))
        for part in range(2):
            each = len(copies) // 2
            for copy in copies[part * each : (part + 1) * each]:
                copy.wait()
            wide = cols[part]
            mine, other = (rights if near else held)[2 * part : 2 * part + 2]
            for i in range(2):
                own = i * wide
                if part and near:
                    own = pl.multiple_of((2 * pos_ref[1] + i) * wide, wide)
                for j in range(len(masks[i])):
                    n = blocks.index(masks[i][j])
                    value = lax.dot_general(
                        buffers[part][0, n],
                        mine[:, pl.ds(own, wide)],
                        dims,
                        preferred_element_type=F32,
                    )
                    value = value + lax.dot_general(
                        buffers[part][1, n],
                        other[:, i * wide : (i + 1) * wide],
                        dims,
                        preferred_element_type=F32,
                    )
                    store(outs, part, i, j, value)

    rights = [*right_out, *right_in]
    lefts = [*left_out, *left_in]
    scratch = [pltpu.VMEM((2, len(blocks), slots, width), BF16) for width in widths]
    scratch.append(pltpu.SemaphoreType.DMA((4, len(blocks) + 1)))
    if not near:
        scratch += [pltpu.VMEM((slots, 2 * cols[k // 2]), BF16) for k in range(4)]
    return call(
        body,
        pos,
        rights if near else [],
        outputs,
        far=lefts if near else lefts + rights,
        scratch=scratch,
        vmem_limit=VMEM_LIMIT if near else MOST_VMEM,
    )


def sent_parts(pos, left_out, right_out, left_in, right_in):
    width_out, width_in = left_out[0].shape[1] // 4, left_in[0].shape[1] // 4
    cols_out, cols_in = right_out[1].shape[1] // 2, right_in[1].shape[1] // 2

    def store(outs, part, i, j, value):
        if part:
            outs[i][2 * width_out :, j * cols_in : (j + 1) * cols_in] = value.astype(BF16)
        else:
            outs[i][j * width_out : (j + 1) * width_out, :] = value.astype(BF16)

    outputs = [((2 * width_out + width_in, cols_out), BF16)] * 2
    sides = (left_out, right_out, left_in, right_in)
    return products(pos, *sides, ((1, 2), (3, 2)), store, outputs, True)


def far_parts(pos, left_out, right_out, left_in, right_in):
    width_out, width_in = left_out[0].shape[1] // 4, left_in[0].shape[1] // 4
    cols_out, cols_in = right_out[1].shape[1] // 2, right_in[1].shape[1] // 2
    half = width_in // 2

    def store(outs, part, i, j, value):
        if part:
            outs[i][width_out:, :cols_in] = value[:half, :]
            outs[i][width_out:, cols_in:] = value[half:, :]
        else:
            outs[i][:width_out, :] = value

    outputs = [((width_out + half, cols_out), F32)] * 2
    sides = (left_out, right_out, left_in, right_in)
    return products(pos, *sides, ((3,), (1,)), store, outputs, False)


def near_parts(pos, left_out, right_out, left_in, right_in):
    width_out, width_in = left_out[0].shape[1] // 4, left_in[0].shape[1] // 4
    cols_out, cols_in = right_out[1].shape[1] // 2, right_in[1].shape[1] // 2

    def store(outs, part, i, j, value):
        outs[2 * part + i][...] = value

    outputs = [((width_out, cols_out), F32)] * 2 + [((width_in, cols_in), F32)] * 2
    sides = (left_out, right_out, left_in, right_in)
    return products(pos, *sides, ((0,), (0,)), store, outputs, False)


def far_sums(pos, far, got):
    rows, cols = far[0].shape
    half, wide = rows // 2, cols // 2

    def body(pos_ref, far_a, far_b, got_a, got_b, out_a, out_b):
        for mine, arrived, out in ((far_a, got_a, out_a), (far_b, got_b, out_b)):
            out[:half, :] = (mine[:half, :] + arrived[half:rows, :].astype(F32)).astype(BF16)
            for k in range(2):
                at = slice(k * wide, (k + 1) * wide)
                value = arrived[rows + k * half : rows + (k + 1) * half, wide:].astype(F32)
                out[half:, at] = (mine[half:, at] + value).astype(BF16)

    return call(body, pos, [*far, *got], [((rows, cols), BF16)] * 2)


def zh_pieces(pos, near_out, near_in, got, far, scale):
    rows_out, cols_out = near_out[0].shape
    rows_in, cols_in = near_in[0].shape
    half = rows_in // 2
    share_out, share_in = rows_out // 8, rows_in // 8

    def body(pos_ref, out_a, out_b, in_a, in_b, got_a, got_b, far_a, far_b, pieces):
        sets = ((out_a, in_a, got_a, far_a), (out_b, in_b, got_b, far_b))
        for i, (out, inner, first, second) in enumerate(sets):
            value = out[...] + first[:rows_out, :].astype(F32) + second[:rows_out, :].astype(F32)
            value = (value * scale).astype(BF16).reshape(8, share_out, cols_out)
            pieces[:, :share_out, i * cols_out : (i + 1) * cols_out] = value
            for k in range(2):
                at = slice(2 * rows_out + k * half, 2 * rows_out + (k + 1) * half)
                value = inner[k * half : (k + 1) * half, :] + first[at, :cols_in].astype(F32)
                value = value + second[rows_out:, k * cols_in : (k + 1) * cols_in].astype(F32)
                value = (value * scale).astype(BF16).reshape(4, 2, share_in // 2, cols_in)
                for m in range(2):
                    start = m * 2 * cols_in + i * cols_in
                    pieces[4 * k : 4 * k + 4, share_out:, start : start + cols_in] = value[:, m]

    return call(
        body,
        pos,
        [*near_out, *near_in, *got, *far],
        [((8, share_out + share_in // 2, 2 * cols_out), BF16)],
        LONG,
    )[0]


def shares(pos, pieces, share_out):
    rows, cols = pieces.shape[1:]
    rows_in = rows - share_out
    cols_in = cols // 2

    def body(pos_ref, got, outer, inner):
        for c in range(2):
            value = sum(got[2 * z + c].astype(F32) for z in range(4))
            outer[:, c * cols : (c + 1) * cols] = value[:share_out]
            at = slice(c * cols_in, (c + 1) * cols_in)
            inner[:rows_in, at] = value[share_out:, :cols_in]
            inner[rows_in:, at] = value[share_out:, cols_in:]

    outer, inner = call(
        body, pos, [pieces], [((share_out, 2 * cols), F32), ((2 * rows_in, cols), F32)]
    )
    return outer[None], inner[None]


def slot_grads_of(pos, grad_pre, weight_in):
    slots, hidden = grad_pre.shape
    width = weight_in.shape[0]
    step = width // 4

    def body(pos_ref, grad, weight, out, held, sems):
        copies = []
        for i in range(4):
            at = pl.ds(i * step, step)
            copies.append(pltpu.make_async_copy(weight.at[at, :], held.at[at, :], sems.at[i]))
            copies[i].start()
        for i in range(4):
            at = slice(i * step, (i + 1) * step)
            copies[i].wait()
            out[:, at] = lax.dot_general(
                grad[...], held[at, :], (((1,), (1,)), ((), ())), preferred_element_type=F32
            ).astype(BF16)

    return call(
        body,
        pos,
        [grad_pre],
        [((slots, width), BF16)],
        far=[weight_in],
        scratch=[pltpu.VMEM((width, hidden), BF16), pltpu.SemaphoreType.DMA((4,))],
        vmem_limit=ALL_VMEM,
    )[0]


def router_grads(pos, dispatch, gate_back, token_lanes, tokens, scale):
    rows, width = tokens.shape
    experts = 8
    step = width // 4

    def body(pos_ref, disp, back, side, tok, logit, router, held, sem):
        copy = pltpu.make_async_copy(tok, held, sem)
        copy.start()
        dims = (((0,), (0,)), ((), ()))
        combine_grad = lax.dot_general(disp[...], back[...], dims, preferred_element_type=F32)
        probs, combine, keep, denominator = (side[k] for k in range(4))
        weighted = jnp.sum(combine_grad * combine, axis=1, keepdims=True)
        probs_grad = keep * (combine_grad - weighted) / denominator
        inner = jnp.sum(probs_grad * probs, axis=1, keepdims=True)
        logit_b = (probs * (probs_grad - inner)).astype(BF16)
        logit[...] = logit_b
        copy.wait()
        for i in range(4):
            at = slice(i * step, (i + 1) * step)
            part = lax.dot_general(logit_b, held[:, at], dims, preferred_element_type=F32)
            router[:, at] = part[:experts] * scale

    return call(
        body,
        pos,
        [dispatch, gate_back, token_lanes],
        [((rows, EXTRA), BF16), ((experts, width), F32)],
        far=[tokens],
        scratch=[pltpu.VMEM((rows, width), BF16), pltpu.SemaphoreType.DMA],
        vmem_limit=ALL_VMEM,
    )


def token_grads(pos, dispatch, back, logit_lanes, weight_lanes):
    rows, width = dispatch.shape[1], back.shape[1]
    step = width // 4

    def body(pos_ref, disp, flat, logit, weight, out):
        for i in range(4):
            at = slice(i * step, (i + 1) * step)
            value = lax.dot_general(
                disp[...], flat[:, at], (((0,), (0,)), ((), ())), preferred_element_type=F32
            )
            value = value + lax.dot_general(
                logit[...], weight[at, :], (((1,), (1,)), ((), ())), preferred_element_type=F32
            )
            out[:, at] = value.astype(BF16)

    return call(
        body, pos, [dispatch, back, logit_lanes, weight_lanes], [((rows, width), BF16)]
    )[0]


def per_device(
    tokens, grad_out, router_weight, weight_in, weight_out, expert_ids, slot_index, keep_mask
):
    tok_rows, model_width = tokens.shape
    experts = 8
    weight_in = weight_in[0]
    weight_out = weight_out[0]
    capacity = tok_rows * expert_ids.shape[1] // experts
    slot_count = experts * capacity
    grad_scale = float(tok_rows * 256) ** (-0.5)
    core = lax.axis_index("core")
    my_y = lax.axis_index("y")

    target = expert_ids * capacity + slot_index
    slot_iota = jnp.arange(slot_count, dtype=jnp.int32)[:, None]
    first_hit = (slot_iota == target[None, :, 0]) & (keep_mask[None, :, 0] == 1)
    second_hit = (slot_iota == target[None, :, 1]) & (keep_mask[None, :, 1] == 1)
    dispatch = (first_hit | second_hit).astype(BF16)

    send_tokens = jnp.dot(dispatch, tokens, preferred_element_type=F32).astype(BF16)
    slot_tokens = exchange(
        send_tokens.reshape(experts, capacity, model_width), GROUP
    ).reshape(slot_count, model_width)

    logits = jnp.dot(tokens, router_weight, preferred_element_type=F32)
    exp_logits = jnp.exp(logits)
    router_probs = exp_logits / jnp.sum(exp_logits, axis=1, keepdims=True)
    picked = expert_ids[:, :, None] == jnp.arange(experts, dtype=jnp.int32)[None, None, :]
    chosen = jnp.sum(jnp.where(picked, router_probs[:, None, :], 0.0), axis=2)
    keep_float = keep_mask.astype(F32)
    denominator = jnp.sum(keep_float * chosen, axis=1) + (1.0 - jnp.max(keep_float, axis=1))
    combine = keep_float * chosen / denominator[:, None]
    def lanes(values, fill=0.0):
        return jnp.pad(values, ((0, 0), (0, EXTRA - experts)), constant_values=fill)

    def per_expert(values):
        return jnp.sum(jnp.where(picked, values[:, :, None], 0.0), axis=1)

    combine_full = per_expert(combine)
    token_lanes = jnp.stack(
        [
            lanes(router_probs),
            lanes(combine_full),
            lanes(per_expert(keep_float)),
            lanes(jnp.broadcast_to(denominator[:, None], (tok_rows, experts)), 1.0),
        ]
    )
    weight_lanes = lanes(router_weight)
    gate_lanes = lanes(combine_full.astype(BF16))
    send_grads = jnp.dot(dispatch, grad_out, preferred_element_type=F32).astype(BF16)
    send_gates = jnp.dot(dispatch, gate_lanes, preferred_element_type=F32).astype(BF16)
    received = exchange(
        jnp.concatenate([send_grads, send_gates], axis=1).reshape(
            experts, capacity, model_width + EXTRA
        ),
        GROUP,
    ).reshape(slot_count, model_width + EXTRA)
    other_tokens = swap(slot_tokens, "core", 1)
    hidden_pre = jnp.dot(slot_tokens, weight_in, preferred_element_type=F32)
    normal_cdf, normal_pdf = gelu_parts(hidden_pre)
    hidden_act = (hidden_pre * normal_cdf).astype(BF16)
    act_slope = normal_cdf + hidden_pre * normal_pdf
    other_act = swap(hidden_act, "core", 1)
    left_in = (slot_tokens, other_tokens)
    left_out = (hidden_act, other_act)
    pos = jnp.stack([my_y, core, lax.axis_index(GROUP), lax.axis_index("zh")]).astype(jnp.int32)


    received, left_in, left_out, act_slope, dispatch, weight_lanes, token_lanes = tie(
        received, left_in, left_out, act_slope, dispatch, weight_lanes, token_lanes
    )
    my_out, give_out = scale_grads(pos, received)
    right_out = (my_out, swap(give_out, "core", 1))
    received, _ = tie(received, give_out)
    grad_pre, give_in, gate_grad = pre_grads(
        pos, received, weight_out, left_out[0], act_slope
    )
    right_in = (grad_pre, swap(give_in, "core", 1))

    sent = sent_parts(pos, left_out, right_out, left_in, right_in)
    got = (swap(sent[0], "y", 1), swap(sent[1], "y", 3))
    pre_for_slots, gate_grad, _ = tie(grad_pre, gate_grad, sent)
    gate_back = exchange(gate_grad.reshape(experts, capacity, EXTRA), GROUP).reshape(
        slot_count, EXTRA
    )
    grad_slots = slot_grads_of(pos, pre_for_slots, weight_in)
    grad_slots, gate_back = tie(grad_slots, gate_back)
    back = exchange(
        grad_slots.reshape(experts, capacity, model_width), GROUP
    ).reshape(slot_count, model_width)

    gate_back, _ = tie(gate_back, grad_slots)
    logit_lanes, router_part = router_grads(
        pos, dispatch, gate_back, token_lanes, tokens, grad_scale
    )

    def router_round(value, axes, one, two, *until):
        near, far, both = (swap(value, axes, mask) for mask in (one, two, one ^ two))
        value, near, far, both, _ = tie(value, near, far, both, until)
        return (value + near) + (far + both)

    left_in, left_out, right_in, right_out, _ = tie(
        left_in, left_out, right_in, right_out, router_part
    )
    far_a, far_b = far_parts(pos, left_out, right_out, left_in, right_in)
    got, far_a, far_b = tie(got, far_a, far_b)
    far_a, far_b = far_sums(pos, (far_a, far_b), got)
    far = (swap(far_a, "y", 3), swap(far_b, "y", 1))
    left_in, left_out, right_in, right_out, _ = tie(
        left_in, left_out, right_in, right_out, far_a
    )
    near = near_parts(pos, left_out, right_out, left_in, right_in)
    router_part = router_round(router_part, "zh", 1, 3, near)

    near, far, router_part = tie(near, far, router_part)
    pieces = zh_pieces(pos, near[:2], near[2:], got, far, grad_scale)
    got = exchange(pieces, ("zh", "core"))

    back, router_part, _ = tie(back, router_part, pieces)
    grad_tokens = token_grads(pos, dispatch, back, logit_lanes, weight_lanes)
    router_part = router_round(router_part, "x", 1, 3, grad_tokens)
    router_part = router_round(router_part, "y", 1, 3)
    router_part = router_part + swap(router_part, "core", 1)
    router_part = router_part + swap(router_part, "zl", 1)
    got, router_part = tie(got, router_part)
    outer_share, inner_share = shares(pos, got, near[0].shape[0] // 8)
    return (grad_tokens, router_part.T, inner_share, outer_share)


def solution(mesh):
    fine = Mesh(mesh.devices.reshape(FINE_SHAPE), FINE)
    placed = (
        P(FINE, None),
        P(FINE, None),
        P(),
        P(GROUP, None, None),
        P(GROUP, None, None),
        P(FINE, None),
        P(FINE, None),
        P(FINE, None),
    )
    return jax.shard_map(
        per_device,
        mesh=fine,
        in_specs=placed,
        out_specs=(
            P(FINE, None),
            P(),
            P(GROUP, ("y", "zh", "core"), None),
            P(GROUP, ("y", "zh", "core"), None),
        ),
        check_vma=False,
    )
```

```python
import jax
import jax.numpy as jnp
from jax import lax
from jax.experimental import pallas as pl
from jax.experimental.pallas import tpu as pltpu
from jax.sharding import Mesh, PartitionSpec as P

FINE = ("y", "zh", "core", "x", "zl")
FINE_SHAPE = (4, 4, 2, 4, 2)
GROUP = ("x", "zl")
EXTRA = 128
VMEM_LIMIT = 20 * 1024 * 1024
ALL_VMEM = 58 * 1024 * 1024
MOST_VMEM = 52 * 1024 * 1024
LONG = 28_000_000_000
F32 = jnp.float32
BF16 = jnp.bfloat16


def gelu_parts(hidden_pre):
    normal_cdf = 0.5 * (1.0 + jax.scipy.special.erf(hidden_pre * 0.7071067811865476))
    normal_pdf = jnp.exp(-0.5 * hidden_pre * hidden_pre) * 0.3989422804014327
    return (normal_cdf, normal_pdf)


def contract_rows(left, right):
    return lax.dot_general(left, right, (((0,), (0,)), ((), ())), preferred_element_type=F32)


def contract_cols(left, right):
    return lax.dot_general(left, right, (((1,), (1,)), ((), ())), preferred_element_type=F32)


def swap(values, axis, mask):
    size = lax.axis_size(axis)
    return lax.ppermute(values, axis, [(i, i ^ mask) for i in range(size)])


def exchange(values, axes):
    return lax.all_to_all(values, axes, split_axis=0, concat_axis=0, tiled=True)


def tie(*values):
    return lax.optimization_barrier(values)


def call(body, pos, inputs, outputs, flops=1000, far=(), scratch=(), vmem_limit=VMEM_LIMIT):
    vmem = pl.BlockSpec(memory_space=pltpu.VMEM)
    return pl.pallas_call(
        body,
        in_specs=[pl.BlockSpec(memory_space=pltpu.SMEM)]
        + [vmem] * len(inputs)
        + [pl.BlockSpec(memory_space=pltpu.HBM)] * len(far),
        out_specs=[vmem] * len(outputs),
        out_shape=[jax.ShapeDtypeStruct(shape, dtype) for shape, dtype in outputs],
        scratch_shapes=scratch,
        cost_estimate=pl.CostEstimate(flops=flops, bytes_accessed=1000, transcendentals=0),
        compiler_params=pltpu.CompilerParams(vmem_limit_bytes=vmem_limit),
    )(pos, *inputs, *far)


def gate_of(pos, lanes):
    lane = lax.broadcasted_iota(jnp.int32, lanes.shape, 1)
    return jnp.sum(jnp.where(lane == pos[2], lanes.astype(F32), 0.0), axis=1, keepdims=True)


def scale_grads(pos, received):
    slots, wide = received.shape
    half = (wide - EXTRA) // 2
    rows = slots // 4

    def body(pos_ref, rec, mine, give):
        core = pos_ref[1]
        for r in range(0, slots, rows):
            at = slice(r, r + rows)
            gate = gate_of(pos_ref, rec[at, 2 * half :])
            for out, which in ((mine, core), (give, 1 - core)):
                start = pl.multiple_of(which * half, half)
                out[at, :] = (gate * rec[at, pl.ds(start, half)].astype(F32)).astype(BF16)

    return call(body, pos, [received], [((slots, half), BF16)] * 2)


def pre_grads(pos, received, weight_out, act, slope):
    slots, wide = received.shape
    hidden, width = weight_out.shape
    step = hidden // 4

    def body(pos_ref, rec, weight, act_ref, slope_ref, grad_pre, give, gate_grad):
        gate = gate_of(pos_ref, rec[:, width:])
        total = None
        for i in range(4):
            at = slice(i * step, (i + 1) * step)
            grad_act = lax.dot_general(
                rec[:, :width], weight[at, :], (((1,), (1,)), ((), ())), preferred_element_type=F32
            )
            part = jnp.sum(act_ref[:, at].astype(F32) * grad_act, axis=1, keepdims=True)
            total = part if total is None else total + part
            grad_pre[:, at] = (gate * grad_act * slope_ref[:, at]).astype(BF16)
        start = pl.multiple_of((1 - pos_ref[1]) * (hidden // 2), hidden // 2)
        give[...] = grad_pre[:, pl.ds(start, hidden // 2)]
        lane = lax.broadcasted_iota(jnp.int32, (slots, EXTRA), 1)
        gate_grad[...] = jnp.where(lane == pos_ref[2], total, 0.0).astype(BF16)

    return call(
        body,
        pos,
        [received, weight_out, act, slope],
        [((slots, hidden), BF16), ((slots, hidden // 2), BF16), ((slots, EXTRA), BF16)],
    )


def products(pos, left_out, right_out, left_in, right_in, masks, store, outputs, near):
    slots = left_in[0].shape[0]
    widths = left_out[0].shape[1] // 4, left_in[0].shape[1] // 4
    cols = right_out[1].shape[1] // 2, right_in[1].shape[1] // 2
    blocks = sorted({r for pair in masks for r in pair})

    def body(pos_ref, *refs):
        count = len(outputs)
        refs = list(refs)
        scratch = refs[8 + count :]
        outs = refs[8 : 8 + count]
        rights, lefts = (refs[:4], refs[4:8]) if near else (refs[4:8], refs[:4])
        buffers, sems = scratch[:2], scratch[2]
        held = scratch[3:7]
        copies = []
        for part in range(2):
            width = widths[part]
            for k in range(2):
                for n, r in enumerate(blocks):
                    start = pl.multiple_of((pos_ref[0] ^ r) * width, width)
                    copies.append(
                        pltpu.make_async_copy(
                            lefts[2 * part + k].at[:, pl.ds(start, width)],
                            buffers[part].at[k, n],
                            sems.at[2 * part + k, n],
                        )
                    )
            if not near:
                for k in range(2):
                    source = rights[2 * part + k]
                    if part == 1 and k == 0:
                        start = pl.multiple_of(pos_ref[1] * 2 * cols[1], 2 * cols[1])
                        source = source.at[:, pl.ds(start, 2 * cols[1])]
                    copies.append(
                        pltpu.make_async_copy(
                            source, held[2 * part + k], sems.at[2 * part + k, len(blocks)]
                        )
                    )
        for copy in copies:
            copy.start()
        dims = (((0,), (0,)), ((), ()))
        for part in range(2):
            each = len(copies) // 2
            for copy in copies[part * each : (part + 1) * each]:
                copy.wait()
            wide = cols[part]
            mine, other = (rights if near else held)[2 * part : 2 * part + 2]
            for i in range(2):
                own = i * wide
                if part and near:
                    own = pl.multiple_of((2 * pos_ref[1] + i) * wide, wide)
                for j in range(len(masks[i])):
                    n = blocks.index(masks[i][j])
                    value = lax.dot_general(
                        buffers[part][0, n],
                        mine[:, pl.ds(own, wide)],
                        dims,
                        preferred_element_type=F32,
                    )
                    value = value + lax.dot_general(
                        buffers[part][1, n],
                        other[:, i * wide : (i + 1) * wide],
                        dims,
                        preferred_element_type=F32,
                    )
                    store(outs, part, i, j, value)

    rights = [*right_out, *right_in]
    lefts = [*left_out, *left_in]
    scratch = [pltpu.VMEM((2, len(blocks), slots, width), BF16) for width in widths]
    scratch.append(pltpu.SemaphoreType.DMA((4, len(blocks) + 1)))
    if not near:
        scratch += [pltpu.VMEM((slots, 2 * cols[k // 2]), BF16) for k in range(4)]
    return call(
        body,
        pos,
        rights if near else [],
        outputs,
        far=lefts if near else lefts + rights,
        scratch=scratch,
        vmem_limit=VMEM_LIMIT if near else MOST_VMEM,
    )


def sent_parts(pos, left_out, right_out, left_in, right_in):
    width_out, width_in = left_out[0].shape[1] // 4, left_in[0].shape[1] // 4
    cols_out, cols_in = right_out[1].shape[1] // 2, right_in[1].shape[1] // 2

    def store(outs, part, i, j, value):
        if part:
            outs[i][2 * width_out :, j * cols_in : (j + 1) * cols_in] = value.astype(BF16)
        else:
            outs[i][j * width_out : (j + 1) * width_out, :] = value.astype(BF16)

    outputs = [((2 * width_out + width_in, cols_out), BF16)] * 2
    sides = (left_out, right_out, left_in, right_in)
    return products(pos, *sides, ((1, 2), (3, 2)), store, outputs, True)


def far_parts(pos, left_out, right_out, left_in, right_in):
    width_out, width_in = left_out[0].shape[1] // 4, left_in[0].shape[1] // 4
    cols_out, cols_in = right_out[1].shape[1] // 2, right_in[1].shape[1] // 2
    half = width_in // 2

    def store(outs, part, i, j, value):
        if part:
            outs[i][width_out:, :cols_in] = value[:half, :]
            outs[i][width_out:, cols_in:] = value[half:, :]
        else:
            outs[i][:width_out, :] = value

    outputs = [((width_out + half, cols_out), F32)] * 2
    sides = (left_out, right_out, left_in, right_in)
    return products(pos, *sides, ((3,), (1,)), store, outputs, False)


def near_parts(pos, left_out, right_out, left_in, right_in):
    width_out, width_in = left_out[0].shape[1] // 4, left_in[0].shape[1] // 4
    cols_out, cols_in = right_out[1].shape[1] // 2, right_in[1].shape[1] // 2

    def store(outs, part, i, j, value):
        outs[2 * part + i][...] = value

    outputs = [((width_out, cols_out), F32)] * 2 + [((width_in, cols_in), F32)] * 2
    sides = (left_out, right_out, left_in, right_in)
    return products(pos, *sides, ((0,), (0,)), store, outputs, False)


def far_sums(pos, far, got):
    rows, cols = far[0].shape
    half, wide = rows // 2, cols // 2

    def body(pos_ref, far_a, far_b, got_a, got_b, out_a, out_b):
        for mine, arrived, out in ((far_a, got_a, out_a), (far_b, got_b, out_b)):
            out[:half, :] = (mine[:half, :] + arrived[half:rows, :].astype(F32)).astype(BF16)
            for k in range(2):
                at = slice(k * wide, (k + 1) * wide)
                value = arrived[rows + k * half : rows + (k + 1) * half, wide:].astype(F32)
                out[half:, at] = (mine[half:, at] + value).astype(BF16)

    return call(body, pos, [*far, *got], [((rows, cols), BF16)] * 2)


def zh_pieces(pos, near_out, near_in, got, far, scale):
    rows_out, cols_out = near_out[0].shape
    rows_in, cols_in = near_in[0].shape
    half = rows_in // 2
    share_out, share_in = rows_out // 8, rows_in // 8

    def body(pos_ref, out_a, out_b, in_a, in_b, got_a, got_b, far_a, far_b, pieces):
        sets = ((out_a, in_a, got_a, far_a), (out_b, in_b, got_b, far_b))
        for i, (out, inner, first, second) in enumerate(sets):
            value = out[...] + first[:rows_out, :].astype(F32) + second[:rows_out, :].astype(F32)
            value = (value * scale).astype(BF16).reshape(8, share_out, cols_out)
            pieces[:, :share_out, i * cols_out : (i + 1) * cols_out] = value
            for k in range(2):
                at = slice(2 * rows_out + k * half, 2 * rows_out + (k + 1) * half)
                value = inner[k * half : (k + 1) * half, :] + first[at, :cols_in].astype(F32)
                value = value + second[rows_out:, k * cols_in : (k + 1) * cols_in].astype(F32)
                value = (value * scale).astype(BF16).reshape(4, 2, share_in // 2, cols_in)
                for m in range(2):
                    start = m * 2 * cols_in + i * cols_in
                    pieces[4 * k : 4 * k + 4, share_out:, start : start + cols_in] = value[:, m]

    return call(
        body,
        pos,
        [*near_out, *near_in, *got, *far],
        [((8, share_out + share_in // 2, 2 * cols_out), BF16)],
        LONG,
    )[0]


def shares(pos, pieces, share_out):
    rows, cols = pieces.shape[1:]
    rows_in = rows - share_out
    cols_in = cols // 2

    def body(pos_ref, got, outer, inner):
        for c in range(2):
            value = sum(got[2 * z + c].astype(F32) for z in range(4))
            outer[:, c * cols : (c + 1) * cols] = value[:share_out]
            at = slice(c * cols_in, (c + 1) * cols_in)
            inner[:rows_in, at] = value[share_out:, :cols_in]
            inner[rows_in:, at] = value[share_out:, cols_in:]

    outer, inner = call(
        body, pos, [pieces], [((share_out, 2 * cols), F32), ((2 * rows_in, cols), F32)]
    )
    return outer[None], inner[None]


def slot_grads_of(pos, grad_pre, weight_in):
    slots, hidden = grad_pre.shape
    width = weight_in.shape[0]
    step = width // 4

    def body(pos_ref, grad, weight, out, held, sems):
        copies = []
        for i in range(4):
            at = pl.ds(i * step, step)
            copies.append(pltpu.make_async_copy(weight.at[at, :], held.at[at, :], sems.at[i]))
            copies[i].start()
        for i in range(4):
            at = slice(i * step, (i + 1) * step)
            copies[i].wait()
            out[:, at] = lax.dot_general(
                grad[...], held[at, :], (((1,), (1,)), ((), ())), preferred_element_type=F32
            ).astype(BF16)

    return call(
        body,
        pos,
        [grad_pre],
        [((slots, width), BF16)],
        far=[weight_in],
        scratch=[pltpu.VMEM((width, hidden), BF16), pltpu.SemaphoreType.DMA((4,))],
        vmem_limit=ALL_VMEM,
    )[0]


def router_grads(pos, dispatch, gate_back, token_lanes, tokens, scale):
    rows, width = tokens.shape
    experts = 8
    step = width // 4

    def body(pos_ref, disp, back, side, tok, logit, router, held, sem):
        copy = pltpu.make_async_copy(tok, held, sem)
        copy.start()
        dims = (((0,), (0,)), ((), ()))
        combine_grad = lax.dot_general(disp[...], back[...], dims, preferred_element_type=F32)
        probs, combine, keep, denominator = (side[k] for k in range(4))
        weighted = jnp.sum(combine_grad * combine, axis=1, keepdims=True)
        probs_grad = keep * (combine_grad - weighted) / denominator
        inner = jnp.sum(probs_grad * probs, axis=1, keepdims=True)
        logit_b = (probs * (probs_grad - inner)).astype(BF16)
        logit[...] = logit_b
        copy.wait()
        for i in range(4):
            at = slice(i * step, (i + 1) * step)
            part = lax.dot_general(logit_b, held[:, at], dims, preferred_element_type=F32)
            router[:, at] = part[:experts] * scale

    return call(
        body,
        pos,
        [dispatch, gate_back, token_lanes],
        [((rows, EXTRA), BF16), ((experts, width), F32)],
        far=[tokens],
        scratch=[pltpu.VMEM((rows, width), BF16), pltpu.SemaphoreType.DMA],
        vmem_limit=ALL_VMEM,
    )


def token_grads(pos, dispatch, back, logit_lanes, weight_lanes):
    rows, width = dispatch.shape[1], back.shape[1]
    step = width // 4

    def body(pos_ref, disp, flat, logit, weight, out):
        for i in range(4):
            at = slice(i * step, (i + 1) * step)
            value = lax.dot_general(
                disp[...], flat[:, at], (((0,), (0,)), ((), ())), preferred_element_type=F32
            )
            value = value + lax.dot_general(
                logit[...], weight[at, :], (((1,), (1,)), ((), ())), preferred_element_type=F32
            )
            out[:, at] = value.astype(BF16)

    return call(
        body, pos, [dispatch, back, logit_lanes, weight_lanes], [((rows, width), BF16)]
    )[0]


def per_device(
    tokens, grad_out, router_weight, weight_in, weight_out, expert_ids, slot_index, keep_mask
):
    tok_rows, model_width = tokens.shape
    experts = 8
    weight_in = weight_in[0]
    weight_out = weight_out[0]
    capacity = tok_rows * expert_ids.shape[1] // experts
    slot_count = experts * capacity
    grad_scale = float(tok_rows * 256) ** (-0.5)
    core = lax.axis_index("core")
    my_y = lax.axis_index("y")

    target = expert_ids * capacity + slot_index
    slot_iota = jnp.arange(slot_count, dtype=jnp.int32)[:, None]
    first_hit = (slot_iota == target[None, :, 0]) & (keep_mask[None, :, 0] == 1)
    second_hit = (slot_iota == target[None, :, 1]) & (keep_mask[None, :, 1] == 1)
    dispatch = (first_hit | second_hit).astype(BF16)

    send_tokens = jnp.dot(dispatch, tokens, preferred_element_type=F32).astype(BF16)
    slot_tokens = exchange(
        send_tokens.reshape(experts, capacity, model_width), GROUP
    ).reshape(slot_count, model_width)

    logits = jnp.dot(tokens, router_weight, preferred_element_type=F32)
    exp_logits = jnp.exp(logits)
    router_probs = exp_logits / jnp.sum(exp_logits, axis=1, keepdims=True)
    picked = expert_ids[:, :, None] == jnp.arange(experts, dtype=jnp.int32)[None, None, :]
    chosen = jnp.sum(jnp.where(picked, router_probs[:, None, :], 0.0), axis=2)
    keep_float = keep_mask.astype(F32)
    denominator = jnp.sum(keep_float * chosen, axis=1) + (1.0 - jnp.max(keep_float, axis=1))
    combine = keep_float * chosen / denominator[:, None]
    def lanes(values, fill=0.0):
        return jnp.pad(values, ((0, 0), (0, EXTRA - experts)), constant_values=fill)

    def per_expert(values):
        return jnp.sum(jnp.where(picked, values[:, :, None], 0.0), axis=1)

    combine_full = per_expert(combine)
    token_lanes = jnp.stack(
        [
            lanes(router_probs),
            lanes(combine_full),
            lanes(per_expert(keep_float)),
            lanes(jnp.broadcast_to(denominator[:, None], (tok_rows, experts)), 1.0),
        ]
    )
    weight_lanes = lanes(router_weight)
    gate_lanes = lanes(combine_full.astype(BF16))
    send_grads = jnp.dot(dispatch, grad_out, preferred_element_type=F32).astype(BF16)
    send_gates = jnp.dot(dispatch, gate_lanes, preferred_element_type=F32).astype(BF16)
    received = exchange(
        jnp.concatenate([send_grads, send_gates], axis=1).reshape(
            experts, capacity, model_width + EXTRA
        ),
        GROUP,
    ).reshape(slot_count, model_width + EXTRA)
    other_tokens = swap(slot_tokens, "core", 1)
    hidden_pre = jnp.dot(slot_tokens, weight_in, preferred_element_type=F32)
    normal_cdf, normal_pdf = gelu_parts(hidden_pre)
    hidden_act = (hidden_pre * normal_cdf).astype(BF16)
    act_slope = normal_cdf + hidden_pre * normal_pdf
    other_act = swap(hidden_act, "core", 1)
    left_in = (slot_tokens, other_tokens)
    left_out = (hidden_act, other_act)
    pos = jnp.stack([my_y, core, lax.axis_index(GROUP), lax.axis_index("zh")]).astype(jnp.int32)


    received, left_in, left_out, act_slope, dispatch, weight_lanes, token_lanes = tie(
        received, left_in, left_out, act_slope, dispatch, weight_lanes, token_lanes
    )
    my_out, give_out = scale_grads(pos, received)
    right_out = (my_out, swap(give_out, "core", 1))
    received, _ = tie(received, give_out)
    grad_pre, give_in, gate_grad = pre_grads(
        pos, received, weight_out, left_out[0], act_slope
    )
    right_in = (grad_pre, swap(give_in, "core", 1))

    sent = sent_parts(pos, left_out, right_out, left_in, right_in)
    got = (swap(sent[0], "y", 1), swap(sent[1], "y", 3))
    pre_for_slots, gate_grad, _ = tie(grad_pre, gate_grad, sent)
    gate_back = exchange(gate_grad.reshape(experts, capacity, EXTRA), GROUP).reshape(
        slot_count, EXTRA
    )
    grad_slots = slot_grads_of(pos, pre_for_slots, weight_in)
    grad_slots, gate_back = tie(grad_slots, gate_back)
    back = exchange(
        grad_slots.reshape(experts, capacity, model_width), GROUP
    ).reshape(slot_count, model_width)

    gate_back, _ = tie(gate_back, grad_slots)
    logit_lanes, router_part = router_grads(
        pos, dispatch, gate_back, token_lanes, tokens, grad_scale
    )

    def router_round(value, axes, one, two, *until):
        near, far, both = (swap(value, axes, mask) for mask in (one, two, one ^ two))
        value, near, far, both, _ = tie(value, near, far, both, until)
        return (value + near) + (far + both)

    left_in, left_out, right_in, right_out, _ = tie(
        left_in, left_out, right_in, right_out, router_part
    )
    far_a, far_b = far_parts(pos, left_out, right_out, left_in, right_in)
    got, far_a, far_b = tie(got, far_a, far_b)
    far_a, far_b = far_sums(pos, (far_a, far_b), got)
    far = (swap(far_a, "y", 3), swap(far_b, "y", 1))
    left_in, left_out, right_in, right_out, _ = tie(
        left_in, left_out, right_in, right_out, far_a
    )
    near = near_parts(pos, left_out, right_out, left_in, right_in)
    other_router = swap(router_part, "core", 1)
    router_part, other_router, _ = tie(router_part, other_router, near)
    router_part = router_part + other_router

    near, far, router_part = tie(near, far, router_part)
    pieces = zh_pieces(pos, near[:2], near[2:], got, far, grad_scale)
    got = exchange(pieces, ("zh", "core"))

    back, router_part, _ = tie(back, router_part, pieces)
    grad_tokens = token_grads(pos, dispatch, back, logit_lanes, weight_lanes)
    router_part = router_round(router_part, "x", 1, 3, grad_tokens)
    router_part = router_round(router_part, "y", 1, 3)
    place = lambda c, z: 4 * (z // 2) + 2 * c + z % 2
    terms = []
    for k in range(4):
        pairs = [
            (place(c, z), place(c, z ^ (4 * c + k))) for c in range(2) for z in range(8) if c or k
        ]
        terms.append(lax.ppermute(router_part, ("zh", "core", "zl"), pairs))
    terms[0] = jnp.where(core == 0, router_part, terms[0])
    router_part = (terms[0] + terms[1]) + (terms[2] + terms[3])
    router_part = router_part + swap(router_part, "core", 1)
    got, router_part = tie(got, router_part)
    outer_share, inner_share = shares(pos, got, near[0].shape[0] // 8)
    return (grad_tokens, router_part.T, inner_share, outer_share)


def solution(mesh):
    fine = Mesh(mesh.devices.reshape(FINE_SHAPE), FINE)
    placed = (
        P(FINE, None),
        P(FINE, None),
        P(),
        P(GROUP, None, None),
        P(GROUP, None, None),
        P(FINE, None),
        P(FINE, None),
        P(FINE, None),
    )
    return jax.shard_map(
        per_device,
        mesh=fine,
        in_specs=placed,
        out_specs=(
            P(FINE, None),
            P(),
            P(GROUP, ("y", "zh", "core"), None),
            P(GROUP, ("y", "zh", "core"), None),
        ),
        check_vma=False,
    )
```

```python
import jax
import jax.numpy as jnp
from jax import lax
from jax.experimental import pallas as pl
from jax.experimental.pallas import tpu as pltpu
from jax.sharding import Mesh, PartitionSpec as P

FINE = ("y", "zh", "core", "x", "zl")
FINE_SHAPE = (4, 4, 2, 4, 2)
GROUP = ("x", "zl")
EXTRA = 128
VMEM_LIMIT = 20 * 1024 * 1024
ALL_VMEM = 58 * 1024 * 1024
LONG = 28_000_000_000
F32 = jnp.float32
BF16 = jnp.bfloat16


def gelu_parts(hidden_pre):
    normal_cdf = 0.5 * (1.0 + jax.scipy.special.erf(hidden_pre * 0.7071067811865476))
    normal_pdf = jnp.exp(-0.5 * hidden_pre * hidden_pre) * 0.3989422804014327
    return (normal_cdf, normal_pdf)


def contract_rows(left, right):
    return lax.dot_general(left, right, (((0,), (0,)), ((), ())), preferred_element_type=F32)


def contract_cols(left, right):
    return lax.dot_general(left, right, (((1,), (1,)), ((), ())), preferred_element_type=F32)


def swap(values, axis, mask):
    size = lax.axis_size(axis)
    return lax.ppermute(values, axis, [(i, i ^ mask) for i in range(size)])


def exchange(values, axes):
    return lax.all_to_all(values, axes, split_axis=0, concat_axis=0, tiled=True)


def tie(*values):
    return lax.optimization_barrier(values)


def call(body, pos, inputs, outputs, flops=1000, far=(), scratch=(), vmem_limit=VMEM_LIMIT):
    vmem = pl.BlockSpec(memory_space=pltpu.VMEM)
    return pl.pallas_call(
        body,
        in_specs=[pl.BlockSpec(memory_space=pltpu.SMEM)]
        + [vmem] * len(inputs)
        + [pl.BlockSpec(memory_space=pltpu.HBM)] * len(far),
        out_specs=[vmem] * len(outputs),
        out_shape=[jax.ShapeDtypeStruct(shape, dtype) for shape, dtype in outputs],
        scratch_shapes=scratch,
        cost_estimate=pl.CostEstimate(flops=flops, bytes_accessed=1000, transcendentals=0),
        compiler_params=pltpu.CompilerParams(vmem_limit_bytes=vmem_limit),
    )(pos, *inputs, *far)


def gate_of(pos, lanes):
    lane = lax.broadcasted_iota(jnp.int32, lanes.shape, 1)
    return jnp.sum(jnp.where(lane == pos[2], lanes.astype(F32), 0.0), axis=1, keepdims=True)


def scale_grads(pos, received):
    slots, wide = received.shape
    half = (wide - EXTRA) // 2
    rows = slots // 4

    def body(pos_ref, rec, mine, give):
        core = pos_ref[1]
        for r in range(0, slots, rows):
            at = slice(r, r + rows)
            gate = gate_of(pos_ref, rec[at, 2 * half :])
            for out, which in ((mine, core), (give, 1 - core)):
                start = pl.multiple_of(which * half, half)
                out[at, :] = (gate * rec[at, pl.ds(start, half)].astype(F32)).astype(BF16)

    return call(body, pos, [received], [((slots, half), BF16)] * 2)


def pre_grads(pos, received, weight_out, act, slope):
    slots, wide = received.shape
    hidden, width = weight_out.shape
    step = hidden // 4

    def body(pos_ref, rec, weight, act_ref, slope_ref, grad_pre, give, gate_grad):
        gate = gate_of(pos_ref, rec[:, width:])
        total = None
        for i in range(4):
            at = slice(i * step, (i + 1) * step)
            grad_act = lax.dot_general(
                rec[:, :width], weight[at, :], (((1,), (1,)), ((), ())), preferred_element_type=F32
            )
            part = jnp.sum(act_ref[:, at].astype(F32) * grad_act, axis=1, keepdims=True)
            total = part if total is None else total + part
            grad_pre[:, at] = (gate * grad_act * slope_ref[:, at]).astype(BF16)
        start = pl.multiple_of((1 - pos_ref[1]) * (hidden // 2), hidden // 2)
        give[...] = grad_pre[:, pl.ds(start, hidden // 2)]
        lane = lax.broadcasted_iota(jnp.int32, (slots, EXTRA), 1)
        gate_grad[...] = jnp.where(lane == pos_ref[2], total, 0.0).astype(BF16)

    return call(
        body,
        pos,
        [received, weight_out, act, slope],
        [((slots, hidden), BF16), ((slots, hidden // 2), BF16), ((slots, EXTRA), BF16)],
    )


def products(pos, left_out, right_out, left_in, right_in, masks, store, outputs, near):
    slots = left_in[0].shape[0]
    widths = left_out[0].shape[1] // 4, left_in[0].shape[1] // 4
    cols = right_out[1].shape[1] // 2, right_in[1].shape[1] // 2
    blocks = sorted({r for pair in masks for r in pair})

    def body(pos_ref, *refs):
        count = len(outputs)
        refs = list(refs)
        scratch = refs[8 + count :]
        outs = refs[8 : 8 + count]
        rights, lefts = (refs[:4], refs[4:8]) if near else (refs[4:8], refs[:4])
        buffers, sems = scratch[:2], scratch[2]
        held = scratch[3:7]
        copies = []
        for part in range(2):
            width = widths[part]
            for k in range(2):
                for n, r in enumerate(blocks):
                    start = pl.multiple_of((pos_ref[0] ^ r) * width, width)
                    copies.append(
                        pltpu.make_async_copy(
                            lefts[2 * part + k].at[:, pl.ds(start, width)],
                            buffers[part].at[k, n],
                            sems.at[2 * part + k, n],
                        )
                    )
            if not near:
                for k in range(2):
                    source = rights[2 * part + k]
                    if part == 1 and k == 0:
                        start = pl.multiple_of(pos_ref[1] * 2 * cols[1], 2 * cols[1])
                        source = source.at[:, pl.ds(start, 2 * cols[1])]
                    copies.append(
                        pltpu.make_async_copy(
                            source, held[2 * part + k], sems.at[2 * part + k, len(blocks)]
                        )
                    )
        for copy in copies:
            copy.start()
        dims = (((0,), (0,)), ((), ()))
        for part in range(2):
            each = len(copies) // 2
            for copy in copies[part * each : (part + 1) * each]:
                copy.wait()
            wide = cols[part]
            mine, other = (rights if near else held)[2 * part : 2 * part + 2]
            for i in range(2):
                own = i * wide
                if part and near:
                    own = pl.multiple_of((2 * pos_ref[1] + i) * wide, wide)
                for j in range(len(masks[i])):
                    n = blocks.index(masks[i][j])
                    value = lax.dot_general(
                        buffers[part][0, n],
                        mine[:, pl.ds(own, wide)],
                        dims,
                        preferred_element_type=F32,
                    )
                    value = value + lax.dot_general(
                        buffers[part][1, n],
                        other[:, i * wide : (i + 1) * wide],
                        dims,
                        preferred_element_type=F32,
                    )
                    store(outs, part, i, j, value)

    rights = [*right_out, *right_in]
    lefts = [*left_out, *left_in]
    scratch = [pltpu.VMEM((2, len(blocks), slots, width), BF16) for width in widths]
    scratch.append(pltpu.SemaphoreType.DMA((4, len(blocks) + 1)))
    if not near:
        scratch += [pltpu.VMEM((slots, 2 * cols[k // 2]), BF16) for k in range(4)]
    return call(
        body,
        pos,
        rights if near else [],
        outputs,
        far=lefts if near else lefts + rights,
        scratch=scratch,
        vmem_limit=VMEM_LIMIT,
    )


def sent_parts(pos, left_out, right_out, left_in, right_in):
    width_out, width_in = left_out[0].shape[1] // 4, left_in[0].shape[1] // 4
    cols_out, cols_in = right_out[1].shape[1] // 2, right_in[1].shape[1] // 2

    def store(outs, part, i, j, value):
        if part:
            outs[i][2 * width_out :, j * cols_in : (j + 1) * cols_in] = value.astype(BF16)
        else:
            outs[i][j * width_out : (j + 1) * width_out, :] = value.astype(BF16)

    outputs = [((2 * width_out + width_in, cols_out), BF16)] * 2
    sides = (left_out, right_out, left_in, right_in)
    return products(pos, *sides, ((1, 2), (3, 2)), store, outputs, True)


def far_parts(pos, left_out, right_out, left_in, right_in):
    width_out, width_in = left_out[0].shape[1] // 4, left_in[0].shape[1] // 4
    cols_out, cols_in = right_out[1].shape[1] // 2, right_in[1].shape[1] // 2
    half = width_in // 2

    def store(outs, part, i, j, value):
        if part:
            outs[i][width_out:, :cols_in] = value[:half, :]
            outs[i][width_out:, cols_in:] = value[half:, :]
        else:
            outs[i][:width_out, :] = value

    outputs = [((width_out + half, cols_out), F32)] * 2
    sides = (left_out, right_out, left_in, right_in)
    return products(pos, *sides, ((3,), (1,)), store, outputs, False)


def near_parts(pos, left_out, right_out, left_in, right_in):
    width_out, width_in = left_out[0].shape[1] // 4, left_in[0].shape[1] // 4
    cols_out, cols_in = right_out[1].shape[1] // 2, right_in[1].shape[1] // 2

    def store(outs, part, i, j, value):
        outs[2 * part + i][...] = value

    outputs = [((width_out, cols_out), F32)] * 2 + [((width_in, cols_in), F32)] * 2
    sides = (left_out, right_out, left_in, right_in)
    return products(pos, *sides, ((0,), (0,)), store, outputs, False)


def far_sums(pos, far, got):
    rows, cols = far[0].shape
    half, wide = rows // 2, cols // 2

    def body(pos_ref, far_a, far_b, got_a, got_b, out_a, out_b):
        for mine, arrived, out in ((far_a, got_a, out_a), (far_b, got_b, out_b)):
            out[:half, :] = (mine[:half, :] + arrived[half:rows, :].astype(F32)).astype(BF16)
            for k in range(2):
                at = slice(k * wide, (k + 1) * wide)
                value = arrived[rows + k * half : rows + (k + 1) * half, wide:].astype(F32)
                out[half:, at] = (mine[half:, at] + value).astype(BF16)

    return call(body, pos, [*far, *got], [((rows, cols), BF16)] * 2)


def zh_pieces(pos, near_out, near_in, got, far, scale):
    rows_out, cols_out = near_out[0].shape
    rows_in, cols_in = near_in[0].shape
    half = rows_in // 2
    share_out, share_in = rows_out // 8, rows_in // 8

    def body(pos_ref, out_a, out_b, in_a, in_b, got_a, got_b, far_a, far_b, pieces):
        sets = ((out_a, in_a, got_a, far_a), (out_b, in_b, got_b, far_b))
        for i, (out, inner, first, second) in enumerate(sets):
            value = out[...] + first[:rows_out, :].astype(F32) + second[:rows_out, :].astype(F32)
            value = (value * scale).astype(BF16).reshape(8, share_out, cols_out)
            pieces[:, :share_out, i * cols_out : (i + 1) * cols_out] = value
            for k in range(2):
                at = slice(2 * rows_out + k * half, 2 * rows_out + (k + 1) * half)
                value = inner[k * half : (k + 1) * half, :] + first[at, :cols_in].astype(F32)
                value = value + second[rows_out:, k * cols_in : (k + 1) * cols_in].astype(F32)
                value = (value * scale).astype(BF16).reshape(4, 2, share_in // 2, cols_in)
                for m in range(2):
                    start = m * 2 * cols_in + i * cols_in
                    pieces[4 * k : 4 * k + 4, share_out:, start : start + cols_in] = value[:, m]

    return call(
        body,
        pos,
        [*near_out, *near_in, *got, *far],
        [((8, share_out + share_in // 2, 2 * cols_out), BF16)],
        LONG,
    )[0]


def shares(pos, pieces, share_out):
    rows, cols = pieces.shape[1:]
    rows_in = rows - share_out
    cols_in = cols // 2

    def body(pos_ref, got, outer, inner):
        for c in range(2):
            value = sum(got[2 * z + c].astype(F32) for z in range(4))
            outer[:, c * cols : (c + 1) * cols] = value[:share_out]
            at = slice(c * cols_in, (c + 1) * cols_in)
            inner[:rows_in, at] = value[share_out:, :cols_in]
            inner[rows_in:, at] = value[share_out:, cols_in:]

    outer, inner = call(
        body, pos, [pieces], [((share_out, 2 * cols), F32), ((2 * rows_in, cols), F32)]
    )
    return outer[None], inner[None]


def slot_grads_of(pos, grad_pre, weight_in, gate_grad):
    slots, hidden = grad_pre.shape
    width = weight_in.shape[0]
    step = width // 4

    def body(pos_ref, grad, gate, weight, out, held, sems):
        copies = []
        for i in range(4):
            at = pl.ds(i * step, step)
            copies.append(pltpu.make_async_copy(weight.at[at, :], held.at[at, :], sems.at[i]))
            copies[i].start()
        for i in range(4):
            at = slice(i * step, (i + 1) * step)
            copies[i].wait()
            out[:, at] = lax.dot_general(
                grad[...], held[at, :], (((1,), (1,)), ((), ())), preferred_element_type=F32
            ).astype(BF16)
        out[:, width:] = gate[...]

    return call(
        body,
        pos,
        [grad_pre, gate_grad],
        [((slots, width + EXTRA), BF16)],
        far=[weight_in],
        scratch=[pltpu.VMEM((width, hidden), BF16), pltpu.SemaphoreType.DMA((4,))],
        vmem_limit=ALL_VMEM,
    )[0]


def router_grads(pos, dispatch, back, token_lanes, tokens, scale):
    rows, width = tokens.shape
    experts = 8
    step = width // 4

    def body(pos_ref, disp, flat, side, tok, logit, router, held, sem):
        copy = pltpu.make_async_copy(tok, held, sem)
        copy.start()
        dims = (((0,), (0,)), ((), ()))
        combine_grad = lax.dot_general(
            disp[...], flat[:, width:], dims, preferred_element_type=F32
        )
        probs, combine, keep, denominator = (side[k] for k in range(4))
        weighted = jnp.sum(combine_grad * combine, axis=1, keepdims=True)
        probs_grad = keep * (combine_grad - weighted) / denominator
        inner = jnp.sum(probs_grad * probs, axis=1, keepdims=True)
        logit_b = (probs * (probs_grad - inner)).astype(BF16)
        logit[...] = logit_b
        copy.wait()
        for i in range(4):
            at = slice(i * step, (i + 1) * step)
            part = lax.dot_general(logit_b, held[:, at], dims, preferred_element_type=F32)
            router[:, at] = part[:experts] * scale

    return call(
        body,
        pos,
        [dispatch, back, token_lanes],
        [((rows, EXTRA), BF16), ((experts, width), F32)],
        far=[tokens],
        scratch=[pltpu.VMEM((rows, width), BF16), pltpu.SemaphoreType.DMA],
        vmem_limit=ALL_VMEM,
    )


def token_grads(pos, dispatch, back, logit_lanes, weight_lanes):
    rows, width = dispatch.shape[1], back.shape[1] - EXTRA
    step = width // 4

    def body(pos_ref, disp, flat, logit, weight, out):
        for i in range(4):
            at = slice(i * step, (i + 1) * step)
            value = lax.dot_general(
                disp[...], flat[:, at], (((0,), (0,)), ((), ())), preferred_element_type=F32
            )
            value = value + lax.dot_general(
                logit[...], weight[at, :], (((1,), (1,)), ((), ())), preferred_element_type=F32
            )
            out[:, at] = value.astype(BF16)

    return call(
        body, pos, [dispatch, back, logit_lanes, weight_lanes], [((rows, width), BF16)]
    )[0]


def per_device(
    tokens, grad_out, router_weight, weight_in, weight_out, expert_ids, slot_index, keep_mask
):
    tok_rows, model_width = tokens.shape
    experts = 8
    weight_in = weight_in[0]
    weight_out = weight_out[0]
    capacity = tok_rows * expert_ids.shape[1] // experts
    slot_count = experts * capacity
    grad_scale = float(tok_rows * 256) ** (-0.5)
    core = lax.axis_index("core")
    my_y = lax.axis_index("y")

    target = expert_ids * capacity + slot_index
    slot_iota = jnp.arange(slot_count, dtype=jnp.int32)[:, None]
    first_hit = (slot_iota == target[None, :, 0]) & (keep_mask[None, :, 0] == 1)
    second_hit = (slot_iota == target[None, :, 1]) & (keep_mask[None, :, 1] == 1)
    dispatch = (first_hit | second_hit).astype(BF16)

    send_tokens = jnp.dot(dispatch, tokens, preferred_element_type=F32).astype(BF16)
    slot_tokens = exchange(
        send_tokens.reshape(experts, capacity, model_width), GROUP
    ).reshape(slot_count, model_width)

    logits = jnp.dot(tokens, router_weight, preferred_element_type=F32)
    exp_logits = jnp.exp(logits)
    router_probs = exp_logits / jnp.sum(exp_logits, axis=1, keepdims=True)
    picked = expert_ids[:, :, None] == jnp.arange(experts, dtype=jnp.int32)[None, None, :]
    chosen = jnp.sum(jnp.where(picked, router_probs[:, None, :], 0.0), axis=2)
    keep_float = keep_mask.astype(F32)
    denominator = jnp.sum(keep_float * chosen, axis=1) + (1.0 - jnp.max(keep_float, axis=1))
    combine = keep_float * chosen / denominator[:, None]
    def lanes(values, fill=0.0):
        return jnp.pad(values, ((0, 0), (0, EXTRA - experts)), constant_values=fill)

    def per_expert(values):
        return jnp.sum(jnp.where(picked, values[:, :, None], 0.0), axis=1)

    combine_full = per_expert(combine)
    token_lanes = jnp.stack(
        [
            lanes(router_probs),
            lanes(combine_full),
            lanes(per_expert(keep_float)),
            lanes(jnp.broadcast_to(denominator[:, None], (tok_rows, experts)), 1.0),
        ]
    )
    weight_lanes = lanes(router_weight)
    gate_lanes = lanes(combine_full.astype(BF16))
    send_grads = jnp.dot(dispatch, grad_out, preferred_element_type=F32).astype(BF16)
    send_gates = jnp.dot(dispatch, gate_lanes, preferred_element_type=F32).astype(BF16)
    received = exchange(
        jnp.concatenate([send_grads, send_gates], axis=1).reshape(
            experts, capacity, model_width + EXTRA
        ),
        GROUP,
    ).reshape(slot_count, model_width + EXTRA)
    other_tokens = swap(slot_tokens, "core", 1)
    hidden_pre = jnp.dot(slot_tokens, weight_in, preferred_element_type=F32)
    normal_cdf, normal_pdf = gelu_parts(hidden_pre)
    hidden_act = (hidden_pre * normal_cdf).astype(BF16)
    act_slope = normal_cdf + hidden_pre * normal_pdf
    other_act = swap(hidden_act, "core", 1)
    left_in = (slot_tokens, other_tokens)
    left_out = (hidden_act, other_act)
    pos = jnp.stack([my_y, core, lax.axis_index(GROUP), lax.axis_index("zh")]).astype(jnp.int32)


    received, left_in, left_out, act_slope, dispatch, weight_lanes, token_lanes = tie(
        received, left_in, left_out, act_slope, dispatch, weight_lanes, token_lanes
    )
    my_out, give_out = scale_grads(pos, received)
    right_out = (my_out, swap(give_out, "core", 1))
    received, _ = tie(received, give_out)
    grad_pre, give_in, gate_grad = pre_grads(
        pos, received, weight_out, left_out[0], act_slope
    )
    right_in = (grad_pre, swap(give_in, "core", 1))

    sent = sent_parts(pos, left_out, right_out, left_in, right_in)
    got = (swap(sent[0], "y", 1), swap(sent[1], "y", 3))
    pre_for_slots, _ = tie(grad_pre, sent)
    grad_slots = slot_grads_of(pos, pre_for_slots, weight_in, gate_grad)
    back = exchange(
        grad_slots.reshape(experts, capacity, model_width + EXTRA), GROUP
    ).reshape(slot_count, model_width + EXTRA)

    def router_round(value, axes, one, two, *until):
        near, far, both = (swap(value, axes, mask) for mask in (one, two, one ^ two))
        value, near, far, both, _ = tie(value, near, far, both, until)
        return (value + near) + (far + both)

    left_in, left_out, right_in, right_out, _ = tie(
        left_in, left_out, right_in, right_out, grad_slots
    )
    far_a, far_b = far_parts(pos, left_out, right_out, left_in, right_in)
    got, far_a, far_b = tie(got, far_a, far_b)
    far_a, far_b = far_sums(pos, (far_a, far_b), got)
    far = (swap(far_a, "y", 3), swap(far_b, "y", 1))
    left_in, left_out, right_in, right_out, _ = tie(
        left_in, left_out, right_in, right_out, far_a
    )
    near = near_parts(pos, left_out, right_out, left_in, right_in)
    near, far = tie(near, far)
    pieces = zh_pieces(pos, near[:2], near[2:], got, far, grad_scale)
    got = exchange(pieces, ("zh", "core"))

    back, _ = tie(back, pieces)
    logit_lanes, router_part = router_grads(
        pos, dispatch, back, token_lanes, tokens, grad_scale
    )
    back, other_router = tie(back, swap(router_part, "core", 1))
    router_part = router_part + other_router
    grad_tokens = token_grads(pos, dispatch, back, logit_lanes, weight_lanes)
    router_part = router_round(router_part, "x", 1, 3, grad_tokens)
    router_part = router_round(router_part, "y", 1, 3)
    place = lambda c, z: 4 * (z // 2) + 2 * c + z % 2
    terms = []
    for k in range(4):
        pairs = [
            (place(c, z), place(c, z ^ (4 * c + k))) for c in range(2) for z in range(8) if c or k
        ]
        terms.append(lax.ppermute(router_part, ("zh", "core", "zl"), pairs))
    terms[0] = jnp.where(core == 0, router_part, terms[0])
    router_part = (terms[0] + terms[1]) + (terms[2] + terms[3])
    router_part = router_part + swap(router_part, "core", 1)
    got, router_part = tie(got, router_part)
    outer_share, inner_share = shares(pos, got, near[0].shape[0] // 8)
    return (grad_tokens, router_part.T, inner_share, outer_share)


def solution(mesh):
    fine = Mesh(mesh.devices.reshape(FINE_SHAPE), FINE)
    placed = (
        P(FINE, None),
        P(FINE, None),
        P(),
        P(GROUP, None, None),
        P(GROUP, None, None),
        P(FINE, None),
        P(FINE, None),
        P(FINE, None),
    )
    return jax.shard_map(
        per_device,
        mesh=fine,
        in_specs=placed,
        out_specs=(
            P(FINE, None),
            P(),
            P(GROUP, ("y", "zh", "core"), None),
            P(GROUP, ("y", "zh", "core"), None),
        ),
        check_vma=False,
    )
```

```python
import jax
import jax.numpy as jnp
from jax import lax
from jax.experimental import pallas as pl
from jax.experimental.pallas import tpu as pltpu
from jax.sharding import Mesh, PartitionSpec as P

FINE = ("y", "zh", "core", "x", "zl")
FINE_SHAPE = (4, 4, 2, 4, 2)
GROUP = ("x", "zl")
EXTRA = 128
VMEM_LIMIT = 20 * 1024 * 1024
LONG = 30_000_000_000
F32 = jnp.float32
BF16 = jnp.bfloat16


def gelu_parts(hidden_pre):
    normal_cdf = 0.5 * (1.0 + jax.scipy.special.erf(hidden_pre * 0.7071067811865476))
    normal_pdf = jnp.exp(-0.5 * hidden_pre * hidden_pre) * 0.3989422804014327
    return (normal_cdf, normal_pdf)


def contract_rows(left, right):
    return lax.dot_general(left, right, (((0,), (0,)), ((), ())), preferred_element_type=F32)


def contract_cols(left, right):
    return lax.dot_general(left, right, (((1,), (1,)), ((), ())), preferred_element_type=F32)


def swap(values, axis, mask):
    size = lax.axis_size(axis)
    return lax.ppermute(values, axis, [(i, i ^ mask) for i in range(size)])


def exchange(values, axes):
    return lax.all_to_all(values, axes, split_axis=0, concat_axis=0, tiled=True)


def tie(*values):
    return lax.optimization_barrier(values)


def call(body, pos, inputs, outputs, flops=1000, far=(), scratch=()):
    vmem = pl.BlockSpec(memory_space=pltpu.VMEM)
    return pl.pallas_call(
        body,
        in_specs=[pl.BlockSpec(memory_space=pltpu.SMEM)]
        + [vmem] * len(inputs)
        + [pl.BlockSpec(memory_space=pltpu.HBM)] * len(far),
        out_specs=[vmem] * len(outputs),
        out_shape=[jax.ShapeDtypeStruct(shape, dtype) for shape, dtype in outputs],
        scratch_shapes=scratch,
        cost_estimate=pl.CostEstimate(flops=flops, bytes_accessed=1000, transcendentals=0),
        compiler_params=pltpu.CompilerParams(vmem_limit_bytes=VMEM_LIMIT),
    )(pos, *inputs, *far)


def gate_of(pos, lanes):
    lane = lax.broadcasted_iota(jnp.int32, lanes.shape, 1)
    return jnp.sum(jnp.where(lane == pos[2], lanes.astype(F32), 0.0), axis=1, keepdims=True)


def scale_grads(pos, received):
    slots, wide = received.shape
    half = (wide - EXTRA) // 2
    rows = slots // 4

    def body(pos_ref, rec, mine, give):
        core = pos_ref[1]
        for r in range(0, slots, rows):
            at = slice(r, r + rows)
            gate = gate_of(pos_ref, rec[at, 2 * half :])
            for out, which in ((mine, core), (give, 1 - core)):
                start = pl.multiple_of(which * half, half)
                out[at, :] = (gate * rec[at, pl.ds(start, half)].astype(F32)).astype(BF16)

    return call(body, pos, [received], [((slots, half), BF16)] * 2)


def pre_grads(pos, received, weight_out, act, slope):
    slots, wide = received.shape
    hidden, width = weight_out.shape
    step = hidden // 4

    def body(pos_ref, rec, weight, act_ref, slope_ref, grad_pre, give, gate_grad):
        gate = gate_of(pos_ref, rec[:, width:])
        total = None
        for i in range(4):
            at = slice(i * step, (i + 1) * step)
            grad_act = lax.dot_general(
                rec[:, :width], weight[at, :], (((1,), (1,)), ((), ())), preferred_element_type=F32
            )
            part = jnp.sum(act_ref[:, at].astype(F32) * grad_act, axis=1, keepdims=True)
            total = part if total is None else total + part
            grad_pre[:, at] = (gate * grad_act * slope_ref[:, at]).astype(BF16)
        start = pl.multiple_of((1 - pos_ref[1]) * (hidden // 2), hidden // 2)
        give[...] = grad_pre[:, pl.ds(start, hidden // 2)]
        lane = lax.broadcasted_iota(jnp.int32, (slots, EXTRA), 1)
        gate_grad[...] = jnp.where(lane == pos_ref[2], total, 0.0).astype(BF16)

    return call(
        body,
        pos,
        [received, weight_out, act, slope],
        [((slots, hidden), BF16), ((slots, hidden // 2), BF16), ((slots, EXTRA), BF16)],
    )


def products(pos, left_out, right_out, left_in, right_in, masks, store, outputs, near):
    slots = left_in[0].shape[0]
    widths = left_out[0].shape[1] // 4, left_in[0].shape[1] // 4
    cols = right_out[1].shape[1] // 2, right_in[1].shape[1] // 2
    blocks = sorted({r for pair in masks for r in pair})

    def body(pos_ref, *refs):
        count = len(outputs)
        refs = list(refs)
        scratch = refs[8 + count :]
        outs = refs[8 : 8 + count]
        rights, lefts = (refs[:4], refs[4:8]) if near else (refs[4:8], refs[:4])
        buffers, sems = scratch[:2], scratch[2]
        held = scratch[3:7]
        copies = []
        for part in range(2):
            width = widths[part]
            for k in range(2):
                for n, r in enumerate(blocks):
                    start = pl.multiple_of((pos_ref[0] ^ r) * width, width)
                    copies.append(
                        pltpu.make_async_copy(
                            lefts[2 * part + k].at[:, pl.ds(start, width)],
                            buffers[part].at[k, n],
                            sems.at[2 * part + k, n],
                        )
                    )
            if not near:
                for k in range(2):
                    source = rights[2 * part + k]
                    if part == 1 and k == 0:
                        start = pl.multiple_of(pos_ref[1] * 2 * cols[1], 2 * cols[1])
                        source = source.at[:, pl.ds(start, 2 * cols[1])]
                    copies.append(
                        pltpu.make_async_copy(
                            source, held[2 * part + k], sems.at[2 * part + k, len(blocks)]
                        )
                    )
        for copy in copies:
            copy.start()
        dims = (((0,), (0,)), ((), ()))
        for part in range(2):
            each = len(copies) // 2
            for copy in copies[part * each : (part + 1) * each]:
                copy.wait()
            wide = cols[part]
            mine, other = (rights if near else held)[2 * part : 2 * part + 2]
            for i in range(2):
                own = i * wide
                if part and near:
                    own = pl.multiple_of((2 * pos_ref[1] + i) * wide, wide)
                for j in range(2):
                    n = blocks.index(masks[i][j])
                    value = lax.dot_general(
                        buffers[part][0, n],
                        mine[:, pl.ds(own, wide)],
                        dims,
                        preferred_element_type=F32,
                    )
                    value = value + lax.dot_general(
                        buffers[part][1, n],
                        other[:, i * wide : (i + 1) * wide],
                        dims,
                        preferred_element_type=F32,
                    )
                    store(outs, part, i, j, value)

    rights = [*right_out, *right_in]
    lefts = [*left_out, *left_in]
    scratch = [pltpu.VMEM((2, len(blocks), slots, width), BF16) for width in widths]
    scratch.append(pltpu.SemaphoreType.DMA((4, len(blocks) + 1)))
    if not near:
        scratch += [pltpu.VMEM((slots, 2 * cols[k // 2]), BF16) for k in range(4)]
    return call(
        body,
        pos,
        rights if near else [],
        outputs,
        far=lefts if near else lefts + rights,
        scratch=scratch,
    )


def sent_parts(pos, left_out, right_out, left_in, right_in):
    width_out, width_in = left_out[0].shape[1] // 4, left_in[0].shape[1] // 4
    cols_out, cols_in = right_out[1].shape[1] // 2, right_in[1].shape[1] // 2

    def store(outs, part, i, j, value):
        if part:
            outs[i][2 * width_out :, j * cols_in : (j + 1) * cols_in] = value.astype(BF16)
        else:
            outs[i][j * width_out : (j + 1) * width_out, :] = value.astype(BF16)

    outputs = [((2 * width_out + width_in, cols_out), BF16)] * 2
    sides = (left_out, right_out, left_in, right_in)
    return products(pos, *sides, ((1, 2), (3, 2)), store, outputs, True)


def kept_parts(pos, left_out, right_out, left_in, right_in):
    width_out, width_in = left_out[0].shape[1] // 4, left_in[0].shape[1] // 4
    cols_out, cols_in = right_out[1].shape[1] // 2, right_in[1].shape[1] // 2
    half = width_in // 2

    def store(outs, part, i, j, value):
        near_out, near_in, far = outs[:2], outs[2:4], outs[4:]
        if j == 0:
            (near_in if part else near_out)[i][...] = value
        elif part:
            far[i][width_out:, :cols_in] = value[:half, :]
            far[i][width_out:, cols_in:] = value[half:, :]
        else:
            far[i][:width_out, :] = value

    outputs = (
        [((width_out, cols_out), F32)] * 2
        + [((width_in, cols_in), F32)] * 2
        + [((width_out + half, cols_out), F32)] * 2
    )
    sides = (left_out, right_out, left_in, right_in)
    return products(pos, *sides, ((0, 3), (0, 1)), store, outputs, False)


def far_sums(pos, far, got):
    rows, cols = far[0].shape
    half, wide = rows // 2, cols // 2

    def body(pos_ref, far_a, far_b, got_a, got_b, out_a, out_b):
        for mine, arrived, out in ((far_a, got_a, out_a), (far_b, got_b, out_b)):
            out[:half, :] = (mine[:half, :] + arrived[half:rows, :].astype(F32)).astype(BF16)
            for k in range(2):
                at = slice(k * wide, (k + 1) * wide)
                value = arrived[rows + k * half : rows + (k + 1) * half, wide:].astype(F32)
                out[half:, at] = (mine[half:, at] + value).astype(BF16)

    return call(body, pos, [*far, *got], [((rows, cols), BF16)] * 2)


def zh_pieces(pos, near_out, near_in, got, far, scale):
    rows_out, cols_out = near_out[0].shape
    rows_in, cols_in = near_in[0].shape
    half = rows_in // 2
    share_out, share_in = rows_out // 8, rows_in // 8

    def body(pos_ref, out_a, out_b, in_a, in_b, got_a, got_b, far_a, far_b, pieces):
        sets = ((out_a, in_a, got_a, far_a), (out_b, in_b, got_b, far_b))
        for i, (out, inner, first, second) in enumerate(sets):
            value = out[...] + first[:rows_out, :].astype(F32) + second[:rows_out, :].astype(F32)
            value = (value * scale).astype(BF16).reshape(8, share_out, cols_out)
            pieces[:, :share_out, i * cols_out : (i + 1) * cols_out] = value
            for k in range(2):
                at = slice(2 * rows_out + k * half, 2 * rows_out + (k + 1) * half)
                value = inner[k * half : (k + 1) * half, :] + first[at, :cols_in].astype(F32)
                value = value + second[rows_out:, k * cols_in : (k + 1) * cols_in].astype(F32)
                value = (value * scale).astype(BF16).reshape(4, 2, share_in // 2, cols_in)
                for m in range(2):
                    start = m * 2 * cols_in + i * cols_in
                    pieces[4 * k : 4 * k + 4, share_out:, start : start + cols_in] = value[:, m]

    return call(
        body,
        pos,
        [*near_out, *near_in, *got, *far],
        [((8, share_out + share_in // 2, 2 * cols_out), BF16)],
        LONG,
    )[0]


def shares(pos, pieces, share_out):
    rows, cols = pieces.shape[1:]
    rows_in = rows - share_out
    cols_in = cols // 2

    def body(pos_ref, got, outer, inner):
        for c in range(2):
            value = sum(got[2 * z + c].astype(F32) for z in range(4))
            outer[:, c * cols : (c + 1) * cols] = value[:share_out]
            at = slice(c * cols_in, (c + 1) * cols_in)
            inner[:rows_in, at] = value[share_out:, :cols_in]
            inner[rows_in:, at] = value[share_out:, cols_in:]

    outer, inner = call(
        body, pos, [pieces], [((share_out, 2 * cols), F32), ((2 * rows_in, cols), F32)]
    )
    return outer[None], inner[None]


def slot_grads_of(pos, grad_pre, weight_in):
    slots, hidden = grad_pre.shape
    width = weight_in.shape[0]
    step = width // 4

    def body(pos_ref, grad, weight, out, held, sems):
        copies = []
        for i in range(4):
            at = pl.ds(i * step, step)
            copies.append(pltpu.make_async_copy(weight.at[at, :], held.at[at, :], sems.at[i]))
            copies[i].start()
        for i in range(4):
            at = slice(i * step, (i + 1) * step)
            copies[i].wait()
            out[:, at] = lax.dot_general(
                grad[...], held[at, :], (((1,), (1,)), ((), ())), preferred_element_type=F32
            ).astype(BF16)

    return call(
        body,
        pos,
        [grad_pre],
        [((slots, width), BF16)],
        far=[weight_in],
        scratch=[pltpu.VMEM((width, hidden), BF16), pltpu.SemaphoreType.DMA((4,))],
    )[0]


def router_grads(pos, dispatch, gate_back, token_lanes, tokens, scale):
    rows, width = tokens.shape
    experts = 8
    step = width // 4

    def body(pos_ref, disp, back, side, tok, logit, router, held, sem):
        copy = pltpu.make_async_copy(tok, held, sem)
        copy.start()
        dims = (((0,), (0,)), ((), ()))
        combine_grad = lax.dot_general(disp[...], back[...], dims, preferred_element_type=F32)
        probs, combine, keep, denominator = (side[k] for k in range(4))
        weighted = jnp.sum(combine_grad * combine, axis=1, keepdims=True)
        probs_grad = keep * (combine_grad - weighted) / denominator
        inner = jnp.sum(probs_grad * probs, axis=1, keepdims=True)
        logit_b = (probs * (probs_grad - inner)).astype(BF16)
        logit[...] = logit_b
        copy.wait()
        for i in range(4):
            at = slice(i * step, (i + 1) * step)
            part = lax.dot_general(logit_b, held[:, at], dims, preferred_element_type=F32)
            router[:, at] = part[:experts] * scale

    return call(
        body,
        pos,
        [dispatch, gate_back, token_lanes],
        [((rows, EXTRA), BF16), ((experts, width), F32)],
        far=[tokens],
        scratch=[pltpu.VMEM((rows, width), BF16), pltpu.SemaphoreType.DMA],
    )


def token_grads(pos, dispatch, back, logit_lanes, weight_lanes):
    rows, width = dispatch.shape[1], back.shape[1]
    step = width // 4

    def body(pos_ref, disp, flat, logit, weight, out):
        for i in range(4):
            at = slice(i * step, (i + 1) * step)
            value = lax.dot_general(
                disp[...], flat[:, at], (((0,), (0,)), ((), ())), preferred_element_type=F32
            )
            value = value + lax.dot_general(
                logit[...], weight[at, :], (((1,), (1,)), ((), ())), preferred_element_type=F32
            )
            out[:, at] = value.astype(BF16)

    return call(
        body, pos, [dispatch, back, logit_lanes, weight_lanes], [((rows, width), BF16)]
    )[0]


def per_device(
    tokens, grad_out, router_weight, weight_in, weight_out, expert_ids, slot_index, keep_mask
):
    tok_rows, model_width = tokens.shape
    experts = 8
    weight_in = weight_in[0]
    weight_out = weight_out[0]
    capacity = tok_rows * expert_ids.shape[1] // experts
    slot_count = experts * capacity
    grad_scale = float(tok_rows * 256) ** (-0.5)
    core = lax.axis_index("core")
    my_y = lax.axis_index("y")

    target = expert_ids * capacity + slot_index
    slot_iota = jnp.arange(slot_count, dtype=jnp.int32)[:, None]
    first_hit = (slot_iota == target[None, :, 0]) & (keep_mask[None, :, 0] == 1)
    second_hit = (slot_iota == target[None, :, 1]) & (keep_mask[None, :, 1] == 1)
    dispatch = (first_hit | second_hit).astype(BF16)

    send_tokens = jnp.dot(dispatch, tokens, preferred_element_type=F32).astype(BF16)
    slot_tokens = exchange(
        send_tokens.reshape(experts, capacity, model_width), GROUP
    ).reshape(slot_count, model_width)

    logits = jnp.dot(tokens, router_weight, preferred_element_type=F32)
    exp_logits = jnp.exp(logits)
    router_probs = exp_logits / jnp.sum(exp_logits, axis=1, keepdims=True)
    picked = expert_ids[:, :, None] == jnp.arange(experts, dtype=jnp.int32)[None, None, :]
    chosen = jnp.sum(jnp.where(picked, router_probs[:, None, :], 0.0), axis=2)
    keep_float = keep_mask.astype(F32)
    denominator = jnp.sum(keep_float * chosen, axis=1) + (1.0 - jnp.max(keep_float, axis=1))
    combine = keep_float * chosen / denominator[:, None]
    def lanes(values, fill=0.0):
        return jnp.pad(values, ((0, 0), (0, EXTRA - experts)), constant_values=fill)

    def per_expert(values):
        return jnp.sum(jnp.where(picked, values[:, :, None], 0.0), axis=1)

    combine_full = per_expert(combine)
    token_lanes = jnp.stack(
        [
            lanes(router_probs),
            lanes(combine_full),
            lanes(per_expert(keep_float)),
            lanes(jnp.broadcast_to(denominator[:, None], (tok_rows, experts)), 1.0),
        ]
    )
    weight_lanes = lanes(router_weight)
    gate_lanes = lanes(combine_full.astype(BF16))
    send_grads = jnp.dot(dispatch, grad_out, preferred_element_type=F32).astype(BF16)
    send_gates = jnp.dot(dispatch, gate_lanes, preferred_element_type=F32).astype(BF16)
    received = exchange(
        jnp.concatenate([send_grads, send_gates], axis=1).reshape(
            experts, capacity, model_width + EXTRA
        ),
        GROUP,
    ).reshape(slot_count, model_width + EXTRA)
    other_tokens = swap(slot_tokens, "core", 1)
    hidden_pre = jnp.dot(slot_tokens, weight_in, preferred_element_type=F32)
    normal_cdf, normal_pdf = gelu_parts(hidden_pre)
    hidden_act = (hidden_pre * normal_cdf).astype(BF16)
    act_slope = normal_cdf + hidden_pre * normal_pdf
    other_act = swap(hidden_act, "core", 1)
    left_in = (slot_tokens, other_tokens)
    left_out = (hidden_act, other_act)
    pos = jnp.stack([my_y, core, lax.axis_index(GROUP), lax.axis_index("zh")]).astype(jnp.int32)


    received, left_in, left_out, act_slope, dispatch, weight_lanes, token_lanes = tie(
        received, left_in, left_out, act_slope, dispatch, weight_lanes, token_lanes
    )
    my_out, give_out = scale_grads(pos, received)
    right_out = (my_out, swap(give_out, "core", 1))
    received, _ = tie(received, give_out)
    grad_pre, give_in, gate_grad = pre_grads(
        pos, received, weight_out, left_out[0], act_slope
    )
    right_in = (grad_pre, swap(give_in, "core", 1))

    sent = sent_parts(pos, left_out, right_out, left_in, right_in)
    got = (swap(sent[0], "y", 1), swap(sent[1], "y", 3))
    pre_for_slots, gate_grad, _ = tie(grad_pre, gate_grad, sent)
    gate_back = exchange(gate_grad.reshape(experts, capacity, EXTRA), GROUP).reshape(
        slot_count, EXTRA
    )
    grad_slots = slot_grads_of(pos, pre_for_slots, weight_in)
    grad_slots, gate_back = tie(grad_slots, gate_back)
    back = exchange(
        grad_slots.reshape(experts, capacity, model_width), GROUP
    ).reshape(slot_count, model_width)

    gate_back, _ = tie(gate_back, grad_slots)
    logit_lanes, router_part = router_grads(
        pos, dispatch, gate_back, token_lanes, tokens, grad_scale
    )

    def router_round(value, axes, one, two, *until):
        near, far, both = (swap(value, axes, mask) for mask in (one, two, one ^ two))
        value, near, far, both, _ = tie(value, near, far, both, until)
        return (value + near) + (far + both)

    left_in, left_out, right_in, right_out, _ = tie(
        left_in, left_out, right_in, right_out, router_part
    )
    *near, far_a, far_b = kept_parts(pos, left_out, right_out, left_in, right_in)
    got, far_a, far_b = tie(got, far_a, far_b)
    far_a, far_b = far_sums(pos, (far_a, far_b), got)
    far = (swap(far_a, "y", 3), swap(far_b, "y", 1))
    router_part, other_router, _ = tie(router_part, swap(router_part, "core", 1), far_a)
    router_part = router_part + other_router
    router_part = router_round(router_part, "zh", 1, 3)

    near, far, router_part = tie(near, far, router_part)
    pieces = zh_pieces(pos, near[:2], near[2:], got, far, grad_scale)
    got = exchange(pieces, ("zh", "core"))

    back, router_part, _ = tie(back, router_part, pieces)
    grad_tokens = token_grads(pos, dispatch, back, logit_lanes, weight_lanes)
    router_part = router_round(router_part, "x", 1, 3, grad_tokens)
    router_part = router_round(router_part, "y", 1, 3)
    router_part = router_part + swap(router_part, "zl", 1)
    got, router_part = tie(got, router_part)
    outer_share, inner_share = shares(pos, got, near[0].shape[0] // 8)
    return (grad_tokens, router_part.T, inner_share, outer_share)


def solution(mesh):
    fine = Mesh(mesh.devices.reshape(FINE_SHAPE), FINE)
    placed = (
        P(FINE, None),
        P(FINE, None),
        P(),
        P(GROUP, None, None),
        P(GROUP, None, None),
        P(FINE, None),
        P(FINE, None),
        P(FINE, None),
    )
    return jax.shard_map(
        per_device,
        mesh=fine,
        in_specs=placed,
        out_specs=(
            P(FINE, None),
            P(),
            P(GROUP, ("y", "zh", "core"), None),
            P(GROUP, ("y", "zh", "core"), None),
        ),
        check_vma=False,
    )
```

```python
import jax
import jax.numpy as jnp
from jax import lax
from jax.experimental import pallas as pl
from jax.experimental.pallas import tpu as pltpu
from jax.sharding import Mesh, PartitionSpec as P

FINE = ("y", "zh", "core", "x", "zl")
FINE_SHAPE = (4, 4, 2, 4, 2)
GROUP = ("x", "zl")
EXTRA = 128
VMEM_LIMIT = 20 * 1024 * 1024
LONG = 30_000_000_000
F32 = jnp.float32
BF16 = jnp.bfloat16


def gelu_parts(hidden_pre):
    normal_cdf = 0.5 * (1.0 + jax.scipy.special.erf(hidden_pre * 0.7071067811865476))
    normal_pdf = jnp.exp(-0.5 * hidden_pre * hidden_pre) * 0.3989422804014327
    return (normal_cdf, normal_pdf)


def contract_rows(left, right):
    return lax.dot_general(left, right, (((0,), (0,)), ((), ())), preferred_element_type=F32)


def contract_cols(left, right):
    return lax.dot_general(left, right, (((1,), (1,)), ((), ())), preferred_element_type=F32)


def swap(values, axis, mask):
    size = lax.axis_size(axis)
    return lax.ppermute(values, axis, [(i, i ^ mask) for i in range(size)])


def exchange(values, axes):
    return lax.all_to_all(values, axes, split_axis=0, concat_axis=0, tiled=True)


def tie(*values):
    return lax.optimization_barrier(values)


def call(body, pos, inputs, outputs, flops=1000, far=(), scratch=()):
    vmem = pl.BlockSpec(memory_space=pltpu.VMEM)
    return pl.pallas_call(
        body,
        in_specs=[pl.BlockSpec(memory_space=pltpu.SMEM)]
        + [vmem] * len(inputs)
        + [pl.BlockSpec(memory_space=pltpu.HBM)] * len(far),
        out_specs=[vmem] * len(outputs),
        out_shape=[jax.ShapeDtypeStruct(shape, dtype) for shape, dtype in outputs],
        scratch_shapes=scratch,
        cost_estimate=pl.CostEstimate(flops=flops, bytes_accessed=1000, transcendentals=0),
        compiler_params=pltpu.CompilerParams(vmem_limit_bytes=VMEM_LIMIT),
    )(pos, *inputs, *far)


def gate_of(pos, lanes):
    lane = lax.broadcasted_iota(jnp.int32, lanes.shape, 1)
    return jnp.sum(jnp.where(lane == pos[2], lanes.astype(F32), 0.0), axis=1, keepdims=True)


def scale_grads(pos, received):
    slots, wide = received.shape
    half = (wide - EXTRA) // 2
    rows = slots // 4

    def body(pos_ref, rec, mine, give):
        core = pos_ref[1]
        for r in range(0, slots, rows):
            at = slice(r, r + rows)
            gate = gate_of(pos_ref, rec[at, 2 * half :])
            for out, which in ((mine, core), (give, 1 - core)):
                start = pl.multiple_of(which * half, half)
                out[at, :] = (gate * rec[at, pl.ds(start, half)].astype(F32)).astype(BF16)

    return call(body, pos, [received], [((slots, half), BF16)] * 2)


def pre_grads(pos, received, weight_out, act, slope):
    slots, wide = received.shape
    hidden, width = weight_out.shape
    step = hidden // 4

    def body(pos_ref, rec, weight, act_ref, slope_ref, grad_pre, give, gate_grad):
        gate = gate_of(pos_ref, rec[:, width:])
        total = None
        for i in range(4):
            at = slice(i * step, (i + 1) * step)
            grad_act = lax.dot_general(
                rec[:, :width], weight[at, :], (((1,), (1,)), ((), ())), preferred_element_type=F32
            )
            part = jnp.sum(act_ref[:, at].astype(F32) * grad_act, axis=1, keepdims=True)
            total = part if total is None else total + part
            grad_pre[:, at] = (gate * grad_act * slope_ref[:, at]).astype(BF16)
        start = pl.multiple_of((1 - pos_ref[1]) * (hidden // 2), hidden // 2)
        give[...] = grad_pre[:, pl.ds(start, hidden // 2)]
        lane = lax.broadcasted_iota(jnp.int32, (slots, EXTRA), 1)
        gate_grad[...] = jnp.where(lane == pos_ref[2], total, 0.0).astype(BF16)

    return call(
        body,
        pos,
        [received, weight_out, act, slope],
        [((slots, hidden), BF16), ((slots, hidden // 2), BF16), ((slots, EXTRA), BF16)],
    )


def products(pos, left_out, right_out, left_in, right_in, masks, store, outputs, near):
    slots = left_in[0].shape[0]
    widths = left_out[0].shape[1] // 4, left_in[0].shape[1] // 4
    cols = right_out[1].shape[1] // 2, right_in[1].shape[1] // 2
    blocks = sorted({r for pair in masks for r in pair})

    def body(pos_ref, *refs):
        count = len(outputs)
        refs = list(refs)
        scratch = refs[8 + count :]
        outs = refs[8 : 8 + count]
        rights, lefts = (refs[:4], refs[4:8]) if near else (refs[4:8], refs[:4])
        buffers, sems = scratch[:2], scratch[2]
        held = scratch[3:7]
        copies = []
        for part in range(2):
            width = widths[part]
            for k in range(2):
                for n, r in enumerate(blocks):
                    start = pl.multiple_of((pos_ref[0] ^ r) * width, width)
                    copies.append(
                        pltpu.make_async_copy(
                            lefts[2 * part + k].at[:, pl.ds(start, width)],
                            buffers[part].at[k, n],
                            sems.at[2 * part + k, n],
                        )
                    )
            if not near:
                for k in range(2):
                    source = rights[2 * part + k]
                    if part == 1 and k == 0:
                        start = pl.multiple_of(pos_ref[1] * 2 * cols[1], 2 * cols[1])
                        source = source.at[:, pl.ds(start, 2 * cols[1])]
                    copies.append(
                        pltpu.make_async_copy(
                            source, held[2 * part + k], sems.at[2 * part + k, len(blocks)]
                        )
                    )
        for copy in copies:
            copy.start()
        dims = (((0,), (0,)), ((), ()))
        for part in range(2):
            each = len(copies) // 2
            for copy in copies[part * each : (part + 1) * each]:
                copy.wait()
            wide = cols[part]
            mine, other = (rights if near else held)[2 * part : 2 * part + 2]
            for i in range(2):
                own = i * wide
                if part and near:
                    own = pl.multiple_of((2 * pos_ref[1] + i) * wide, wide)
                for j in range(2):
                    n = blocks.index(masks[i][j])
                    value = lax.dot_general(
                        buffers[part][0, n],
                        mine[:, pl.ds(own, wide)],
                        dims,
                        preferred_element_type=F32,
                    )
                    value = value + lax.dot_general(
                        buffers[part][1, n],
                        other[:, i * wide : (i + 1) * wide],
                        dims,
                        preferred_element_type=F32,
                    )
                    store(outs, part, i, j, value)

    rights = [*right_out, *right_in]
    lefts = [*left_out, *left_in]
    scratch = [pltpu.VMEM((2, len(blocks), slots, width), BF16) for width in widths]
    scratch.append(pltpu.SemaphoreType.DMA((4, len(blocks) + 1)))
    if not near:
        scratch += [pltpu.VMEM((slots, 2 * cols[k // 2]), BF16) for k in range(4)]
    return call(
        body,
        pos,
        rights if near else [],
        outputs,
        far=lefts if near else lefts + rights,
        scratch=scratch,
    )


def sent_parts(pos, left_out, right_out, left_in, right_in):
    width_out, width_in = left_out[0].shape[1] // 4, left_in[0].shape[1] // 4
    cols_out, cols_in = right_out[1].shape[1] // 2, right_in[1].shape[1] // 2

    def store(outs, part, i, j, value):
        if part:
            outs[i][2 * width_out :, j * cols_in : (j + 1) * cols_in] = value.astype(BF16)
        else:
            outs[i][j * width_out : (j + 1) * width_out, :] = value.astype(BF16)

    outputs = [((2 * width_out + width_in, cols_out), BF16)] * 2
    sides = (left_out, right_out, left_in, right_in)
    return products(pos, *sides, ((1, 2), (3, 2)), store, outputs, True)


def kept_parts(pos, left_out, right_out, left_in, right_in):
    width_out, width_in = left_out[0].shape[1] // 4, left_in[0].shape[1] // 4
    cols_out, cols_in = right_out[1].shape[1] // 2, right_in[1].shape[1] // 2
    half = width_in // 2

    def store(outs, part, i, j, value):
        near_out, near_in, far = outs[:2], outs[2:4], outs[4:]
        if j == 0:
            (near_in if part else near_out)[i][...] = value
        elif part:
            far[i][width_out:, :cols_in] = value[:half, :]
            far[i][width_out:, cols_in:] = value[half:, :]
        else:
            far[i][:width_out, :] = value

    outputs = (
        [((width_out, cols_out), F32)] * 2
        + [((width_in, cols_in), F32)] * 2
        + [((width_out + half, cols_out), F32)] * 2
    )
    sides = (left_out, right_out, left_in, right_in)
    return products(pos, *sides, ((0, 3), (0, 1)), store, outputs, False)


def far_sums(pos, far, got):
    rows, cols = far[0].shape
    half, wide = rows // 2, cols // 2

    def body(pos_ref, far_a, far_b, got_a, got_b, out_a, out_b):
        for mine, arrived, out in ((far_a, got_a, out_a), (far_b, got_b, out_b)):
            out[:half, :] = (mine[:half, :] + arrived[half:rows, :].astype(F32)).astype(BF16)
            for k in range(2):
                at = slice(k * wide, (k + 1) * wide)
                value = arrived[rows + k * half : rows + (k + 1) * half, wide:].astype(F32)
                out[half:, at] = (mine[half:, at] + value).astype(BF16)

    return call(body, pos, [*far, *got], [((rows, cols), BF16)] * 2)


def zh_pieces(pos, near_out, near_in, got, far, scale):
    rows_out, cols_out = near_out[0].shape
    rows_in, cols_in = near_in[0].shape
    half = rows_in // 2
    share_out, share_in = rows_out // 8, rows_in // 8

    def body(pos_ref, out_a, out_b, in_a, in_b, got_a, got_b, far_a, far_b, pieces):
        sets = ((out_a, in_a, got_a, far_a), (out_b, in_b, got_b, far_b))
        for i, (out, inner, first, second) in enumerate(sets):
            value = out[...] + first[:rows_out, :].astype(F32) + second[:rows_out, :].astype(F32)
            value = (value * scale).astype(BF16).reshape(8, share_out, cols_out)
            pieces[:, :share_out, i * cols_out : (i + 1) * cols_out] = value
            for k in range(2):
                at = slice(2 * rows_out + k * half, 2 * rows_out + (k + 1) * half)
                value = inner[k * half : (k + 1) * half, :] + first[at, :cols_in].astype(F32)
                value = value + second[rows_out:, k * cols_in : (k + 1) * cols_in].astype(F32)
                value = (value * scale).astype(BF16).reshape(4, 2, share_in // 2, cols_in)
                for m in range(2):
                    start = m * 2 * cols_in + i * cols_in
                    pieces[4 * k : 4 * k + 4, share_out:, start : start + cols_in] = value[:, m]

    return call(
        body,
        pos,
        [*near_out, *near_in, *got, *far],
        [((8, share_out + share_in // 2, 2 * cols_out), BF16)],
        LONG,
    )[0]


def shares(pos, pieces, share_out):
    rows, cols = pieces.shape[1:]
    rows_in = rows - share_out
    cols_in = cols // 2

    def body(pos_ref, got, outer, inner):
        for c in range(2):
            value = sum(got[2 * z + c].astype(F32) for z in range(4))
            outer[:, c * cols : (c + 1) * cols] = value[:share_out]
            at = slice(c * cols_in, (c + 1) * cols_in)
            inner[:rows_in, at] = value[share_out:, :cols_in]
            inner[rows_in:, at] = value[share_out:, cols_in:]

    outer, inner = call(
        body, pos, [pieces], [((share_out, 2 * cols), F32), ((2 * rows_in, cols), F32)]
    )
    return outer[None], inner[None]


def slot_grads_of(pos, grad_pre, weight_in):
    slots, hidden = grad_pre.shape
    width = weight_in.shape[0]
    step = width // 4

    def body(pos_ref, grad, weight, out, held, sems):
        copies = []
        for i in range(4):
            at = pl.ds(i * step, step)
            copies.append(pltpu.make_async_copy(weight.at[at, :], held.at[at, :], sems.at[i]))
            copies[i].start()
        for i in range(4):
            at = slice(i * step, (i + 1) * step)
            copies[i].wait()
            out[:, at] = lax.dot_general(
                grad[...], held[at, :], (((1,), (1,)), ((), ())), preferred_element_type=F32
            ).astype(BF16)

    return call(
        body,
        pos,
        [grad_pre],
        [((slots, width), BF16)],
        far=[weight_in],
        scratch=[pltpu.VMEM((width, hidden), BF16), pltpu.SemaphoreType.DMA((4,))],
    )[0]


def router_grads(pos, dispatch, gate_back, token_lanes):
    rows = dispatch.shape[1]

    def body(pos_ref, disp, back, side, logit):
        dims = (((0,), (0,)), ((), ()))
        combine_grad = lax.dot_general(disp[...], back[...], dims, preferred_element_type=F32)
        probs, combine, keep, denominator = (side[k] for k in range(4))
        weighted = jnp.sum(combine_grad * combine, axis=1, keepdims=True)
        probs_grad = keep * (combine_grad - weighted) / denominator
        inner = jnp.sum(probs_grad * probs, axis=1, keepdims=True)
        logit[...] = (probs * (probs_grad - inner)).astype(BF16)

    return call(body, pos, [dispatch, gate_back, token_lanes], [((rows, EXTRA), BF16)])[0]


def token_grads(pos, dispatch, back, logit_lanes, weight_lanes):
    rows, width = dispatch.shape[1], back.shape[1]
    step = width // 4

    def body(pos_ref, disp, flat, logit, weight, out):
        for i in range(4):
            at = slice(i * step, (i + 1) * step)
            value = lax.dot_general(
                disp[...], flat[:, at], (((0,), (0,)), ((), ())), preferred_element_type=F32
            )
            value = value + lax.dot_general(
                logit[...], weight[at, :], (((1,), (1,)), ((), ())), preferred_element_type=F32
            )
            out[:, at] = value.astype(BF16)

    return call(
        body, pos, [dispatch, back, logit_lanes, weight_lanes], [((rows, width), BF16)]
    )[0]


def per_device(
    tokens, grad_out, router_weight, weight_in, weight_out, expert_ids, slot_index, keep_mask
):
    tok_rows, model_width = tokens.shape
    experts = 8
    weight_in = weight_in[0]
    weight_out = weight_out[0]
    capacity = tok_rows * expert_ids.shape[1] // experts
    slot_count = experts * capacity
    grad_scale = float(tok_rows * 256) ** (-0.5)
    core = lax.axis_index("core")
    my_y = lax.axis_index("y")

    target = expert_ids * capacity + slot_index
    slot_iota = jnp.arange(slot_count, dtype=jnp.int32)[:, None]
    first_hit = (slot_iota == target[None, :, 0]) & (keep_mask[None, :, 0] == 1)
    second_hit = (slot_iota == target[None, :, 1]) & (keep_mask[None, :, 1] == 1)
    dispatch = (first_hit | second_hit).astype(BF16)

    send_tokens = jnp.dot(dispatch, tokens, preferred_element_type=F32).astype(BF16)
    slot_tokens = exchange(
        send_tokens.reshape(experts, capacity, model_width), GROUP
    ).reshape(slot_count, model_width)

    logits = jnp.dot(tokens, router_weight, preferred_element_type=F32)
    exp_logits = jnp.exp(logits)
    router_probs = exp_logits / jnp.sum(exp_logits, axis=1, keepdims=True)
    picked = expert_ids[:, :, None] == jnp.arange(experts, dtype=jnp.int32)[None, None, :]
    chosen = jnp.sum(jnp.where(picked, router_probs[:, None, :], 0.0), axis=2)
    keep_float = keep_mask.astype(F32)
    denominator = jnp.sum(keep_float * chosen, axis=1) + (1.0 - jnp.max(keep_float, axis=1))
    combine = keep_float * chosen / denominator[:, None]
    def lanes(values, fill=0.0):
        return jnp.pad(values, ((0, 0), (0, EXTRA - experts)), constant_values=fill)

    def per_expert(values):
        return jnp.sum(jnp.where(picked, values[:, :, None], 0.0), axis=1)

    combine_full = per_expert(combine)
    token_lanes = jnp.stack(
        [
            lanes(router_probs),
            lanes(combine_full),
            lanes(per_expert(keep_float)),
            lanes(jnp.broadcast_to(denominator[:, None], (tok_rows, experts)), 1.0),
        ]
    )
    weight_lanes = lanes(router_weight)
    gate_lanes = lanes(combine_full.astype(BF16))
    send_grads = jnp.dot(dispatch, grad_out, preferred_element_type=F32).astype(BF16)
    send_gates = jnp.dot(dispatch, gate_lanes, preferred_element_type=F32).astype(BF16)
    received = exchange(
        jnp.concatenate([send_grads, send_gates], axis=1).reshape(
            experts, capacity, model_width + EXTRA
        ),
        GROUP,
    ).reshape(slot_count, model_width + EXTRA)
    other_tokens = swap(slot_tokens, "core", 1)
    hidden_pre = jnp.dot(slot_tokens, weight_in, preferred_element_type=F32)
    normal_cdf, normal_pdf = gelu_parts(hidden_pre)
    hidden_act = (hidden_pre * normal_cdf).astype(BF16)
    act_slope = normal_cdf + hidden_pre * normal_pdf
    other_act = swap(hidden_act, "core", 1)
    left_in = (slot_tokens, other_tokens)
    left_out = (hidden_act, other_act)
    pos = jnp.stack([my_y, core, lax.axis_index(GROUP), lax.axis_index("zh")]).astype(jnp.int32)


    received, left_in, left_out, act_slope, dispatch, weight_lanes, token_lanes = tie(
        received, left_in, left_out, act_slope, dispatch, weight_lanes, token_lanes
    )
    my_out, give_out = scale_grads(pos, received)
    right_out = (my_out, swap(give_out, "core", 1))
    received, _ = tie(received, give_out)
    grad_pre, give_in, gate_grad = pre_grads(
        pos, received, weight_out, left_out[0], act_slope
    )
    right_in = (grad_pre, swap(give_in, "core", 1))

    sent = sent_parts(pos, left_out, right_out, left_in, right_in)
    got = (swap(sent[0], "y", 1), swap(sent[1], "y", 3))
    pre_for_slots, gate_grad, _ = tie(grad_pre, gate_grad, sent)
    gate_back = exchange(gate_grad.reshape(experts, capacity, EXTRA), GROUP).reshape(
        slot_count, EXTRA
    )
    grad_slots = slot_grads_of(pos, pre_for_slots, weight_in)
    grad_slots, gate_back = tie(grad_slots, gate_back)
    back = exchange(
        grad_slots.reshape(experts, capacity, model_width), GROUP
    ).reshape(slot_count, model_width)

    gate_back, _ = tie(gate_back, grad_slots)
    logit_lanes = router_grads(pos, dispatch, gate_back, token_lanes)
    router_part = contract_rows(logit_lanes[:, :experts], tokens) * grad_scale

    def router_round(value, axes, one, two, *until):
        near, far, both = (swap(value, axes, mask) for mask in (one, two, one ^ two))
        value, near, far, both, _ = tie(value, near, far, both, until)
        return (value + near) + (far + both)

    left_in, left_out, right_in, right_out, _ = tie(
        left_in, left_out, right_in, right_out, router_part
    )
    *near, far_a, far_b = kept_parts(pos, left_out, right_out, left_in, right_in)
    got, far_a, far_b = tie(got, far_a, far_b)
    far_a, far_b = far_sums(pos, (far_a, far_b), got)
    far = (swap(far_a, "y", 3), swap(far_b, "y", 1))
    router_part, other_router, _ = tie(router_part, swap(router_part, "core", 1), far_a)
    router_part = router_part + other_router
    router_part = router_round(router_part, "zh", 1, 3)

    near, far, router_part = tie(near, far, router_part)
    pieces = zh_pieces(pos, near[:2], near[2:], got, far, grad_scale)
    got = exchange(pieces, ("zh", "core"))

    back, router_part, _ = tie(back, router_part, pieces)
    grad_tokens = token_grads(pos, dispatch, back, logit_lanes, weight_lanes)
    router_part = router_round(router_part, "x", 1, 3, grad_tokens)
    router_part = router_round(router_part, "y", 1, 3)
    router_part = router_part + swap(router_part, "zl", 1)
    got, router_part = tie(got, router_part)
    outer_share, inner_share = shares(pos, got, near[0].shape[0] // 8)
    return (grad_tokens, router_part.T, inner_share, outer_share)


def solution(mesh):
    fine = Mesh(mesh.devices.reshape(FINE_SHAPE), FINE)
    placed = (
        P(FINE, None),
        P(FINE, None),
        P(),
        P(GROUP, None, None),
        P(GROUP, None, None),
        P(FINE, None),
        P(FINE, None),
        P(FINE, None),
    )
    return jax.shard_map(
        per_device,
        mesh=fine,
        in_specs=placed,
        out_specs=(
            P(FINE, None),
            P(),
            P(GROUP, ("y", "zh", "core"), None),
            P(GROUP, ("y", "zh", "core"), None),
        ),
        check_vma=False,
    )
```
